32 devices in a mesh: section: 2 (over x), dp: 16 (over z, y, core).
Axes of the slice: x: 2, y: 2, z: 4, core: 2. Of those that a mesh axis runs over, the one named last changes fastest.
Arguments:
- atom_features: bfloat16 [2, 16, 2048, 128], P(None, 'dp'), may hold values from -6 to 6
- atom_single: bfloat16 [2048, 128], replicated, may hold values from -6 to 6
- atom_pairs: bfloat16 [64, 16, 32, 128], P('dp'), may hold values from -6 to 6
- atom_token: int32 [2048], replicated, may hold values from 0 to 511, never falling along the last dimension, each value on 1 to 12 neighbouring positions
- window_start: int32 [64], replicated, may hold values from 0 to 1920, as said below
- pair_repr: bfloat16 [512, 512, 128], P('dp'), may hold values from -6 to 6
- single_repr: bfloat16 [512, 384], replicated, may hold values from -6 to 6
- noise_table: float32 [200, 384], replicated, may hold values from -6 to 6
- noise_index: int32 [2, 16], P(None, 'dp'), may hold values from 0 to 199
- cotangent: bfloat16 [2, 16, 512, 768], P(None, 'dp'), may hold values from -6 to 6
- atomcond_gain: bfloat16 [128], replicated, may hold values from 0.5 to 1.5
- atomcond_weight: bfloat16 [128, 768], replicated, may hold values from -0.5 to 0.5
- atomcond_bias: bfloat16 [768], replicated, may hold values from -3 to 3
- atomproj_weight: bfloat16 [128, 512], replicated, may hold values from -0.5 to 0.5
- atomquery_bias: bfloat16 [128], replicated, may hold values from -4 to 4
- atomout_weight: bfloat16 [128, 128], replicated, may hold values from -2 to 2
- atomgu_weight: bfloat16 [128, 512], replicated, may hold values from -0.5 to 0.5
- atomdown_weight: bfloat16 [256, 128], replicated, may hold values from -0.375 to 0.375
- atompair_gain: bfloat16 [16], replicated, may hold values from 0.099609375 to 1.8984375
- atompair_weight: bfloat16 [16, 4], replicated, may hold values from -1.5 to 1.5
- gather_weight: bfloat16 [128, 768], replicated, may hold values from -0.5 to 0.5
- tokcond_gain: bfloat16 [384], replicated, may hold values from 0.5 to 1.5
- tokcond_weight: bfloat16 [384, 4608], replicated, may hold values from -0.3125 to 0.3125
- tokcond_bias: bfloat16 [4608], replicated, may hold values from -3 to 3
- tokproj_weight: bfloat16 [768, 3072], replicated, may hold values from -0.21875 to 0.21875
- tokquery_bias: bfloat16 [768], replicated, may hold values from -4 to 4
- tokout_weight: bfloat16 [768, 768], replicated, may hold values from -0.875 to 0.875
- tokgu_weight: bfloat16 [768, 3072], replicated, may hold values from -0.21875 to 0.21875
- tokdown_weight: bfloat16 [1536, 768], replicated, may hold values from -0.15625 to 0.15625
- tokpair_gain: bfloat16 [128], replicated, may hold values from 0.099609375 to 1.8984375
- tokpair_weight: bfloat16 [128, 16], replicated, may hold values from -0.5 to 0.5
Outputs:
- output: bfloat16 [2, 16, 512, 768], P(None, 'dp', 'section')
- features_grad: float32 [2, 16, 2048, 128], P(None, 'dp', 'section')
- atomcondgain_grad: float32 [128], P('section')
- atomcondweight_grad: float32 [128, 768], P('section')
- atomcondbias_grad: float32 [768], P('section')
- atomproj_grad: float32 [128, 512], P('section')
- atomquery_grad: float32 [128], P('section')
- atomout_grad: float32 [128, 128], P('section')
- atomgu_grad: float32 [128, 512], P('section')
- atomdown_grad: float32 [256, 128], P('section')
- atompairgain_grad: float32 [16], P('section')
- atompairweight_grad: float32 [16, 4], P('section')
- gather_grad: float32 [128, 768], P('section')
- tokcondgain_grad: float32 [384], P('section')
- tokcondweight_grad: float32 [384, 4608], P('section')
- tokcondbias_grad: float32 [4608], P('section')
- tokproj_grad: float32 [768, 3072], P('section')
- tokquery_grad: float32 [768], P('section')
- tokout_grad: float32 [768, 768], P('section')
- tokgu_grad: float32 [768, 3072], P('section')
- tokdown_grad: float32 [1536, 768], P('section')
- tokpairgain_grad: float32 [128], P('section')
- tokpairweight_grad: float32 [128, 16], P('section')
The draws below stay inside these ranges and needn't reach their ends.
Inputs may be any that keep to these rules, and one draw needn't show every extreme that they name: `atom_token`: non-decreasing; each of the 512 tokens has 1 to 12 atoms. `window_start`: window w holds its 32 query atoms w * 32 to w * 32 + 31 among its 128 keys. `noise_index`: rows of noise_table.
All inputs are finite; a program needn't handle non-finite values.
Results may differ from the reference program's by a relative error of at most 0.03.
Values may be sent and summed in bfloat16 or wider, within the bound.
No kernel may reach another device: no remote copies, remote signals or barrier semaphores. Data moves between devices by JAX's collectives and lax.ppermute only.
A program may use at most 576 MiB of HBM per device.

```python
import math
from functools import partial
import jax
import jax.numpy as jnp
import numpy as np
from jax import lax

C = 128
HA = 4
CP = 16
FA = 256
WQ = 32
WK = 128
D = 768
H = 16
CZ = 128
CS = 384
FF = 1536
L = 512
WIN = 64
MOST = 12
NLEV = 200
MICRO = 2
SAMPLES = 16
ATOMS = 2048


def draw_window_start(key, part):
    key = jax.random.fold_in(key, 7)
    jitter = jax.random.randint(key, (WIN,), -(WQ // 4), WQ // 4 + 1)
    centre = WQ * jnp.arange(WIN, dtype=jnp.int32) + WQ // 2 - WK // 2
    return jnp.clip(centre + jitter, 0, ATOMS - WK).astype(jnp.int32)


def place_ends(drawn, own_key, smallest, top_value):
    index_at = [jax.random.randint(jax.random.fold_in(own_key, axis), (), 0, length) for axis, length in enumerate(drawn.shape)]
    longest = drawn.shape.index(max(drawn.shape))
    neighbour = index_at[:longest] + [(index_at[longest] + 1) % drawn.shape[longest]] + index_at[longest + 1:]
    return drawn.at[tuple(index_at)].set(smallest).at[tuple(neighbour)].set(top_value)


def block_levels(rng, shape, cuts, smallest, largest):
    def one(position, blocks):
        heights = jax.random.uniform(jax.random.fold_in(jax.random.fold_in(rng, 6), position), (blocks,), jnp.float32, smallest / len(cuts), largest / len(cuts))
        return jnp.repeat(jnp.exp(heights), shape[position] // blocks).reshape((-1,) + (1,) * (len(shape) - position - 1))

    level = one(*cuts[0])
    for cut in cuts[1:]:
        level = level * one(*cut)
    return level


def profile(count, total, reach, slope):
    weights = [(1 << 20) // math.isqrt(grade ** slope) + 1 for grade in range(2, count + 1)]
    rest, given = total - reach - (count - 1), [1] * (count - 1)
    while rest > 0:
        movable = [i for i in range(count - 1) if given[i] < reach]
        pool, budget = sum([weights[i] for i in movable]), rest
        for i in movable:
            addition = min(reach - given[i], max(1, budget * weights[i] // pool), rest)
            given[i] = given[i] + addition
            rest = rest - addition
    return np.array([reach] + given)


def uneven_parts(own_key, amount, total, most, skew):
    if amount == 2:
        one = jax.random.randint(own_key, (), max(1, total - most), min(most, total - 1) + 1)
        return jnp.stack([one, total - one])
    lengths = jnp.asarray(profile(amount, total, most, skew), jnp.int32)
    pairs = (amount - 1) // 2
    giver, sink = lengths[1:1 + 2 * pairs:2], lengths[2:2 + 2 * pairs:2]
    slack = jnp.minimum(giver - 1, most - sink)
    passed = jax.random.randint(jax.random.fold_in(own_key, 1), (pairs,), 0, 1 << 20) % (slack + 1)
    lengths = lengths.at[1:1 + 2 * pairs:2].set(giver - passed).at[2:2 + 2 * pairs:2].set(sink + passed)
    return lengths[jax.random.permutation(jax.random.fold_in(own_key, 2), amount)]


def bell_draw(rng, shape, scale, limit, shards=(), kind=jnp.bfloat16):
    array = scale * jax.random.normal(rng, shape, jnp.float32)
    if shards:
        array = array * block_levels(rng, shape, shards, -0.22, 0.18)
    return jnp.clip(array, -limit, limit).astype(kind)


def setup_inputs(seed: int = 0) -> dict:
    streams_of = jax.random.split(jax.random.key(seed), 32)
    atom_features = bell_draw(streams_of[0], (MICRO, SAMPLES, ATOMS, C), 1.0, 6.0, ((1, 16),))
    atom_single = bell_draw(streams_of[1], (ATOMS, C), 1.0, 6.0)
    atom_pairs = bell_draw(streams_of[2], (WIN, CP, WQ, WK), 1.0, 6.0, ((0, 16),))
    atom_token = jnp.searchsorted(jnp.cumsum(uneven_parts(streams_of[3], L, ATOMS, MOST, 2)), jnp.arange(ATOMS), side="right").astype(jnp.int32)
    window_start = draw_window_start(jax.random.fold_in(streams_of[31], 71), 0)
    pair_repr = bell_draw(streams_of[5], (L, L, CZ), 1.0, 6.0, ((0, 16),))
    single_repr = bell_draw(streams_of[6], (L, CS), 1.0, 6.0)
    noise_table = bell_draw(streams_of[7], (NLEV, CS), 1.0, 6.0, (), jnp.float32)
    noise_index = place_ends(jax.random.randint(streams_of[8], (MICRO, SAMPLES), 0, NLEV), jax.random.fold_in(streams_of[8], 1), 0, NLEV - 1).astype(jnp.int32)
    cotangent = bell_draw(streams_of[9], (MICRO, SAMPLES, L, D), 1.0, 6.0, ((1, 16),))
    atomcond_gain = jnp.clip(1.0 + 0.1 * jax.random.normal(streams_of[10], (C,), jnp.float32), 0.5, 1.5).astype(jnp.bfloat16)
    atomcond_weight = bell_draw(streams_of[11], (C, 6 * C), C ** -0.5, 0.5)
    atomcond_bias = bell_draw(streams_of[12], (6 * C,), 0.5, 3.0)
    atomproj_weight = bell_draw(streams_of[13], (C, 4 * C), C ** -0.5, 0.5)
    atomquery_bias = bell_draw(streams_of[14], (C,), 1.0, 4.0)
    atomout_weight = bell_draw(streams_of[15], (C, C), (C // 16) ** -0.5, 2.0)
    atomgu_weight = bell_draw(streams_of[16], (C, 2 * FA), C ** -0.5, 0.5)
    atomdown_weight = bell_draw(streams_of[17], (FA, C), FA ** -0.5, 0.375)
    atompair_gain = jnp.clip(1.0 + 0.18 * jax.random.normal(streams_of[18], (CP,), jnp.float32), 0.099609375, 1.8984375).astype(jnp.bfloat16)
    atompair_weight = bell_draw(streams_of[19], (CP, HA), CP ** -0.5, 1.5)
    gather_weight = bell_draw(streams_of[20], (C, D), C ** -0.5, 0.5)
    tokcond_gain = jnp.clip(1.0 + 0.1 * jax.random.normal(streams_of[21], (CS,), jnp.float32), 0.5, 1.5).astype(jnp.bfloat16)
    tokcond_weight = bell_draw(streams_of[22], (CS, 6 * D), CS ** -0.5, 0.3125)
    tokcond_bias = bell_draw(streams_of[23], (6 * D,), 0.5, 3.0)
    tokproj_weight = bell_draw(streams_of[24], (D, 4 * D), D ** -0.5, 0.21875)
    tokquery_bias = bell_draw(streams_of[25], (D,), 1.0, 4.0)
    tokout_weight = bell_draw(streams_of[26], (D, D), (D // 16) ** -0.5, 0.875)
    tokgu_weight = bell_draw(streams_of[27], (D, 2 * FF), D ** -0.5, 0.21875)
    tokdown_weight = bell_draw(streams_of[28], (FF, D), FF ** -0.5, 0.15625)
    tokpair_gain = jnp.clip(1.0 + 0.18 * jax.random.normal(streams_of[29], (CZ,), jnp.float32), 0.099609375, 1.8984375).astype(jnp.bfloat16)
    tokpair_weight = bell_draw(streams_of[30], (CZ, H), CZ ** -0.5, 0.5)
    return dict(atom_features=atom_features, atom_single=atom_single, atom_pairs=atom_pairs, atom_token=atom_token, window_start=window_start, pair_repr=pair_repr, single_repr=single_repr, noise_table=noise_table, noise_index=noise_index, cotangent=cotangent, atomcond_gain=atomcond_gain, atomcond_weight=atomcond_weight, atomcond_bias=atomcond_bias, atomproj_weight=atomproj_weight, atomquery_bias=atomquery_bias, atomout_weight=atomout_weight, atomgu_weight=atomgu_weight, atomdown_weight=atomdown_weight, atompair_gain=atompair_gain, atompair_weight=atompair_weight, gather_weight=gather_weight, tokcond_gain=tokcond_gain, tokcond_weight=tokcond_weight, tokcond_bias=tokcond_bias, tokproj_weight=tokproj_weight, tokquery_bias=tokquery_bias, tokout_weight=tokout_weight, tokgu_weight=tokgu_weight, tokdown_weight=tokdown_weight, tokpair_gain=tokpair_gain, tokpair_weight=tokpair_weight)


@jax.custom_vjp
def low(v):
    return lax.optimization_barrier(v.astype(jnp.bfloat16)).astype(jnp.float32)

@jax.custom_vjp
def low_back(v):
    return v

def low_keep(v):
    return (low(v), None)

def low_pass(kept, grad):
    return (grad,)

def back_keep(v):
    return (v, None)

def back_low(kept, grad):
    return (low(grad),)
low.defvjp(low_keep, low_pass)
low_back.defvjp(back_keep, back_low)
EPS = 1e-05
HIGH = lax.Precision.HIGHEST

def layer_norm(values, axis=-1):
    centre = values - lax.optimization_barrier(jnp.mean(values, axis=axis, keepdims=True))
    spread = lax.optimization_barrier(jnp.mean(centre * centre, axis=axis, keepdims=True))
    return centre * lax.rsqrt(spread + EPS)

def product(left, right):
    return jnp.dot(left, right, precision=HIGH)

def token_slab(pair_rows, pair_gain, pair_weight):
    normed = layer_norm(pair_rows) * pair_gain
    return jnp.einsum('ijc,ch->hij', normed, pair_weight, precision=HIGH)

def atom_slab(pair_rows, pair_gain, pair_weight):
    normed = layer_norm(pair_rows, 1) * pair_gain[None, :, None, None]
    return jnp.einsum('wcqk,ch->whqk', normed, pair_weight, precision=HIGH)

def windowed(query_win, key_win, value_win, bias_rows, factor):
    scores = jnp.einsum('wqhe,wkhe->whqk', query_win, key_win, precision=HIGH) * factor + bias_rows
    scores = low_back(scores)
    maximum = lax.optimization_barrier(jnp.max(scores, axis=-1, keepdims=True))
    exponent = jnp.exp(scores - maximum)
    probability = low(exponent / lax.optimization_barrier(jnp.sum(exponent, axis=-1, keepdims=True)))
    return low_back(jnp.einsum('whqk,wkhe->wqhe', probability, value_win, precision=HIGH))

def atom_attend(queries, key_rows, value_rows, atom_bias, positions):
    windows, head_count, span_query, span_key = atom_bias.shape
    col_count = queries.shape[1]
    head_size = col_count // head_count
    query_win = queries.reshape(windows, span_query, head_count, head_size)
    key_win = key_rows[positions].reshape(windows, span_key, head_count, head_size)
    value_win = value_rows[positions].reshape(windows, span_key, head_count, head_size)
    attended = windowed(query_win, key_win, value_win, atom_bias, head_size ** (-0.5))
    return attended.reshape(windows * span_query, col_count)

def token_attend(queries, key_rows, value_rows, token_bias):
    head_count = token_bias.shape[0]
    row_count, col_count = queries.shape
    head_size = col_count // head_count
    shaped = [member.reshape(1, row_count, head_count, head_size) for member in (queries, key_rows, value_rows)]
    attended = windowed(shaped[0], shaped[1], shaped[2], token_bias[None], head_size ** (-0.5))
    return attended.reshape(row_count, col_count)

def block(features, condition, weights, attend):
    cond_gain, cond_weight, cond_bias, proj_weight, query_bias, out_weight, gu_weight, down_weight = weights
    col_count = features.shape[-1]
    normed = layer_norm(condition) * cond_gain
    projected = low_back(product(low(normed), cond_weight) + cond_bias)
    pieces = jnp.split(projected, 6, axis=-1)
    normed_one = layer_norm(features) * jax.nn.sigmoid(pieces[0]) + pieces[1]
    padding = jnp.zeros((3 * col_count,), query_bias.dtype)
    projections = low(low_back(product(low(normed_one), proj_weight) + jnp.concatenate([query_bias, padding])))
    queries, key_rows, value_rows, gate_cols = jnp.split(projections, 4, axis=-1)
    attended = attend(queries, key_rows, value_rows)
    gated = low(low_back(attended * jax.nn.sigmoid(gate_cols)))
    attn_out = low_back(product(gated, out_weight))
    middle = features + jax.nn.sigmoid(pieces[2]) * attn_out
    normed_two = layer_norm(middle) * jax.nn.sigmoid(pieces[3]) + pieces[4]
    gate_up = low_back(product(low(normed_two), gu_weight))
    gate_half, up_half = jnp.split(gate_up, 2, axis=-1)
    hidden = low(low_back(jax.nn.silu(gate_half) * up_half))
    down_out = low_back(product(hidden, down_weight))
    return middle + jax.nn.sigmoid(pieces[5]) * down_out

def reference(atom_features, atom_single, atom_pairs, atom_token, window_start, pair_repr, single_repr, noise_table, noise_index, cotangent, atomcond_gain, atomcond_weight, atomcond_bias, atomproj_weight, atomquery_bias, atomout_weight, atomgu_weight, atomdown_weight, atompair_gain, atompair_weight, gather_weight, tokcond_gain, tokcond_weight, tokcond_bias, tokproj_weight, tokquery_bias, tokout_weight, tokgu_weight, tokdown_weight, tokpair_gain, tokpair_weight):
    params = tuple((member.astype(jnp.float32) for member in (atomcond_gain, atomcond_weight, atomcond_bias, atomproj_weight, atomquery_bias, atomout_weight, atomgu_weight, atomdown_weight, atompair_gain, atompair_weight, gather_weight, tokcond_gain, tokcond_weight, tokcond_bias, tokproj_weight, tokquery_bias, tokout_weight, tokgu_weight, tokdown_weight, tokpair_gain, tokpair_weight)))
    atom_cond = atom_single.astype(jnp.float32)
    pairs_wide = atom_pairs.astype(jnp.float32)
    repr_wide = pair_repr.astype(jnp.float32)
    single_wide = single_repr.astype(jnp.float32)
    table_wide = noise_table.astype(jnp.float32)
    positions = window_start[:, None] + jnp.arange(WK, dtype=jnp.int32)[None, :]
    onehot = (atom_token[None, :] == jnp.arange(L, dtype=jnp.int32)[:, None]).astype(jnp.float32)
    counts = lax.optimization_barrier(jnp.sum(onehot, axis=1, keepdims=True))

    def forward(weights, features):
        atom_bias = low(atom_slab(pairs_wide, weights[8], weights[9]))
        token_bias = low(token_slab(repr_wide, weights[19], weights[20]))
        atom_fn = partial(atom_attend, atom_bias=atom_bias, positions=positions)
        token_fn = partial(token_attend, token_bias=token_bias)

        def one_sample(state_in, inputs):
            sample_rows, noise_level = inputs
            result = block(sample_rows, atom_cond, weights[0:8], atom_fn)
            pre_act = low_back(product(low(result), weights[10]))
            pooled = product(onehot, low(jax.nn.silu(pre_act))) / counts
            token_in = low(low_back(pooled))
            condition = single_wide + table_wide[noise_level]
            return (state_in, block(token_in, condition, weights[11:19], token_fn))
        flattened = features.reshape(MICRO * SAMPLES, ATOMS, C)
        _, results = lax.scan(jax.checkpoint(one_sample), jnp.zeros((), jnp.float32), (flattened, noise_index.reshape(-1)))
        return results.reshape(MICRO, SAMPLES, L, D)
    output, pullback = jax.vjp(forward, params, atom_features.astype(jnp.float32))
    grad_params, grad_atoms = pullback(cotangent.astype(jnp.float32))
    return (output.astype(jnp.bfloat16), grad_atoms, grad_params[0], grad_params[1], grad_params[2], grad_params[3], grad_params[4], grad_params[5], grad_params[6], grad_params[7], grad_params[8], grad_params[9], grad_params[10], grad_params[11], grad_params[12], grad_params[13], grad_params[14], grad_params[15], grad_params[16], grad_params[17], grad_params[18], grad_params[19], grad_params[20])
```

```python
from functools import partial

import jax
import jax.numpy as jnp
from jax import lax
from jax.sharding import PartitionSpec as P

EPS = 1e-05
HIGH = lax.Precision.HIGHEST
LOWTYPE = jnp.bfloat16
WIDE = jnp.float32


def from_behind(block, axis, distance):
    devices = range(lax.axis_size(axis))
    route = [(i - distance, i) for i in devices if i - distance in devices]
    return lax.ppermute(block, axis, route)


def layer_norm(values, axis=-1):
    centre = values - jnp.mean(values, axis=axis, keepdims=True)
    spread = jnp.mean(centre * centre, axis=axis, keepdims=True)
    return centre * lax.rsqrt(spread + EPS)


def cond_norm(condition, cond_gain):
    return layer_norm(condition) * cond_gain


def modulate(features, scale_in, shift_in):
    return layer_norm(features) * jax.nn.sigmoid(scale_in) + shift_in


def rounded(values):
    return lax.optimization_barrier(values.astype(LOWTYPE)).astype(WIDE)


def product(left, right):
    return jnp.dot(left, right, preferred_element_type=WIDE)


def product_left(left, right):
    return lax.dot_general(left, right, (((0,), (0,)), ((), ())), preferred_element_type=WIDE)


def product_right(left, right):
    return lax.dot_general(left, right, (((1,), (1,)), ((), ())), preferred_element_type=WIDE)


def silu_slope(values):
    logistic = jax.nn.sigmoid(values)
    return logistic * (1.0 + values * (1.0 - logistic))


def sigmoid_slope(values):
    logistic = jax.nn.sigmoid(values)
    return logistic * (1.0 - logistic)


def token_slab(pair_rows, pair_gain, pair_weight):
    normed = layer_norm(pair_rows) * pair_gain
    return jnp.einsum("ijc,ch->hij", normed, pair_weight, precision=HIGH)


def atom_slab(pair_rows, pair_gain, pair_weight):
    normed = layer_norm(pair_rows, 1) * pair_gain[None, :, None, None]
    return jnp.einsum("wcqk,ch->whqk", normed, pair_weight, precision=HIGH)


def softmax_rows(scores):
    maximum = jnp.max(scores, axis=-1, keepdims=True)
    exponent = jnp.exp(scores - maximum)
    return exponent / jnp.sum(exponent, axis=-1, keepdims=True)


def window_scores(query_win, key_win, bias_rows, factor):
    raw_scores = jnp.einsum("wqhe,wkhe->whqk", query_win, key_win, preferred_element_type=WIDE)
    return raw_scores * factor + bias_rows.astype(WIDE)


def attend_forward(query_win, key_win, value_win, bias_rows, factor):
    probability = softmax_rows(window_scores(query_win, key_win, bias_rows, factor)).astype(LOWTYPE)
    return jnp.einsum("whqk,wkhe->wqhe", probability, value_win, preferred_element_type=WIDE)


def attend_backward(query_win, key_win, value_win, bias_rows, factor, d_attended):
    probability = softmax_rows(window_scores(query_win, key_win, bias_rows, factor))
    d_probability = jnp.einsum(
        "wqhe,wkhe->whqk", d_attended, value_win, preferred_element_type=WIDE
    )
    d_scores = (
        probability * (d_probability - jnp.sum(probability * d_probability, axis=-1, keepdims=True))
    ).astype(LOWTYPE)
    d_queries = (
        jnp.einsum("whqk,wkhe->wqhe", d_scores, key_win, preferred_element_type=WIDE) * factor
    )
    d_keys = (
        jnp.einsum("whqk,wqhe->wkhe", d_scores, query_win, preferred_element_type=WIDE) * factor
    )
    d_values = jnp.einsum(
        "whqk,wqhe->wkhe", probability.astype(LOWTYPE), d_attended, preferred_element_type=WIDE
    )
    return (d_queries, d_keys, d_values, d_scores)


def atom_windows(queries, key_rows, value_rows, atom_bias, positions):
    windows, head_count, span_query, span_key = atom_bias.shape
    col_count = queries.shape[1]
    head_size = col_count // head_count
    query_win = queries.reshape(windows, span_query, head_count, head_size)
    key_win = key_rows[positions].reshape(windows, span_key, head_count, head_size)
    value_win = value_rows[positions].reshape(windows, span_key, head_count, head_size)
    return (query_win, key_win, value_win, head_size)


def atom_forward_attend(queries, key_rows, value_rows, atom_bias, positions):
    query_win, key_win, value_win, head_size = atom_windows(
        queries, key_rows, value_rows, atom_bias, positions
    )
    attended = attend_forward(query_win, key_win, value_win, atom_bias, head_size ** (-0.5))
    return attended.reshape(queries.shape)


def atom_backward_attend(queries, key_rows, value_rows, d_attended, atom_bias, positions):
    query_win, key_win, value_win, head_size = atom_windows(
        queries, key_rows, value_rows, atom_bias, positions
    )
    atom_count, col_count = queries.shape
    d_window = d_attended.reshape(query_win.shape)
    d_query_win, d_key_win, d_value_win, d_scores = attend_backward(
        query_win, key_win, value_win, atom_bias, head_size ** (-0.5), d_window
    )
    flat_positions = positions.reshape(-1)
    d_keys = (
        jnp.zeros((atom_count, col_count), WIDE)
        .at[flat_positions]
        .add(d_key_win.reshape(-1, col_count))
    )
    d_values = (
        jnp.zeros((atom_count, col_count), WIDE)
        .at[flat_positions]
        .add(d_value_win.reshape(-1, col_count))
    )
    return (d_query_win.reshape(atom_count, col_count), d_keys, d_values, d_scores)


def token_shapes(queries, key_rows, value_rows, token_bias):
    head_count = token_bias.shape[0]
    row_count, col_count = queries.shape
    head_size = col_count // head_count
    shaped = [
        member.reshape(1, row_count, head_count, head_size)
        for member in (queries, key_rows, value_rows)
    ]
    return (shaped, head_size)


def token_forward_attend(queries, key_rows, value_rows, token_bias):
    shaped, head_size = token_shapes(queries, key_rows, value_rows, token_bias)
    attended = attend_forward(
        shaped[0], shaped[1], shaped[2], token_bias[None], head_size ** (-0.5)
    )
    return attended.reshape(queries.shape)


def token_backward_attend(queries, key_rows, value_rows, d_attended, token_bias):
    shaped, head_size = token_shapes(queries, key_rows, value_rows, token_bias)
    d_window = d_attended.reshape(shaped[0].shape)
    d_query_win, d_key_win, d_value_win, d_scores = attend_backward(
        shaped[0], shaped[1], shaped[2], token_bias[None], head_size ** (-0.5), d_window
    )
    return (
        d_query_win.reshape(queries.shape),
        d_key_win.reshape(queries.shape),
        d_value_win.reshape(queries.shape),
        d_scores[0],
    )


def block_forward(features, condition, weights, attend):
    (
        cond_gain,
        cond_weight,
        cond_bias,
        proj_weight,
        query_bias,
        out_weight,
        gu_weight,
        down_weight,
    ) = weights
    col_count = features.shape[1]
    normed_low = cond_norm(condition, cond_gain.astype(WIDE)).astype(LOWTYPE)
    projected = product(normed_low, cond_weight) + cond_bias.astype(WIDE)
    pieces = jnp.split(projected, 6, axis=1)
    normed_one_low = modulate(features, pieces[0], pieces[1]).astype(LOWTYPE)
    raw_proj = product(normed_one_low, proj_weight)
    projections = jnp.concatenate(
        [raw_proj[:, :col_count] + query_bias.astype(WIDE), raw_proj[:, col_count:]], axis=1
    ).astype(LOWTYPE)
    queries, key_rows, value_rows, gate_low = jnp.split(projections, 4, axis=1)
    gate_cols = gate_low.astype(WIDE)
    attended = attend(queries, key_rows, value_rows)
    gated_low = (attended * jax.nn.sigmoid(gate_cols)).astype(LOWTYPE)
    attn_out = product(gated_low, out_weight)
    middle = features + jax.nn.sigmoid(pieces[2]) * attn_out
    normed_two_low = modulate(middle, pieces[3], pieces[4]).astype(LOWTYPE)
    gate_up = product(normed_two_low, gu_weight)
    gate_half, up_half = jnp.split(gate_up, 2, axis=1)
    hidden_low = (jax.nn.silu(gate_half) * up_half).astype(LOWTYPE)
    down_out = product(hidden_low, down_weight)
    result = middle + jax.nn.sigmoid(pieces[5]) * down_out
    stored = (
        normed_low,
        pieces,
        normed_one_low,
        queries,
        key_rows,
        value_rows,
        gate_cols,
        attended,
        gated_low,
        attn_out,
        middle,
        normed_two_low,
        gate_up,
        hidden_low,
        down_out,
    )
    return (result, stored)


def block_backward(features, condition, weights, stored, attend_back, d_result):
    (
        cond_gain,
        cond_weight,
        cond_bias,
        proj_weight,
        query_bias,
        out_weight,
        gu_weight,
        down_weight,
    ) = weights
    (
        normed_low,
        pieces,
        normed_one_low,
        queries,
        key_rows,
        value_rows,
        gate_cols,
        attended,
        gated_low,
        attn_out,
        middle,
        normed_two_low,
        gate_up,
        hidden_low,
        down_out,
    ) = stored
    col_count = features.shape[1]
    d_down = (d_result * jax.nn.sigmoid(pieces[5])).astype(LOWTYPE)
    d_last = d_result * down_out * sigmoid_slope(pieces[5])
    grad_down = product_left(hidden_low, d_down)
    d_hidden = rounded(product_right(d_down, down_weight))
    gate_half, up_half = jnp.split(gate_up, 2, axis=1)
    d_gate_up = jnp.concatenate(
        [d_hidden * up_half * silu_slope(gate_half), d_hidden * jax.nn.silu(gate_half)], axis=1
    ).astype(LOWTYPE)
    grad_updown = product_left(normed_two_low, d_gate_up)
    d_normed_two = product_right(d_gate_up, gu_weight)
    _, modulate_back = jax.vjp(modulate, middle, pieces[3], pieces[4])
    d_middle_part, d_scale_two, d_shift_two = modulate_back(d_normed_two)
    d_middle = d_result + d_middle_part
    d_attn_out = (d_middle * jax.nn.sigmoid(pieces[2])).astype(LOWTYPE)
    d_first = d_middle * attn_out * sigmoid_slope(pieces[2])
    grad_output = product_left(gated_low, d_attn_out)
    d_gated = rounded(product_right(d_attn_out, out_weight))
    d_attended = (d_gated * jax.nn.sigmoid(gate_cols)).astype(LOWTYPE)
    d_gate_cols = d_gated * attended * sigmoid_slope(gate_cols)
    d_queries, d_keys, d_values, d_scores = attend_back(queries, key_rows, value_rows, d_attended)
    d_projections = jnp.concatenate([d_queries, d_keys, d_values, d_gate_cols], axis=1).astype(
        LOWTYPE
    )
    grad_inproj = product_left(normed_one_low, d_projections)
    grad_query = jnp.sum(d_projections[:, :col_count].astype(WIDE), axis=0)
    d_normed_one = product_right(d_projections, proj_weight)
    _, modulate_back = jax.vjp(modulate, features, pieces[0], pieces[1])
    d_features_part, d_scale_one, d_shift_one = modulate_back(d_normed_one)
    d_features = d_middle + d_features_part
    d_projected = jnp.concatenate(
        [d_scale_one, d_shift_one, d_first, d_scale_two, d_shift_two, d_last], axis=1
    ).astype(LOWTYPE)
    grad_condition = product_left(normed_low, d_projected)
    grad_offset = jnp.sum(d_projected.astype(WIDE), axis=0)
    d_normed = product_right(d_projected, cond_weight)
    _, norm_back = jax.vjp(cond_norm, condition, cond_gain.astype(WIDE))
    _, grad_gain = norm_back(d_normed)
    gradients = (
        grad_gain,
        grad_condition,
        grad_offset,
        grad_inproj,
        grad_query,
        grad_output,
        grad_updown,
        grad_down,
    )
    return (d_features, gradients, d_scores.astype(WIDE))


def local(
    atom_features,
    atom_single,
    atom_pairs,
    atom_token,
    window_start,
    pair_repr,
    single_repr,
    noise_table,
    noise_index,
    cotangent,
    atomcond_gain,
    atomcond_weight,
    atomcond_bias,
    atomproj_weight,
    atomquery_bias,
    atomout_weight,
    atomgu_weight,
    atomdown_weight,
    atompair_gain,
    atompair_weight,
    gather_weight,
    tokcond_gain,
    tokcond_weight,
    tokcond_bias,
    tokproj_weight,
    tokquery_bias,
    tokout_weight,
    tokgu_weight,
    tokdown_weight,
    tokpair_gain,
    tokpair_weight,
):
    atom_block = (
        atomcond_gain,
        atomcond_weight,
        atomcond_bias,
        atomproj_weight,
        atomquery_bias,
        atomout_weight,
        atomgu_weight,
        atomdown_weight,
    )
    token_block = (
        tokcond_gain,
        tokcond_weight,
        tokcond_bias,
        tokproj_weight,
        tokquery_bias,
        tokout_weight,
        tokgu_weight,
        tokdown_weight,
    )
    section = lax.axis_index("section")
    sections = lax.axis_size("section")
    length = cotangent.shape[2]

    def mine(member):
        return lax.dynamic_index_in_dim(member, section, 0, keepdims=False)[0]

    rows = pair_repr.shape[0] // sections
    repr_wide = lax.dynamic_slice_in_dim(pair_repr, section * rows, rows, 0).astype(WIDE)
    span = atom_pairs.shape[2] // sections
    pairs_wide = lax.dynamic_slice_in_dim(atom_pairs, section * span, span, 2).astype(WIDE)
    both = ("dp", "section")
    token_part = token_slab(
        repr_wide, tokpair_gain.astype(WIDE), tokpair_weight.astype(WIDE)
    ).astype(LOWTYPE)
    atom_part = atom_slab(
        pairs_wide, atompair_gain.astype(WIDE), atompair_weight.astype(WIDE)
    ).astype(LOWTYPE)
    token_bias = lax.all_gather(token_part, both, axis=1, tiled=True)
    windows = atom_pairs.shape[0] * lax.axis_size("dp")
    atom_bias = lax.all_gather(atom_part[:, :, None], both, axis=0, tiled=True)
    atom_bias = atom_bias.reshape(windows // atom_pairs.shape[0], sections, atom_pairs.shape[0], -1, span, atom_pairs.shape[3])
    atom_bias = atom_bias.transpose(0, 2, 3, 1, 4, 5).reshape(windows, -1, atom_pairs.shape[2], atom_pairs.shape[3])
    positions = window_start[:, None] + jnp.arange(atom_bias.shape[3], dtype=jnp.int32)[None, :]
    onehot_wide = (atom_token[None, :] == jnp.arange(length, dtype=jnp.int32)[:, None]).astype(WIDE)
    counts = jnp.sum(onehot_wide, axis=1, keepdims=True)
    onehot_low = onehot_wide.astype(LOWTYPE)
    atom_cond = atom_single.astype(WIDE)
    atom_fwd = partial(atom_forward_attend, atom_bias=atom_bias, positions=positions)
    atom_bwd = partial(atom_backward_attend, atom_bias=atom_bias, positions=positions)
    token_fwd = partial(token_forward_attend, token_bias=token_bias)
    token_bwd = partial(token_backward_attend, token_bias=token_bias)

    features = mine(atom_features).astype(WIDE)
    condition = single_repr.astype(WIDE) + noise_table[mine(noise_index)]
    result, atom_stored = block_forward(features, atom_cond, atom_block, atom_fwd)
    result_low = result.astype(LOWTYPE)
    pre_act = product(result_low, gather_weight)
    pooled = product(onehot_low, jax.nn.silu(pre_act).astype(LOWTYPE)) / counts
    token_in = pooled.astype(LOWTYPE).astype(WIDE)
    output, token_stored = block_forward(token_in, condition, token_block, token_fwd)

    d_token_in, token_grads, d_token_bias = block_backward(
        token_in, condition, token_block, token_stored, token_bwd, mine(cotangent).astype(WIDE)
    )
    d_scaled = (d_token_in.astype(LOWTYPE).astype(WIDE) / counts).astype(LOWTYPE)
    d_rows = product_left(onehot_low, d_scaled)
    d_pre = (d_rows * silu_slope(pre_act)).astype(LOWTYPE)
    grad_gather = product_left(result_low, d_pre)
    d_result = product_right(d_pre, gather_weight)
    d_features, atom_grads, d_atom_bias = block_backward(
        features, atom_cond, atom_block, atom_stored, atom_bwd, d_result
    )
    slab_token = lax.psum_scatter(d_token_bias.astype(LOWTYPE), both, scatter_dimension=1, tiled=True).astype(WIDE)
    shape = d_atom_bias.shape
    d_atom_bias = d_atom_bias.reshape(-1, atom_pairs.shape[0], shape[1], sections, span, shape[3]).transpose(0, 3, 1, 2, 4, 5)
    d_atom_bias = d_atom_bias.reshape(-1, shape[1], span, shape[3])
    slab_atom = lax.psum_scatter(d_atom_bias.astype(LOWTYPE), both, scatter_dimension=0, tiled=True).astype(WIDE)
    _, token_slab_back = jax.vjp(
        partial(token_slab, repr_wide), tokpair_gain.astype(WIDE), tokpair_weight.astype(WIDE)
    )
    grad_tok_gain, grad_tok_weight = token_slab_back(slab_token)
    _, atom_slab_back = jax.vjp(
        partial(atom_slab, pairs_wide), atompair_gain.astype(WIDE), atompair_weight.astype(WIDE)
    )
    grad_atom_gain, grad_atom_weight = atom_slab_back(slab_atom)
    grads = (
        tuple(atom_grads)
        + (grad_atom_gain, grad_atom_weight, grad_gather)
        + tuple(token_grads)
        + (grad_tok_gain, grad_tok_weight)
    )
    large = [i for i, member in enumerate(grads) if member.size > 500000]
    small = [i for i in range(len(grads)) if i not in large]
    finished = [None] * len(grads)
    flat = jnp.concatenate([grads[i].astype(LOWTYPE).reshape(sections, -1) for i in small], axis=1)
    flat = lax.psum_scatter(flat, "section", scatter_dimension=0, tiled=True)
    flat = lax.psum(flat, "dp")[0].astype(WIDE)
    start = 0
    for i in small:
        size = grads[i].size // sections
        finished[i] = flat[start : start + size].reshape((-1,) + grads[i].shape[1:])
        start += size
    for i in large:
        half = lax.psum_scatter(grads[i].astype(LOWTYPE), "section", scatter_dimension=0, tiled=True)
        finished[i] = lax.psum(half, "dp").astype(WIDE)

    def to_halves(member):
        halves = member.reshape(sections, -1, member.shape[1])
        return lax.all_to_all(halves, "section", 0, 0, tiled=False)[:, None]

    return (to_halves(output.astype(LOWTYPE)), to_halves(d_features.astype(LOWTYPE)).astype(WIDE)) + tuple(finished)


def solution(mesh):
    return jax.shard_map(
        local,
        mesh=mesh,
        in_specs=(
            P(None, "dp", None, None),
            P(),
            P("dp", None, None, None),
            P(),
            P(),
            P("dp", None, None),
            P(),
            P(),
            P(None, "dp"),
            P(None, "dp", None, None),
            P(),
            P(),
            P(),
            P(),
            P(),
            P(),
            P(),
            P(),
            P(),
            P(),
            P(),
            P(),
            P(),
            P(),
            P(),
            P(),
            P(),
            P(),
            P(),
            P(),
            P(),
        ),
        out_specs=(
            P(None, "dp", "section", None),
            P(None, "dp", "section", None),
            P("section"),
            P("section", None),
            P("section"),
            P("section", None),
            P("section"),
            P("section", None),
            P("section", None),
            P("section", None),
            P("section"),
            P("section", None),
            P("section", None),
            P("section"),
            P("section", None),
            P("section"),
            P("section", None),
            P("section"),
            P("section", None),
            P("section", None),
            P("section", None),
            P("section"),
            P("section", None),
        ),
        check_vma=False,
    )
```

```python
import functools

import jax
import jax.numpy as jnp
from jax import lax
from jax.experimental import pallas as pl
from jax.experimental.pallas import tpu as pltpu
from jax.sharding import PartitionSpec as P

EPS = 1e-05
LOWTYPE = jnp.bfloat16
WIDE = jnp.float32
ATOM_ROWS = 256
MEBI = 1024 * 1024


def takes(microseconds):
    return pl.CostEstimate(flops=0, transcendentals=0, bytes_accessed=int(microseconds * 3690000))

FAR = 4


def product(left, right):
    return jnp.dot(left, right, preferred_element_type=WIDE)


def product_left(left, right):
    return lax.dot_general(left, right, (((0,), (0,)), ((), ())), preferred_element_type=WIDE)


def product_right(left, right):
    return lax.dot_general(left, right, (((1,), (1,)), ((), ())), preferred_element_type=WIDE)


def sigmoid(values):
    return jax.nn.sigmoid(values)


def normalise(values):
    centre = values - jnp.mean(values, axis=-1, keepdims=True)
    scale = lax.rsqrt(jnp.mean(centre * centre, axis=-1, keepdims=True) + EPS)
    return centre * scale, scale


def normalise_back(grad, unit, scale):
    return scale * (
        grad
        - jnp.mean(grad, axis=-1, keepdims=True)
        - unit * jnp.mean(grad * unit, axis=-1, keepdims=True)
    )


def column_sum(values):
    return jnp.sum(values, axis=0, keepdims=True)


def low(values):
    return values.astype(LOWTYPE)


def wide(values):
    return values.astype(WIDE)


def head_masks(head_count, head_size, width, kind):
    lanes = lax.broadcasted_iota(jnp.int32, (1, width), 1)
    return [
        jnp.where((lanes >= h * head_size) & (lanes < (h + 1) * head_size), 1.0, 0.0).astype(kind)
        for h in range(head_count)
    ]


def full_spec(member):
    rank = len(member.shape)
    return pl.BlockSpec(member.shape, lambda *_: (0,) * rank)


def atom_forward_kernel(
    starts,
    place,
    features,
    single,
    token_rows,
    bias_own,
    bias_other,
    cond_gain,
    cond_weight,
    cond_bias,
    proj_weight,
    query_bias,
    out_weight,
    gu_weight,
    down_weight,
    gather_weight,
    pooled,
    counts,
    projections,
    attended,
    probability,
    key_wide,
    value_wide,
    pool_sum,
    count_sum,
):
    step = pl.program_id(0)
    blocks = pl.num_programs(0) // 2
    width = features.shape[1]
    _, _, half_group, head_count, span, keys = bias_own.shape
    group = 2 * half_group
    head_size = width // head_count
    factor = head_size**-0.5
    half = gu_weight.shape[1] // 2

    def conditioned(rows, first, last):
        unit, _ = normalise(wide(single[rows, :]))
        normed = low(unit * wide(cond_gain[...]))
        return product(normed, cond_weight[:, first:last]) + wide(cond_bias[:, first:last])

    @pl.when(step < blocks)
    def _():
        rows = pl.ds(pl.multiple_of(step * ATOM_ROWS, ATOM_ROWS), ATOM_ROWS)
        pieces = conditioned(rows, 0, 2 * width)
        unit, _ = normalise(wide(features[rows, :]))
        normed_one = low(unit * sigmoid(pieces[:, :width]) + pieces[:, width:])
        raw = product(normed_one, proj_weight[...])
        queries = low(raw[:, :width] + wide(query_bias[...]))
        rest = low(raw[:, width:])
        projections[rows, :width] = queries
        projections[rows, width:] = rest
        key_wide[rows, :] = wide(rest[:, :width])
        value_wide[rows, :] = wide(rest[:, width : 2 * width])

    @pl.when(step >= blocks)
    def _():
        block = step - blocks
        rows = pl.ds(pl.multiple_of(block * ATOM_ROWS, ATOM_ROWS), ATOM_ROWS)
        masks = head_masks(head_count, head_size, width, LOWTYPE)
        wide_masks = head_masks(head_count, head_size, width, WIDE)
        query_rows = projections[rows, :width]
        parts = []
        for u in range(group):
            start = starts[block * group + u]
            key_win = low(key_wide[pl.ds(start, keys), :])
            value_win = low(value_wide[pl.ds(start, keys), :])
            query_win = query_rows[u * span : (u + 1) * span]
            stacked = jnp.concatenate([query_win * mask for mask in masks], axis=0)
            scores = product_right(stacked, key_win) * factor
            own, other = bias_own[0, 0, u % half_group], bias_other[0, 0, u % half_group]
            bias = jnp.where(place[3] == u // half_group, own, other)
            scores = scores + wide(bias.reshape(head_count * span, keys))
            exponent = jnp.exp(scores - jnp.max(scores, axis=-1, keepdims=True))
            chance = low(exponent / jnp.sum(exponent, axis=-1, keepdims=True))
            probability[u] = chance
            mixed = product(chance, value_win)
            parts.append(
                sum(mixed[h * span : (h + 1) * span] * wide_masks[h] for h in range(head_count))
            )
        mixed = jnp.concatenate(parts, axis=0)
        attended[rows, :] = mixed
        gated = low(mixed * sigmoid(wide(projections[rows, 3 * width :])))
        pieces = conditioned(rows, 2 * width, 6 * width)
        middle = wide(features[rows, :]) + sigmoid(pieces[:, :width]) * product(
            gated, out_weight[...]
        )
        unit, _ = normalise(middle)
        normed_two = low(
            unit * sigmoid(pieces[:, width : 2 * width]) + pieces[:, 2 * width : 3 * width]
        )
        gate_up = product(normed_two, gu_weight[...])
        gate_half = gate_up[:, :half]
        hidden = low(gate_half * sigmoid(gate_half) * gate_up[:, half:])
        result = low(middle + sigmoid(pieces[:, 3 * width :]) * product(hidden, down_weight[...]))
        pre_act = product(result, gather_weight[...])
        pooled_atoms = low(pre_act * sigmoid(pre_act))
        token_ids = token_rows[block]
        tokens = lax.broadcasted_iota(jnp.int32, (pooled.shape[0], ATOM_ROWS), 0)
        onehot = jnp.where(tokens == token_ids, 1.0, 0.0)
        part = product(low(onehot), pooled_atoms)
        part_count = jnp.sum(onehot, axis=1, keepdims=True)

        @pl.when(block == 0)
        def _():
            pool_sum[...] = part
            count_sum[...] = part_count

        @pl.when(block > 0)
        def _():
            pool_sum[...] += part
            count_sum[...] += part_count

        @pl.when(block == blocks - 1)
        def _():
            counts[...] = count_sum[...]
            pooled[...] = low(pool_sum[...] / count_sum[...])


def far_at(run, place):
    distance = run ^ place[1]
    return distance % 2 * 2 + distance // 2


def block_of(step, place):
    return step % 2 ^ place[2], far_at(step // 2, place)


def atom_forward(
    starts, place, features, single, atom_token, bias, weights, gather_weight, length
):
    atoms, width = features.shape
    blocks = atoms // ATOM_ROWS
    _, _, half_group, head_count, span, keys = bias[0].shape
    windows = 2 * half_group * blocks
    model_width = gather_weight.shape[1]
    token_rows = atom_token.reshape(blocks, 1, ATOM_ROWS)
    flat = [member[None] if member.ndim == 1 else member for member in weights]
    whole = [features, single, token_rows]

    def bias_block(i, starts, place):
        near, far = block_of(jnp.maximum(i - blocks, 0), place)
        return near, far, 0, 0, 0, 0

    later3 = lambda i, *_: (jnp.maximum(i - blocks, 0), 0, 0)
    outs = [
        jax.ShapeDtypeStruct((length, model_width), LOWTYPE),
        jax.ShapeDtypeStruct((length, 1), WIDE),
        jax.ShapeDtypeStruct((atoms, 4 * width), LOWTYPE),
        jax.ShapeDtypeStruct((atoms, width), WIDE),
        jax.ShapeDtypeStruct((windows, head_count * span, keys), LOWTYPE),
    ]
    return pl.pallas_call(
        atom_forward_kernel,
        grid_spec=pltpu.PrefetchScalarGridSpec(
            num_scalar_prefetch=2,
            grid=(2 * blocks,),
            in_specs=[full_spec(member) for member in whole]
            + [pl.BlockSpec((1, 1, half_group, head_count, span, keys), bias_block)] * 2
            + [full_spec(member) for member in flat + [gather_weight]],
            out_specs=[full_spec(member) for member in outs[:4]]
            + [pl.BlockSpec((2 * half_group, head_count * span, keys), later3)],
            scratch_shapes=[
                pltpu.VMEM((atoms, width), WIDE),
                pltpu.VMEM((atoms, width), WIDE),
                pltpu.VMEM((length, model_width), WIDE),
                pltpu.VMEM((length, 1), WIDE),
            ],
        ),
        out_shape=outs,
        cost_estimate=takes(40),
        compiler_params=pltpu.CompilerParams(
            dimension_semantics=("arbitrary",), vmem_limit_bytes=48 * MEBI
        ),
        name="atom_forward",
    )(starts, place, *whole, *bias, *flat, gather_weight)


def atom_tokens_back_kernel(
    features,
    single,
    token_cols,
    gates,
    attended,
    d_tokens,
    counts,
    cond_gain,
    cond_weight,
    cond_bias,
    out_weight,
    gu_weight,
    down_weight,
    gather_weight,
    d_attended,
    d_gates,
    d_middles,
    d_pieces,
    packed,
    grad_out,
    grad_gu,
    grad_down,
    grad_gather,
):
    step = pl.program_id(0)
    blocks = pl.num_programs(0)
    width = features.shape[1]
    half = gu_weight.shape[1] // 2

    @pl.when(step == 0)
    def _():
        for member in (grad_out, grad_gu, grad_down, grad_gather):
            member[...] = jnp.zeros_like(member)

    rows = slice(None)
    unit, _ = normalise(wide(single[rows, :]))
    normed = low(unit * wide(cond_gain[...]))
    pieces = product(normed, cond_weight[:, 2 * width :]) + wide(cond_bias[:, 2 * width :])
    mixed = attended[rows, :]
    gate = sigmoid(wide(gates[rows, :]))
    gated = low(mixed * gate)
    attn_out = product(gated, out_weight[...])
    gate_one = sigmoid(pieces[:, :width])
    middle = wide(features[rows, :]) + gate_one * attn_out
    unit_two, spread_two = normalise(middle)
    scale_two = sigmoid(pieces[:, width : 2 * width])
    normed_two = low(unit_two * scale_two + pieces[:, 2 * width : 3 * width])
    gate_up = product(normed_two, gu_weight[...])
    gate_half, up_half = gate_up[:, :half], gate_up[:, half:]
    logistic = sigmoid(gate_half)
    hidden = low(gate_half * logistic * up_half)
    down_out = product(hidden, down_weight[...])
    gate_two = sigmoid(pieces[:, 3 * width :])
    result = low(middle + gate_two * down_out)
    pre_act = product(result, gather_weight[...])

    d_scaled = low(wide(d_tokens[...]) / counts[...])
    tokens = lax.broadcasted_iota(jnp.int32, (ATOM_ROWS, d_tokens.shape[0]), 1)
    onehot = low(jnp.where(tokens == token_cols[...], 1.0, 0.0))
    d_rows = product(onehot, d_scaled)
    pre_logistic = sigmoid(pre_act)
    d_pre = low(d_rows * (pre_logistic * (1.0 + pre_act * (1.0 - pre_logistic))))
    grad_gather[...] += product_left(result, d_pre)
    d_result = product_right(d_pre, gather_weight[...])

    d_down = low(d_result * gate_two)
    d_pieces[rows, 3 * width :] = low(d_result * down_out * gate_two * (1.0 - gate_two))
    grad_down[...] += product_left(hidden, d_down)
    d_hidden = wide(low(product_right(d_down, down_weight[...])))
    d_gate_half = low(d_hidden * up_half * logistic * (1.0 + gate_half * (1.0 - logistic)))
    d_up_half = low(d_hidden * gate_half * logistic)
    d_gate_up = jnp.concatenate([d_gate_half, d_up_half], axis=1)
    grad_gu[...] += product_left(normed_two, d_gate_up)
    d_normed_two = product_right(d_gate_up, gu_weight[...])
    d_pieces[rows, 2 * width : 3 * width] = low(d_normed_two)
    d_pieces[rows, width : 2 * width] = low(
        d_normed_two * unit_two * scale_two * (1.0 - scale_two)
    )
    d_middle = d_result + normalise_back(d_normed_two * scale_two, unit_two, spread_two)
    d_middles[rows, :] = d_middle
    d_attn_out = low(d_middle * gate_one)
    d_pieces[rows, :width] = low(
        d_middle * attn_out * gate_one * (1.0 - gate_one)
    )
    grad_out[...] += product_left(gated, d_attn_out)
    d_gated = wide(low(product_right(d_attn_out, out_weight[...])))
    d_attended[rows, :] = low(d_gated * gate)
    d_gates[rows, :] = low(d_gated * mixed * gate * (1.0 - gate))

    @pl.when(step == blocks - 1)
    def _():
        model_width = gather_weight.shape[1]
        packed[:, :model_width] = low(grad_gather[...])
        last = model_width + 2 * half
        packed[:, model_width:last] = low(grad_gu[...])
        packed[:, last : last + width] = low(grad_out[...])
        last = last + width
        run = grad_down.shape[0] // 4
        for part in range(4):
            rows_at = slice(part // 2 * run, (part // 2 + 1) * run)
            columns = slice(last + part % 2 * width, last + (part % 2 + 1) * width)
            packed[rows_at, columns] = low(grad_down[part * run : (part + 1) * run, :])


def atom_attention_back_kernel(
    starts,
    place,
    projections,
    attended,
    probability,
    d_attended,
    d_projections,
    d_bias_own,
    d_bias_other,
    key_wide,
    value_wide,
    d_keys,
    d_values,
):
    step = pl.program_id(0)
    blocks = pl.num_programs(0)
    width = attended.shape[1]
    group, stack, keys = probability.shape
    half_group = group // 2
    span = ATOM_ROWS // group
    head_count = stack // span
    head_size = width // head_count
    factor = head_size**-0.5

    @pl.when(step == 0)
    def _():
        for member in (d_keys, d_values):
            member[...] = jnp.zeros_like(member)
        key_wide[...] = wide(projections[:, width : 2 * width])
        value_wide[...] = wide(projections[:, 2 * width : 3 * width])

    rows = pl.ds(pl.multiple_of(step * ATOM_ROWS, ATOM_ROWS), ATOM_ROWS)
    row_grad = d_attended[...]
    row_part = wide(row_grad) * attended[...]

    masks = head_masks(head_count, head_size, width, LOWTYPE)
    wide_masks = head_masks(head_count, head_size, width, WIDE)
    query_rows = projections[rows, :width]
    score_grads, query_grads = [], []
    for u in range(group):
        start = starts[step * group + u]
        cut = slice(u * span, (u + 1) * span)
        key_win = low(key_wide[pl.ds(start, keys), :])
        value_win = low(value_wide[pl.ds(start, keys), :])
        stacked_query = jnp.concatenate([query_rows[cut] * mask for mask in masks], axis=0)
        stacked_grad = jnp.concatenate([row_grad[cut] * mask for mask in masks], axis=0)
        stacked_part = jnp.concatenate([row_part[cut] * mask for mask in wide_masks], axis=0)
        row_sum = jnp.sum(stacked_part, axis=-1, keepdims=True)
        chance = probability[u]
        d_chance = product_right(stacked_grad, value_win)
        d_scores = low(wide(chance) * (d_chance - row_sum))
        score_grads.append(d_scores)
        d_stacked = product(d_scores, key_win) * factor
        query_grads.append(
            sum(d_stacked[h * span : (h + 1) * span] * wide_masks[h] for h in range(head_count))
        )
        d_keys[pl.ds(start, keys), :] += product_left(d_scores, stacked_query) * factor
        d_values[pl.ds(start, keys), :] += product_left(chance, stacked_grad)
    d_projections[rows, :width] = low(jnp.concatenate(query_grads, axis=0))
    for u in range(half_group):
        first = place[3] == 0
        d_bias_own[0, 0, u] = jnp.where(first, score_grads[u], score_grads[u + half_group])
        d_bias_other[0, 0, u] = jnp.where(first, score_grads[u + half_group], score_grads[u])

    @pl.when(step == blocks - 1)
    def _():
        d_projections[:, width : 2 * width] = low(d_keys[...])
        d_projections[:, 2 * width : 3 * width] = low(d_values[...])


def atom_features_back_kernel(
    features,
    single,
    d_projections,
    d_gates,
    d_middles,
    d_pieces,
    cond_gain,
    cond_weight,
    cond_bias,
    proj_weight,
    d_features,
    packed,
    grad_gain,
    grad_offset,
    grad_query,
    grad_cond,
    grad_proj,
):
    step = pl.program_id(0)
    blocks = pl.num_programs(0)
    width = features.shape[1]

    @pl.when(step == 0)
    def _():
        for member in (grad_gain, grad_offset, grad_query, grad_cond, grad_proj):
            member[...] = jnp.zeros_like(member)

    unit, _ = normalise(wide(single[...]))
    normed = low(unit * wide(cond_gain[...]))
    pieces = product(normed, cond_weight[:, : 2 * width]) + wide(cond_bias[:, : 2 * width])
    unit_one, spread_one = normalise(wide(features[...]))
    scale_one = sigmoid(pieces[:, :width])
    normed_one = low(unit_one * scale_one + pieces[:, width:])
    d_projection = jnp.concatenate([d_projections[...], d_gates[...]], axis=1)
    grad_proj[...] += product_left(normed_one, d_projection)
    grad_query[...] += column_sum(wide(d_projection[:, :width]))
    d_normed_one = product_right(d_projection, proj_weight[...])
    d_features[...] = d_middles[...] + normalise_back(
        d_normed_one * scale_one, unit_one, spread_one
    )
    d_projected = jnp.concatenate(
        [
            low(d_normed_one * unit_one * scale_one * (1.0 - scale_one)),
            low(d_normed_one),
            d_pieces[...],
        ],
        axis=1,
    )
    grad_cond[...] += product_left(normed, d_projected)
    grad_offset[...] += column_sum(wide(d_projected))
    d_normed = product_right(d_projected, cond_weight[...])
    grad_gain[...] += column_sum(d_normed * unit)

    @pl.when(step == blocks - 1)
    def _():
        packed[:, : 6 * width] = low(grad_cond[...])
        packed[:, 6 * width :] = low(grad_proj[...])


def atom_tokens_back(features, single, atom_token, d_tokens, counts, stored, weights, gather_weight):
    projections, attended, _ = stored
    atoms, width = features.shape
    gain, cond, offset, _, _, out, gu, down = weights
    flat = [gain[None], cond, offset[None], out, gu, down, gather_weight]
    token_cols = atom_token.reshape(atoms, 1)
    columns = gather_weight.shape[1] + gu.shape[1] + 3 * width
    outs = [
        jax.ShapeDtypeStruct((atoms, width), LOWTYPE),
        jax.ShapeDtypeStruct((atoms, width), LOWTYPE),
        jax.ShapeDtypeStruct((atoms, width), WIDE),
        jax.ShapeDtypeStruct((atoms, 4 * width), LOWTYPE),
        jax.ShapeDtypeStruct((width, columns), LOWTYPE),
    ]

    def rows_of(member):
        return pl.BlockSpec((ATOM_ROWS, member.shape[1]), lambda i: (i, 0))

    return pl.pallas_call(
        atom_tokens_back_kernel,
        grid=(atoms // ATOM_ROWS,),
        in_specs=[
            rows_of(features),
            rows_of(single),
            rows_of(token_cols),
            pl.BlockSpec((ATOM_ROWS, width), lambda i: (i, 3)),
            rows_of(attended),
            full_spec(d_tokens),
            full_spec(counts),
        ]
        + [full_spec(member) for member in flat],
        out_specs=[rows_of(member) for member in outs[:4]] + [full_spec(outs[4])],
        out_shape=outs,
        scratch_shapes=[
            pltpu.VMEM(member.shape, WIDE) for member in (out, gu, down, gather_weight)
        ],
        cost_estimate=takes(3),
        compiler_params=pltpu.CompilerParams(
            dimension_semantics=("arbitrary",), vmem_limit_bytes=48 * MEBI
        ),
        name="atom_tokens_back",
    )(features, single, token_cols, projections, attended, d_tokens, counts, *flat)


def atom_attention_back(starts, place, d_attended, stored):
    projections, attended, probability = stored
    atoms, width = attended.shape
    blocks = atoms // ATOM_ROWS
    windows, stack, keys = probability.shape
    group = windows // blocks
    score_shape = (2, blocks // 2, group // 2, stack, keys)
    outs = [
        jax.ShapeDtypeStruct((atoms, 3 * width), LOWTYPE),
        jax.ShapeDtypeStruct(score_shape, LOWTYPE),
        jax.ShapeDtypeStruct(score_shape, LOWTYPE),
    ]

    def bias_block(i, starts, place):
        near, far = block_of(i, place)
        return near, far, 0, 0, 0

    block = pl.BlockSpec((ATOM_ROWS, width), lambda i, *_: (i, 0))
    return pl.pallas_call(
        atom_attention_back_kernel,
        grid_spec=pltpu.PrefetchScalarGridSpec(
            num_scalar_prefetch=2,
            grid=(blocks,),
            in_specs=[
                full_spec(projections),
                block,
                pl.BlockSpec((group, stack, keys), lambda i, *_: (i, 0, 0)),
                block,
            ],
            out_specs=[full_spec(outs[0])]
            + [pl.BlockSpec((1, 1, group // 2, stack, keys), bias_block)] * 2,
            scratch_shapes=[pltpu.VMEM((atoms, width), WIDE)] * 4,
        ),
        out_shape=outs,
        cost_estimate=takes(2),
        compiler_params=pltpu.CompilerParams(
            dimension_semantics=("arbitrary",), vmem_limit_bytes=48 * MEBI
        ),
        name="atom_attention_back",
    )(starts, place, projections, attended, probability, d_attended)


def atom_features_back(features, single, d_projections, d_gates, d_middles, d_pieces, weights):
    atoms, width = features.shape
    gain, cond, offset, proj = weights[:4]
    flat = [gain[None], cond, offset[None], proj]
    rows = [features, single, d_projections, d_gates, d_middles, d_pieces]
    outs = [
        jax.ShapeDtypeStruct((atoms, width), WIDE),
        jax.ShapeDtypeStruct((width, 10 * width), LOWTYPE),
        jax.ShapeDtypeStruct((1, width), WIDE),
        jax.ShapeDtypeStruct((1, 6 * width), WIDE),
        jax.ShapeDtypeStruct((1, width), WIDE),
    ]
    return pl.pallas_call(
        atom_features_back_kernel,
        grid=(atoms // ATOM_ROWS,),
        in_specs=[
            pl.BlockSpec((ATOM_ROWS, member.shape[1]), lambda i: (i, 0)) for member in rows
        ]
        + [full_spec(member) for member in flat],
        out_specs=[pl.BlockSpec((ATOM_ROWS, width), lambda i: (i, 0))]
        + [full_spec(member) for member in outs[1:]],
        out_shape=outs,
        scratch_shapes=[pltpu.VMEM(cond.shape, WIDE), pltpu.VMEM(proj.shape, WIDE)],
        cost_estimate=takes(0.5),
        compiler_params=pltpu.CompilerParams(
            dimension_semantics=("arbitrary",), vmem_limit_bytes=32 * MEBI
        ),
        name="atom_features_back",
    )(*rows, *flat)


LANES = 128
GROUP_HEADS = 8


def head_window(head, head_size, total):
    first = min(head * head_size // LANES * LANES, total - 2 * LANES)
    return first, head * head_size - first


def head_lanes(offset, head_size, kind):
    lanes = lax.broadcasted_iota(jnp.int32, (1, 2 * LANES), 1)
    return jnp.where((lanes >= offset) & (lanes < offset + head_size), 1.0, 0.0).astype(kind)


def chosen_rows(place, own, other, head):
    parts = []
    for near in range(2):
        for core in range(2):
            for section in range(2):
                at = (near ^ place[2], section ^ place[0])
                parts.append(
                    jnp.where(place[3] == core, own[(*at, 0, head)], other[(*at, 0, head)])
                )
    return jnp.concatenate(parts, axis=0)


def token_forward_kernel(
    place, queries, keys, values, gates, own_a, other_a, own_b, other_b, probability, attended, gated
):
    heads = probability.shape[0]
    rows, total = queries.shape
    head_size = total // heads
    factor = head_size**-0.5

    def attend(own, other):
        tiles = [None] * (total // LANES)
        for h in range(heads):
            first, offset = head_window(h, head_size, total)
            cut = slice(first, first + 2 * LANES)
            mask = head_lanes(offset, head_size, LOWTYPE)
            scores = product_right(queries[:, cut] * mask, keys[:, cut]) * factor
            scores = scores + wide(chosen_rows(place, own, other, h))
            exponent = jnp.exp(scores - jnp.max(scores, axis=-1, keepdims=True))
            chance = low(exponent * (1.0 / jnp.sum(exponent, axis=-1, keepdims=True)))
            probability[h] = chance
            mixed = product(chance, values[:, cut]) * wide(mask)
            for t in range(2):
                at = first // LANES + t
                part = mixed[:, t * LANES : (t + 1) * LANES]
                tiles[at] = part if tiles[at] is None else tiles[at] + part
        whole = jnp.concatenate(tiles, axis=1)
        attended[...] = whole
        gated[...] = low(whole * sigmoid(wide(gates[...])))

    @pl.when(pl.program_id(0) == 0)
    def _():
        attend(own_a, other_a)

    @pl.when(pl.program_id(0) == 1)
    def _():
        attend(own_b, other_b)


def bias_spec(member, group):
    shape = member.shape
    resting = 0 if group else FAR - 1

    def index(g, i, place):
        run = jnp.where(g == group, i, resting)
        return 0, 0, far_at(run, place), 0, 0, 0

    return pl.BlockSpec((*shape[:2], 1, *shape[3:]), index)


def token_forward(place, projections, bias):
    length, columns = projections.shape
    width = columns // 4
    rows = length // FAR
    group_heads = bias[0].shape[3]
    groups = len(bias) // 2
    heads = group_heads * groups
    total = width // groups
    block = pl.BlockSpec((rows, total), lambda g, i, _: (i, g))
    return pl.pallas_call(
        token_forward_kernel,
        grid_spec=pltpu.PrefetchScalarGridSpec(
            num_scalar_prefetch=1,
            grid=(groups, FAR),
            in_specs=[
                block,
                pl.BlockSpec((length, total), lambda g, i, _: (0, groups + g)),
                pl.BlockSpec((length, total), lambda g, i, _: (0, 2 * groups + g)),
                pl.BlockSpec((rows, total), lambda g, i, _: (i, 3 * groups + g)),
            ]
            + [bias_spec(member, index // 2) for index, member in enumerate(bias)],
            out_specs=[
                pl.BlockSpec((group_heads, rows, length), lambda g, i, _: (g, i, 0)),
                block,
                block,
            ],
        ),
        out_shape=[
            jax.ShapeDtypeStruct((heads, length, length), LOWTYPE),
            jax.ShapeDtypeStruct((length, width), WIDE),
            jax.ShapeDtypeStruct((length, width), LOWTYPE),
        ],
        cost_estimate=takes(31),
        compiler_params=pltpu.CompilerParams(
            dimension_semantics=("arbitrary", "arbitrary"), vmem_limit_bytes=48 * MEBI
        ),
        name="token_forward",
    )(place, projections, projections, projections, projections, *bias)


def token_backward_kernel(
    place,
    queries,
    keys,
    values,
    gates,
    probability,
    attended,
    d_gated,
    own,
    other,
    d_projections,
    d_keys,
    d_values,
):
    group, step = pl.program_id(0), pl.program_id(1)
    heads = probability.shape[0]
    rows, total = queries.shape
    head_size = total // heads
    factor = head_size**-0.5
    width = d_projections.shape[1] // 4
    run = own.shape[4]

    @pl.when(step == 0)
    def _():
        d_keys[...] = jnp.zeros_like(d_keys)
        d_values[...] = jnp.zeros_like(d_values)

    gate = sigmoid(wide(gates[...]))
    grad = wide(d_gated[...])
    mixed = attended[...]
    d_attended = low(grad * gate)
    d_gates = low(grad * mixed * gate * (1.0 - gate))
    row_part = wide(d_attended) * mixed
    tiles = [None] * (total // LANES)
    for h in range(heads):
        first, offset = head_window(h, head_size, total)
        cut = slice(first, first + 2 * LANES)
        mask = head_lanes(offset, head_size, LOWTYPE)
        row_sum = jnp.sum(row_part[:, cut] * wide(mask), axis=-1, keepdims=True)
        head_grad = d_attended[:, cut] * mask
        chance = probability[h]
        d_scores = low(wide(chance) * (product_right(head_grad, values[:, cut]) - row_sum))
        for near in range(2):
            for section in range(2):
                at = (near ^ place[2], section ^ place[0], 0, h)
                pair = []
                for core in range(2):
                    start = (4 * near + 2 * core + section) * run
                    pair.append(d_scores[start : start + run])
                own[at] = jnp.where(place[3] == 0, pair[0], pair[1])
                other[at] = jnp.where(place[3] == 0, pair[1], pair[0])
        part = product(d_scores, keys[:, cut]) * (wide(mask) * factor)
        for t in range(2):
            at = first // LANES + t
            piece = part[:, t * LANES : (t + 1) * LANES]
            tiles[at] = piece if tiles[at] is None else tiles[at] + piece
        d_keys[:, cut] += product_left(d_scores, queries[:, cut] * mask)
        d_values[:, cut] += product_left(chance, head_grad)
    rows_at = pl.ds(pl.multiple_of(step * rows, rows), rows)
    first = group * total
    d_projections[rows_at, pl.ds(pl.multiple_of(first, LANES), total)] = low(
        jnp.concatenate(tiles, axis=1)
    )
    gates_at = pl.ds(pl.multiple_of(first + 3 * width, LANES), total)
    d_projections[rows_at, gates_at] = d_gates

    @pl.when(step == pl.num_programs(1) - 1)
    def _():
        first = group * total
        d_projections[:, pl.ds(pl.multiple_of(first + width, LANES), total)] = low(
            d_keys[...] * factor
        )
        d_projections[:, pl.ds(pl.multiple_of(first + 2 * width, LANES), total)] = low(
            d_values[...]
        )


def token_backward(place, projections, probability, attended, d_gated, run):
    length, columns = projections.shape
    width = columns // 4
    rows = length // FAR
    heads = probability.shape[0]
    groups = heads // GROUP_HEADS
    total = width // groups
    block = pl.BlockSpec((rows, total), lambda g, i, _: (i, g))
    grad = jax.ShapeDtypeStruct((2, 2, FAR, heads, run, length), LOWTYPE)
    grad_spec = pl.BlockSpec(
        (2, 2, 1, GROUP_HEADS, run, length), lambda g, i, place: (0, 0, far_at(i, place), g, 0, 0)
    )
    return pl.pallas_call(
        token_backward_kernel,
        grid_spec=pltpu.PrefetchScalarGridSpec(
            num_scalar_prefetch=1,
            grid=(groups, FAR),
            in_specs=[
                block,
                pl.BlockSpec((length, total), lambda g, i, _: (0, groups + g)),
                pl.BlockSpec((length, total), lambda g, i, _: (0, 2 * groups + g)),
                pl.BlockSpec((rows, total), lambda g, i, _: (i, 3 * groups + g)),
                pl.BlockSpec((GROUP_HEADS, rows, length), lambda g, i, _: (g, i, 0)),
                block,
                block,
            ],
            out_specs=[grad_spec] * 2
            + [pl.BlockSpec((length, columns), lambda g, i, _: (0, 0))],
            scratch_shapes=[pltpu.VMEM((length, total), WIDE)] * 2,
        ),
        out_shape=[grad] * 2 + [jax.ShapeDtypeStruct((length, columns), LOWTYPE)],
        cost_estimate=takes(8),
        compiler_params=pltpu.CompilerParams(
            dimension_semantics=("arbitrary", "arbitrary"), vmem_limit_bytes=48 * MEBI
        ),
        name="token_backward",
    )(place, projections, projections, projections, projections, probability, attended, d_gated)


PIECES = 8
COLUMNS = 384


def places():
    place = lax.axis_index("dp")
    return lax.axis_index("section"), place // 4, place // 2 % 2, place % 2


def swap_section(member):
    return lax.ppermute(member, "section", [(0, 1), (1, 0)])


def swap_bit(member, bit):
    return lax.ppermute(member, "dp", [(i, i ^ (1 << bit)) for i in range(lax.axis_size("dp"))])


def swap_core(member):
    return swap_bit(member, 0)


def swap_near(member):
    return swap_bit(member, 1)


def swap_far(member, bit):
    return swap_bit(member, 2 + bit)


def more_bits():
    return range(4, (lax.axis_size("dp") - 1).bit_length())


def piece_index():
    place = lax.axis_index("dp")
    return place // 2 % 2 * 4 + place // 4 % 2 * 2 + place // 8 % 2


def run_of(member, index, count):
    rows = member.shape[0] // count
    return lax.dynamic_slice_in_dim(member, index * rows, rows, 0)


def add_low(*members):
    return low(sum(wide(member) for member in members))


def scatter_plane(member):
    for bit, half in ((2, 2), (3, 1)):
        member = add_low(member[:half], swap_bit(member[half:], bit))
    for bit in more_bits():
        member = add_low(member, swap_bit(member, bit))
    return member


def rest_sum(*members):
    total = add_low(*members)
    for bit in more_bits():
        total = add_low(total, swap_bit(total, bit))
    return total


def from_here(member):
    half = member.shape[1] // 2
    first, second = member[:, :half], member[:, half:]
    turned = jnp.concatenate([second, first], axis=1)
    return jnp.where(lax.axis_index("section") == 0, member, turned)


def gather_pieces(member):
    for bit in (3, 2, 1):
        member = jnp.concatenate([member, swap_bit(member, bit)], axis=0)
    return member


class Weight:
    def __init__(self, rows, columns):
        self.rows, self.columns = rows // 2, columns
        self.blocks = columns // 2 // COLUMNS
        self.run = self.blocks * self.rows // PIECES

    def segments(self, piece):
        at, last, found = piece * self.run, (piece + 1) * self.run, []
        while at < last:
            block, row = divmod(at, self.rows)
            size = min(self.rows - row, last - at)
            found.append((block, row, size, at - piece * self.run))
            at += size
        return found


def aligned(start, size, step):
    return pl.ds(pl.multiple_of(start, step), size)


def product_blocks(place, weights, members, core, half):
    found, at = [], 0
    for weight in weights:
        if weight.direct:
            held = members[at]
            at += 1
        else:
            left, right = members[at], members[at + 1]
            at += 2
            if weight.rows % LANES:
                side = left[:, half * weight.rows : (half + 1) * weight.rows]
            else:
                side = left[:, aligned((half ^ place[0]) * weight.rows, weight.rows, LANES)]
        blocks = []
        for block in range(weight.blocks):
            columns = aligned(
                core * (weight.columns // 2) + block * COLUMNS, COLUMNS, LANES
            )
            if weight.direct:
                rows = aligned((half ^ place[0]) * weight.rows, weight.rows, 16)
                blocks.append(wide(held[rows, columns]))
            else:
                blocks.append(product_left(side, right[:, columns]))
        found.append(blocks)
    return found


def store_pieces(place, weights, found, store):
    for piece in range(PIECES):
        at = 0
        for weight, blocks in zip(weights, found):
            for block, row, size, offset in weight.segments(piece):
                store(piece ^ place[4], slice(at + offset, at + offset + size), blocks[block][row : row + size])
            at += weight.run


def given_kernel(weights, place, *refs):
    *members, out = refs
    for half in range(2):

        @pl.when(pl.program_id(0) == half)
        def _(half=half):
            def store(piece, rows, values):
                out[0, piece, rows, :] = low(values)

            store_pieces(
                place, weights, product_blocks(place, weights, members, 1 - place[3], half), store
            )


def kept_kernel(weights, place, *refs):
    *members, received, given, kept = refs
    for step, (half, target) in enumerate(((1, given), (0, kept))):

        @pl.when(pl.program_id(0) == step)
        def _(half=half, target=target):
            def store(piece, rows, values):
                target[piece, rows, :] = low(values + wide(received[0, piece, rows, :]))

            store_pieces(
                place, weights, product_blocks(place, weights, members, place[3], half), store
            )


def chunk_rows(weights):
    return sum(weight.run for weight in weights)


def chunk_given(place, weights, members):
    block = (1, PIECES, chunk_rows(weights), COLUMNS)
    return pl.pallas_call(
        functools.partial(given_kernel, weights),
        grid_spec=pltpu.PrefetchScalarGridSpec(
            num_scalar_prefetch=1,
            grid=(2,),
            in_specs=[full_spec(member) for member in members],
            out_specs=pl.BlockSpec(block, lambda i, _: (i, 0, 0, 0)),
        ),
        out_shape=jax.ShapeDtypeStruct((2, *block[1:]), LOWTYPE),
        cost_estimate=takes(15),
        compiler_params=pltpu.CompilerParams(
            dimension_semantics=("arbitrary",), vmem_limit_bytes=48 * MEBI
        ),
        name="chunk_given",
    )(place, *members)


def chunk_kept(place, weights, members, received):
    block = (1, PIECES, chunk_rows(weights), COLUMNS)
    out = jax.ShapeDtypeStruct(block[1:], LOWTYPE)
    return pl.pallas_call(
        functools.partial(kept_kernel, weights),
        grid_spec=pltpu.PrefetchScalarGridSpec(
            num_scalar_prefetch=1,
            grid=(2,),
            in_specs=[full_spec(member) for member in members]
            + [pl.BlockSpec(block, lambda i, _: (1 - i, 0, 0, 0))],
            out_specs=[full_spec(out), full_spec(out)],
        ),
        out_shape=[out, out],
        cost_estimate=takes(20),
        compiler_params=pltpu.CompilerParams(
            dimension_semantics=("arbitrary",), vmem_limit_bytes=48 * MEBI
        ),
        name="chunk_kept",
    )(place, *members, received)


def assemble_kernel(weights, place, own, other, *outs):
    for source, core in ((own, place[3]), (other, 1 - place[3])):
        for piece in range(PIECES):
            at = 0
            for weight, out in zip(weights, outs):
                for block, row, size, offset in weight.segments(piece):
                    columns = aligned(
                        core * (weight.columns // 2) + block * COLUMNS, COLUMNS, LANES
                    )
                    rows = slice(at + offset, at + offset + size)
                    out[row : row + size, columns] = wide(source[piece ^ place[4], rows, :])
                at += weight.run


def assemble(place, weights, own, other):
    outs = [jax.ShapeDtypeStruct((weight.rows, weight.columns), WIDE) for weight in weights]
    return pl.pallas_call(
        functools.partial(assemble_kernel, weights),
        grid_spec=pltpu.PrefetchScalarGridSpec(
            num_scalar_prefetch=1,
            grid=(1,),
            in_specs=[full_spec(own), full_spec(other)],
            out_specs=[full_spec(member) for member in outs],
        ),
        out_shape=outs,
        cost_estimate=takes(2),
        compiler_params=pltpu.CompilerParams(
            dimension_semantics=("arbitrary",), vmem_limit_bytes=48 * MEBI
        ),
        name="assemble",
    )(place, own, other)


def products(*shapes):
    weights = [Weight(*shape) for shape in shapes]
    for weight in weights:
        weight.direct = False
    return weights


def vector_sum(member):
    section = lax.axis_index("section")
    kept = lax.dynamic_index_in_dim(member, section, 0, keepdims=False)
    total = kept + swap_section(lax.dynamic_index_in_dim(member, 1 - section, 0, keepdims=False))
    for bit in range((lax.axis_size("dp") - 1).bit_length()):
        total = total + swap_bit(total, bit)
    return total


def half_block(shape, count=2):
    axis = len(shape) - 2
    if shape[axis] % (16 * count):
        axis -= 1
    block = list(shape)
    block[axis] //= count
    return pl.BlockSpec(tuple(block), lambda i: tuple(i if a == axis else 0 for a in range(len(shape))))


def exchange_kernel(entries, *refs):
    refs = list(refs)
    members = [[refs.pop(0) for _ in range(1 + count)] for _, count in entries]
    for (axis, _), (kept, *got) in zip(entries, members):
        if axis == "join":
            out = refs.pop(0)
            rows = kept.shape[0]
            for index, member in enumerate([kept, *got]):
                out[index * rows : (index + 1) * rows] = member[...]
        elif axis == "far":
            rows = got[0].shape[0]
            refs.pop(0)[...] = low(
                wide(kept[:rows]) + wide(got[0][...]) + wide(got[1][...]) + wide(got[2][...])
            )
        elif axis is None:
            refs.pop(0)[...] = low(wide(kept[...]) + wide(got[0][...]))
        else:
            for side in range(2):
                at = (slice(None),) * axis + (side,)
                refs.pop(0)[...] = low(wide(kept[at]) + wide(got[0][at]))


def exchange(*entries):
    shapes, inputs, kinds = [], [], []
    for axis, kept, got in entries:
        got = list(got) if isinstance(got, (list, tuple)) else [got]
        inputs += [kept, *got]
        kinds.append((axis, len(got)))
        if axis == "join":
            shapes.append(((1 + len(got)) * kept.shape[0], *kept.shape[1:]))
        elif axis == "far":
            shapes.append(got[0].shape)
        elif axis is None:
            shapes.append(kept.shape)
        else:
            shapes += [kept.shape[:axis] + kept.shape[axis + 1 :]] * 2
    return pl.pallas_call(
        functools.partial(exchange_kernel, kinds),
        grid=(2,),
        in_specs=[half_block(member.shape) for member in inputs],
        out_specs=[half_block(shape) for shape in shapes],
        out_shape=[jax.ShapeDtypeStruct(shape, LOWTYPE) for shape in shapes],
        cost_estimate=takes(0.5),
        compiler_params=pltpu.CompilerParams(
            dimension_semantics=("arbitrary",), vmem_limit_bytes=48 * MEBI
        ),
        name="exchange",
    )(*inputs)


def swap_plane(member, distance):
    size = lax.axis_size("dp")
    return lax.ppermute(member, "dp", [(i, i ^ (distance << 2)) for i in range(size)])


def far_parts(member):
    run = member.shape[0] // FAR
    return [
        swap_plane(member[index * run : (index + 1) * run], distance)
        for index, distance in ((1, 2), (2, 1), (3, 3))
    ]


def far_copies(member):
    return [swap_plane(member, distance) for distance in (2, 1, 3)]


def paired(member):
    return member.reshape(2, member.shape[0] // 2, *member.shape[1:])


def vector_back_kernel(d_projected, cond_weight, unit, d_queries, offset, gain, query, d_normed):
    step = pl.program_id(0)
    offset[...] = column_sum(wide(d_projected[...]))
    part = product_right(d_projected[...], cond_weight[...])

    @pl.when(step == 0)
    def _():
        d_normed[...] = part
        query[...] = column_sum(wide(d_queries[...]))

    @pl.when(step > 0)
    def _():
        d_normed[...] += part

    @pl.when(step == pl.num_programs(0) - 1)
    def _():
        gain[...] = column_sum(d_normed[...] * unit[...])


def vector_back(d_projected, cond_weight, unit, d_projections):
    length, columns = d_projected.shape
    width = columns // 6
    depth = unit.shape[1]
    return pl.pallas_call(
        vector_back_kernel,
        grid=(6,),
        in_specs=[
            pl.BlockSpec((length, width), lambda i: (0, i)),
            pl.BlockSpec((depth, width), lambda i: (0, i)),
            full_spec(unit),
            pl.BlockSpec((length, width), lambda i: (0, 0)),
        ],
        out_specs=[
            pl.BlockSpec((1, width), lambda i: (0, i)),
            pl.BlockSpec((1, depth), lambda i: (0, 0)),
            pl.BlockSpec((1, width), lambda i: (0, 0)),
        ],
        out_shape=[
            jax.ShapeDtypeStruct((1, columns), WIDE),
            jax.ShapeDtypeStruct((1, depth), WIDE),
            jax.ShapeDtypeStruct((1, width), WIDE),
        ],
        scratch_shapes=[pltpu.VMEM((length, depth), WIDE)],
        cost_estimate=takes(15),
        compiler_params=pltpu.CompilerParams(
            dimension_semantics=("arbitrary",), vmem_limit_bytes=32 * MEBI
        ),
        name="vector_back",
    )(d_projected, cond_weight, unit, d_projections)


TOKEN_ROWS = 256


def rows_spec(columns, at=0):
    return pl.BlockSpec((TOKEN_ROWS, columns), lambda i: (i, at))


def transition_back_kernel(d_result, gate_two, down_out, gate_up, down_weight, d_down, d_last, d_gate_up):
    half = gate_up.shape[1] // 2
    result = wide(d_result[...])
    gate = sigmoid(gate_two[...])
    given = low(result * gate)
    d_down[...] = given
    d_last[...] = low(result * down_out[...] * gate * (1.0 - gate))
    d_hidden = wide(low(product_right(given, down_weight[...])))
    gate_half = gate_up[:, :half]
    logistic = sigmoid(gate_half)
    d_gate_up[:, :half] = low(
        d_hidden * gate_up[:, half:] * logistic * (1.0 + gate_half * (1.0 - logistic))
    )
    d_gate_up[:, half:] = low(d_hidden * gate_half * logistic)


def transition_back(d_result, projected, down_out, gate_up, down_weight):
    length, width = d_result.shape
    outs = [
        jax.ShapeDtypeStruct((length, width), LOWTYPE),
        jax.ShapeDtypeStruct((length, width), LOWTYPE),
        jax.ShapeDtypeStruct(gate_up.shape, LOWTYPE),
    ]
    return pl.pallas_call(
        transition_back_kernel,
        grid=(length // TOKEN_ROWS,),
        in_specs=[
            rows_spec(width),
            rows_spec(width, 5),
            rows_spec(width),
            rows_spec(gate_up.shape[1]),
            full_spec(down_weight),
        ],
        out_specs=[rows_spec(member.shape[1]) for member in outs],
        out_shape=outs,
        cost_estimate=takes(5),
        compiler_params=pltpu.CompilerParams(
            dimension_semantics=("arbitrary",), vmem_limit_bytes=48 * MEBI
        ),
        name="transition_back",
    )(d_result, projected, down_out, gate_up, down_weight)


def middle_back_kernel(
    d_result,
    gate_one,
    scale_two,
    d_gate_up,
    unit_two,
    spread_two,
    attn_out,
    gu_weight,
    out_weight,
    d_middle,
    d_attn_out,
    d_gated,
    d_pieces,
):
    width = d_result.shape[1]
    d_normed = product_right(d_gate_up[...], gu_weight[...])
    scale = sigmoid(scale_two[...])
    unit = unit_two[...]
    d_pieces[:, width : 2 * width] = low(d_normed * unit * scale * (1.0 - scale))
    d_pieces[:, 2 * width :] = low(d_normed)
    middle = wide(d_result[...]) + normalise_back(d_normed * scale, unit, spread_two[...])
    d_middle[...] = middle
    gate = sigmoid(gate_one[...])
    given = low(middle * gate)
    d_attn_out[...] = given
    d_pieces[:, :width] = low(middle * attn_out[...] * gate * (1.0 - gate))
    d_gated[...] = low(product_right(given, out_weight[...]))


def middle_back(
    d_result, projected, d_gate_up, unit_two, spread_two, attn_out, gu_weight, out_weight
):
    length, width = d_result.shape
    outs = [
        jax.ShapeDtypeStruct((length, width), WIDE),
        jax.ShapeDtypeStruct((length, width), LOWTYPE),
        jax.ShapeDtypeStruct((length, width), LOWTYPE),
        jax.ShapeDtypeStruct((length, 3 * width), LOWTYPE),
    ]
    return pl.pallas_call(
        middle_back_kernel,
        grid=(length // TOKEN_ROWS,),
        in_specs=[
            rows_spec(width),
            rows_spec(width, 2),
            rows_spec(width, 3),
            rows_spec(d_gate_up.shape[1]),
            rows_spec(width),
            rows_spec(1),
            rows_spec(width),
            full_spec(gu_weight),
            full_spec(out_weight),
        ],
        out_specs=[rows_spec(member.shape[1]) for member in outs],
        out_shape=outs,
        cost_estimate=takes(8),
        compiler_params=pltpu.CompilerParams(
            dimension_semantics=("arbitrary",), vmem_limit_bytes=48 * MEBI
        ),
        name="middle_back",
    )(
        d_result,
        projected,
        projected,
        d_gate_up,
        unit_two,
        spread_two,
        attn_out,
        gu_weight,
        out_weight,
    )


def input_back_kernel(
    d_projections,
    scale_one,
    unit_one,
    spread_one,
    d_middle,
    d_pieces,
    d_last,
    proj_weight,
    d_projected,
    d_tokens,
):
    width = unit_one.shape[1]
    d_normed = product_right(d_projections[...], proj_weight[...])
    scale = sigmoid(scale_one[...])
    unit = unit_one[...]
    d_projected[:, :width] = low(d_normed * unit * scale * (1.0 - scale))
    d_projected[:, width : 2 * width] = low(d_normed)
    d_projected[:, 2 * width : 5 * width] = d_pieces[...]
    d_projected[:, 5 * width :] = d_last[...]
    d_tokens[...] = low(d_middle[...] + normalise_back(d_normed * scale, unit, spread_one[...]))


def input_back(
    d_projections, projected, unit_one, spread_one, d_middle, d_pieces, d_last, proj_weight
):
    length, width = unit_one.shape
    outs = [
        jax.ShapeDtypeStruct((length, 6 * width), LOWTYPE),
        jax.ShapeDtypeStruct((length, width), LOWTYPE),
    ]
    return pl.pallas_call(
        input_back_kernel,
        grid=(length // TOKEN_ROWS,),
        in_specs=[
            rows_spec(4 * width),
            rows_spec(width),
            rows_spec(width),
            rows_spec(1),
            rows_spec(width),
            rows_spec(3 * width),
            rows_spec(width),
            full_spec(proj_weight),
        ],
        out_specs=[rows_spec(member.shape[1]) for member in outs],
        out_shape=outs,
        cost_estimate=takes(15),
        compiler_params=pltpu.CompilerParams(
            dimension_semantics=("arbitrary",), vmem_limit_bytes=48 * MEBI
        ),
        name="input_back",
    )(d_projections, projected, unit_one, spread_one, d_middle, d_pieces, d_last, proj_weight)


def together(*members):
    return lax.optimization_barrier(members)


def token_units(pair_rows):
    unit, _ = normalise(wide(pair_rows).reshape(-1, pair_rows.shape[-1]))
    return low(unit)


def atom_units(pair_rows):
    values = wide(pair_rows)
    centre = values - jnp.mean(values, axis=1, keepdims=True)
    return centre * lax.rsqrt(jnp.mean(centre * centre, axis=1, keepdims=True) + EPS)


def in_turn(member):
    member = jnp.stack([member, swap_bit(member, 3)])
    return jnp.concatenate([member, swap_bit(member, 2)], axis=0)


def gather_token_bias(part):
    groups = part.shape[0] // GROUP_HEADS
    gathered = []
    for group in range(groups):
        runs = in_turn(part[group * GROUP_HEADS : (group + 1) * GROUP_HEADS])
        if group % 2:
            runs = jnp.stack([runs, swap_section(runs)])
            runs = jnp.stack([runs, swap_near(runs)])
        else:
            runs = jnp.stack([runs, swap_near(runs)])
            runs = jnp.stack([runs, swap_section(runs)], axis=1)
        gathered += [runs, swap_core(runs)]
    return gathered


def halves_sum(kept, got):
    half = kept.shape[0] // 2
    return add_low(kept[:half], got[:half]), add_low(kept[half:], got[half:])


def cross_of_all(d_token_bias, d_atom_bias, both, pair_units, heads):
    whole = jnp.stack(d_token_bias).transpose(3, 1, 0, 2, 5, 4, 6)
    whole = whole.reshape(-1, heads, whole.shape[-1])
    slab = lax.psum_scatter(whole, both, scatter_dimension=0, tiled=True).transpose(1, 0, 2)
    token_cross = product(slab.reshape(heads, -1), pair_units)
    whole = jnp.stack(d_atom_bias).transpose(2, 1, 0, 3, 4, 5)
    whole = whole.reshape(-1, *whole.shape[4:])
    return token_cross, lax.psum_scatter(whole, "dp", scatter_dimension=0, tiled=True)


def gather_atom_bias(part):
    runs = in_turn(part)
    runs = jnp.stack([runs, swap_near(runs)])
    return [runs, swap_core(runs)]


def token_block_forward(place, token_in, condition, weights, bias):
    gain, cond_weight, cond_bias, proj_weight, query_bias, out_weight, gu_weight, down_weight = (
        weights
    )
    width = token_in.shape[1]
    unit_cond, _ = normalise(condition)
    normed = low(unit_cond * wide(gain))
    projected = product(normed, cond_weight) + wide(cond_bias)
    pieces = [projected[:, i * width : (i + 1) * width] for i in range(6)]
    unit_one, spread_one = normalise(token_in)
    normed_one = low(unit_one * sigmoid(pieces[0]) + pieces[1])
    offset = jnp.concatenate([wide(query_bias), jnp.zeros((3 * width,), WIDE)])
    projections = low(product(normed_one, proj_weight) + offset)
    probability, attended, gated = token_forward(place, projections, bias)
    attn_out = product(gated, out_weight)
    middle = token_in + sigmoid(pieces[2]) * attn_out
    unit_two, spread_two = normalise(middle)
    normed_two = low(unit_two * sigmoid(pieces[3]) + pieces[4])
    gate_up = product(normed_two, gu_weight)
    half = gate_up.shape[1] // 2
    gate_half, up_half = gate_up[:, :half], gate_up[:, half:]
    hidden = low(gate_half * sigmoid(gate_half) * up_half)
    down_out = product(hidden, down_weight)
    output = middle + sigmoid(pieces[5]) * down_out
    stored = (
        unit_cond,
        normed,
        projected,
        unit_one,
        spread_one,
        normed_one,
        projections,
        probability,
        attended,
        gated,
        attn_out,
        unit_two,
        spread_two,
        normed_two,
        gate_up,
        hidden,
        down_out,
    )
    return output, stored


def local(
    atom_features,
    atom_single,
    atom_pairs,
    atom_token,
    window_start,
    pair_repr,
    single_repr,
    noise_table,
    noise_index,
    cotangent,
    *params,
):
    atom_block, atompair_gain, atompair_weight, gather_weight = (
        params[:8],
        params[8],
        params[9],
        params[10],
    )
    token_block, tokpair_gain, tokpair_weight = params[11:19], params[19], params[20]
    section, far, near, core = places()
    here = jnp.stack([section, far, near, core, piece_index()]).astype(jnp.int32)
    length = cotangent.shape[2]
    both = ("dp", "section")

    def mine(member):
        return lax.dynamic_index_in_dim(member, section, 0, keepdims=False)[0]

    rows = pair_repr.shape[0] // 2
    heads = tokpair_weight.shape[1]
    window_units = atom_units(atom_pairs)
    atom_gained = wide(atompair_gain)[:, None] * wide(atompair_weight)
    atom_part = low(
        jnp.sum(window_units[:, :, None] * atom_gained[None, :, :, None, None], axis=1)
    )
    windows, atom_heads, span, keys = atom_part.shape
    pair_units = token_units(lax.dynamic_slice_in_dim(pair_repr, section * rows, rows, 0))
    gained = low(wide(tokpair_gain)[:, None] * wide(tokpair_weight))
    token_part = low(
        lax.dot_general(
            gained, pair_units, (((0,), (1,)), ((), ())), preferred_element_type=WIDE
        )
    ).reshape(heads, rows, length)
    run = length // (8 * FAR)
    direct = lax.axis_size("dp") == 4 * FAR and rows == run
    if direct:
        place = here
        atom_bias = gather_atom_bias(atom_part)
        token_bias = gather_token_bias(token_part)
    else:
        place = jnp.zeros((5,), jnp.int32)
        whole = lax.all_gather(atom_part, "dp", axis=0, tiled=True)
        whole = whole.reshape(FAR, 2, 2, -1, atom_heads, span, keys).transpose(2, 1, 0, 3, 4, 5, 6)
        atom_bias = [whole[0], whole[1]]
        whole = lax.all_gather(token_part, both, axis=0).transpose(0, 2, 1, 3)
        whole = whole.reshape(FAR, 2, 2, 2, run, -1, GROUP_HEADS, length)
        whole = whole.transpose(5, 2, 1, 3, 0, 6, 4, 7)
        token_bias = [whole[g, c] for g in range(whole.shape[0]) for c in range(2)]

    features = mine(atom_features)
    condition = wide(single_repr) + noise_table[mine(noise_index)]
    pooled, counts, *atom_stored = atom_forward(
        window_start,
        place,
        features,
        atom_single,
        atom_token,
        atom_bias,
        atom_block,
        gather_weight,
        length,
    )
    output, token_stored = token_block_forward(
        place, wide(pooled), condition, token_block, token_bias
    )

    (
        unit_cond,
        normed,
        projected,
        unit_one,
        spread_one,
        normed_one,
        projections,
        probability,
        attended,
        gated,
        attn_out,
        unit_two,
        spread_two,
        normed_two,
        gate_up,
        hidden,
        down_out,
    ) = token_stored
    _, cond_weight, _, proj_weight, _, out_weight, gu_weight, down_weight = token_block
    width = output.shape[1]
    chunk_a = products(gu_weight.shape, down_weight.shape)
    chunk_b = products(proj_weight.shape, out_weight.shape, cond_weight.shape)
    d_result = mine(cotangent)
    output_halves = exchange_halves(low(output))
    normed_here = from_here(normed)
    d_result, output_halves, normed_here = together(d_result, output_halves, normed_here)
    d_down, d_last, d_gate_up = transition_back(
        d_result, projected, down_out, gate_up, down_weight
    )
    members_a = [normed_two, d_gate_up, hidden, d_down]
    given_a = chunk_given(here, chunk_a, members_a)
    given_a_there = swap_core(given_a)
    d_gate_up, given_a_there = together(d_gate_up, given_a_there)
    send_a, keep_a = chunk_kept(here, chunk_a, members_a, given_a_there)
    d_gate_up, send_a = together(d_gate_up, send_a)
    got_a = swap_section(send_a)
    d_middle, d_attn_out, d_gated, d_pieces = middle_back(
        d_result, projected, d_gate_up, unit_two, spread_two, attn_out, gu_weight, out_weight
    )
    *d_token_bias, d_projections = token_backward(
        place, projections, probability, attended, d_gated, run
    )
    if direct:
        got_bias = swap_core(d_token_bias[1])

    d_projections, got_a = together(d_projections, got_a)
    keep_a, send_a = exchange((0, paired(keep_a), paired(got_a)))
    d_projections, send_a = together(d_projections, send_a)
    got_a = swap_near(send_a)
    d_projected, d_tokens = input_back(
        d_projections, projected, unit_one, spread_one, d_middle, d_pieces, d_last, proj_weight
    )
    members_b = [normed_one, d_projections, gated, d_attn_out, normed_here, d_projected]
    given_b = chunk_given(here, chunk_b, members_b)
    d_projected, given_b = together(d_projected, given_b)
    given_b_there = swap_core(given_b)
    grad_offset, grad_gain, grad_query = vector_back(
        d_projected, cond_weight, unit_cond, d_projections
    )
    given_b_there, grad_query = together(given_b_there, grad_query)
    send_b, keep_b = chunk_kept(here, chunk_b, members_b, given_b_there)
    d_tokens, send_b, got_a = together(d_tokens, send_b, got_a)
    got_b = swap_section(send_b)

    entries = [(0, paired(keep_a), paired(got_a))]
    if direct:
        entries.append((0, d_token_bias[0], got_bias))
    keep_a, send_a, *bias = exchange(*entries)
    d_tokens, send_a, *bias = together(d_tokens, send_a, *bias)
    got_a = swap_plane(send_a, 1)
    if direct:
        bias, send_bias = bias
        got_bias = swap_near(send_bias)
    d_attended, d_gates, d_middles, d_atom_pieces, packed_a = atom_tokens_back(
        features, atom_single, atom_token, d_tokens, counts, atom_stored, atom_block, gather_weight
    )
    d_attended, got_a = together(d_attended, got_a)
    keep_a, send_a = exchange((0, paired(keep_a), paired(got_a)))
    d_attended, send_a = together(d_attended, send_a)
    got_a = swap_plane(send_a, 2)
    d_atom_projections, *d_atom_bias = atom_attention_back(
        window_start, place, d_attended, atom_stored
    )
    d_atom_projections, got_b, got_a = together(d_atom_projections, got_b, got_a)
    entries = [(0, paired(keep_b), paired(got_b)), (None, keep_a, got_a)]
    keep_b, send_b, total_a = exchange(*entries)
    total_a = rest_sum(total_a)
    d_middles, send_b, total_a = together(d_middles, send_b, total_a)
    got_b, got_a = swap_near(send_b), swap_plane(total_a, 2)
    if direct:
        d_middles, got_bias = together(d_middles, got_bias)
        bias, send_bias = exchange((0, bias, got_bias))
        d_middles, send_bias = together(d_middles, send_bias)
        got_bias = swap_section(send_bias)
        got_atom = swap_core(d_atom_bias[1])
    d_features, packed_b, gain, offset, query = atom_features_back(
        features, atom_single, d_atom_projections, d_gates, d_middles, d_atom_pieces, atom_block
    )
    packed = jnp.concatenate([packed_b, packed_a], axis=1)
    packed = jnp.pad(packed, ((0, 0), (0, -packed.shape[1] % (2 * COLUMNS))))
    chunk_d = products(packed.shape)
    chunk_d[0].direct = True
    given_d = chunk_given(here, chunk_d, [packed])
    got_d = swap_core(given_d)
    given_d, got_a = together(given_d, got_a)
    entries = [("join", total_a, got_a)]
    if direct:
        entries.append((0, d_atom_bias[0], got_atom))
    total_a, *atom = exchange(*entries)
    got_d, total_a, *atom = together(got_d, total_a, *atom)
    got_a = swap_plane(total_a, 1)
    if direct:
        atom, send_atom = atom
        got_atom = swap_near(send_atom)
    send_d, keep_d = chunk_kept(here, chunk_d, [packed], got_d)
    got_d = swap_section(send_d)
    feature_halves = exchange_halves(low(d_features))
    got_d, feature_halves = together(got_d, feature_halves)

    entries = [
        (0, paired(keep_b), paired(got_b)),
        (0, paired(keep_d), paired(got_d)),
        ("join", total_a, got_a),
    ]
    if direct:
        entries += [(0, paired(atom), paired(got_atom)), (0, paired(bias), paired(got_bias))]
    keep_b, send_b, keep_d, send_d, total_a, *atom = exchange(*entries)
    got_b, got_d, got_a = swap_plane(send_b, 1), swap_near(send_d), swap_near(total_a)
    if direct:
        *atom, bias, send_bias = atom
        got_atom, got_bias = swap_plane(atom[1], 1), swap_plane(send_bias, 1)

    entries = [
        (0, paired(keep_b), paired(got_b)),
        (0, paired(keep_d), paired(got_d)),
        ("join", total_a, got_a),
    ]
    if direct:
        entries += [(0, paired(atom[0]), paired(got_atom)), (0, paired(bias), paired(got_bias))]
    keep_b, send_b, keep_d, send_d, total_a, *atom = exchange(*entries)
    got_b, got_d, core_a = swap_plane(send_b, 2), swap_plane(send_d, 1), swap_core(total_a)
    if direct:
        *atom, bias, send_bias = atom
        got_atom, got_bias = swap_plane(atom[1], 2), swap_plane(send_bias, 2)

    entries = [(None, keep_b, got_b), (0, paired(keep_d), paired(got_d))]
    if direct:
        entries += [(None, atom[0], got_atom), (None, bias, got_bias)]
    total_b, keep_d, send_d, *atom = exchange(*entries)
    total_b = rest_sum(total_b)
    got_b, got_d = swap_plane(total_b, 2), swap_plane(send_d, 2)
    if direct:
        atom_slab, token_slab = atom
        token_cross = product(token_slab.reshape(heads, -1), pair_units)
    else:
        token_cross, atom_slab = cross_of_all(d_token_bias, d_atom_bias, both, pair_units, heads)
    atom_slab = atom_slab.reshape(windows, atom_heads, span, keys)
    atom_cross = jnp.sum(window_units[:, :, None] * wide(atom_slab)[:, None], axis=(0, 3, 4))
    vectors = [gain, offset, query, grad_gain, grad_offset, grad_query]
    vectors += [token_cross.reshape(1, -1), atom_cross.reshape(1, -1)]
    total = jnp.concatenate(vectors, axis=1)
    got_b, got_d, total = together(got_b, got_d, total)
    got = swap_section(total)

    total_b, total_d = exchange(("join", total_b, got_b), (None, keep_d, got_d))
    total_d = rest_sum(total_d)
    got_b, got_d = swap_plane(total_b, 1), swap_plane(total_d, 2)
    grad_gu, grad_down = assemble(here, chunk_a, total_a, core_a)
    got_b, got_d, got, grad_gu = together(got_b, got_d, got, grad_gu)
    total = total + got

    total_b, total_d = exchange(("join", total_b, got_b), ("join", total_d, got_d))
    total_b, total_d, total = together(total_b, total_d, total)
    got_b, got_d, got = swap_near(total_b), swap_plane(total_d, 1), swap_plane(total, 1)
    got_d, got = together(got_d, got)
    total = total + got
    (total_d,) = exchange(("join", total_d, got_d))
    total_d, total = together(total_d, total)
    got_d, got = swap_near(total_d), swap_plane(total, 2)
    got_d, got_b, got = together(got_d, got_b, got)
    total = total + got
    for bit in more_bits():
        total = total + swap_bit(total, bit)
    total_b, total_d = exchange(("join", total_b, got_b), ("join", total_d, got_d))
    core_b, core_d, got = swap_core(total_b), swap_core(total_d), swap_near(total)
    core_d, got = together(core_d, got)
    total = total + got
    got = swap_core(total)
    (packed,) = assemble(here, chunk_d, total_d, core_d)
    core_b, packed, got = together(core_b, packed, got)
    total = (total + got)[0]
    grad_proj, grad_out, grad_cond = assemble(here, chunk_b, total_b, core_b)

    atom_width = features.shape[1]
    sizes = [6 * atom_width, 4 * atom_width, width, atom_block[6].shape[1], atom_width]
    sizes.append(2 * atom_width)
    pieces_of = []
    first = 0
    for size in sizes:
        pieces_of.append(packed[:, first : first + size])
        first += size
    atom_cond, atom_proj, atom_gather, atom_gu, atom_out, quarters = pieces_of
    atom_down = quarters.reshape(-1, 2, atom_width).transpose(1, 0, 2).reshape(-1, atom_width)


    sums = []
    first = 0
    for member in vectors:
        sums.append(total[first : first + member.size])
        first += member.size
    gain, offset, query, token_gain, token_offset, token_query = [
        run_of(member, section, 2) for member in sums[:6]
    ]
    token_cross = run_of(sums[6].reshape(heads, -1).T, section, 2)
    atom_cross = run_of(sums[7].reshape(atom_cross.shape), section, 2)
    token_pair_gain = jnp.sum(token_cross * wide(run_of(tokpair_weight, section, 2)), axis=1)
    token_pair_weight = token_cross * wide(run_of(tokpair_gain, section, 2))[:, None]
    pair_gain = jnp.sum(atom_cross * wide(run_of(atompair_weight, section, 2)), axis=1)
    pair_weight = atom_cross * wide(run_of(atompair_gain, section, 2))[:, None]
    return (
        output_halves,
        wide(feature_halves),
        gain,
        atom_cond,
        offset,
        atom_proj,
        query,
        atom_out,
        atom_gu,
        atom_down,
        pair_gain,
        pair_weight,
        atom_gather,
        token_gain,
        grad_cond,
        token_offset,
        grad_proj,
        token_query,
        grad_out,
        grad_gu,
        grad_down,
        token_pair_gain,
        token_pair_weight,
    )


def exchange_halves(member):
    section = lax.axis_index("section")
    halves = member.reshape(2, -1, member.shape[1])
    given = lax.dynamic_index_in_dim(halves, 1 - section, 0, keepdims=False)
    kept = lax.dynamic_index_in_dim(halves, section, 0, keepdims=False)
    taken = swap_section(given)
    first = section == 0
    return jnp.stack([jnp.where(first, kept, taken), jnp.where(first, taken, kept)])[:, None]


def solution(mesh):
    weights = [P()] * 21
    halves = P(None, "dp", "section", None)
    grads = [1, 2, 1, 2, 1, 2, 2, 2, 1, 2, 2, 1, 2, 1, 2, 1, 2, 2, 2, 1, 2]
    return jax.shard_map(
        local,
        mesh=mesh,
        in_specs=(
            P(None, "dp", None, None),
            P(),
            P("dp", None, None, None),
            P(),
            P(),
            P("dp", None, None),
            P(),
            P(),
            P(None, "dp"),
            P(None, "dp", None, None),
            *weights,
        ),
        out_specs=(halves, halves)
        + tuple(P("section") if rank == 1 else P("section", None) for rank in grads),
        check_vma=False,
    )
```

```python
import functools

import jax
import jax.numpy as jnp
from jax import lax
from jax.experimental import pallas as pl
from jax.experimental.pallas import tpu as pltpu
from jax.sharding import PartitionSpec as P

EPS = 1e-05
LOWTYPE = jnp.bfloat16
WIDE = jnp.float32
ATOM_ROWS = 256
MEBI = 1024 * 1024


def takes(microseconds):
    return pl.CostEstimate(flops=0, transcendentals=0, bytes_accessed=int(microseconds * 3690000))

FAR = 4


def product(left, right):
    return jnp.dot(left, right, preferred_element_type=WIDE)


def product_left(left, right):
    return lax.dot_general(left, right, (((0,), (0,)), ((), ())), preferred_element_type=WIDE)


def product_right(left, right):
    return lax.dot_general(left, right, (((1,), (1,)), ((), ())), preferred_element_type=WIDE)


def sigmoid(values):
    return 0.5 * jnp.tanh(0.5 * values) + 0.5


def normalise(values):
    centre = values - jnp.mean(values, axis=-1, keepdims=True)
    scale = lax.rsqrt(jnp.mean(centre * centre, axis=-1, keepdims=True) + EPS)
    return centre * scale, scale


def normalise_back(grad, unit, scale):
    return scale * (
        grad
        - jnp.mean(grad, axis=-1, keepdims=True)
        - unit * jnp.mean(grad * unit, axis=-1, keepdims=True)
    )


def column_sum(values):
    return jnp.sum(values, axis=0, keepdims=True)


def low(values):
    return values.astype(LOWTYPE)


def wide(values):
    return values.astype(WIDE)


def head_masks(head_count, head_size, width, kind):
    lanes = lax.broadcasted_iota(jnp.int32, (1, width), 1)
    return [
        jnp.where((lanes >= h * head_size) & (lanes < (h + 1) * head_size), 1.0, 0.0).astype(kind)
        for h in range(head_count)
    ]


def full_spec(member):
    rank = len(member.shape)
    return pl.BlockSpec(member.shape, lambda *_: (0,) * rank)


def conditioning(single, cond_gain, cond_weight, cond_bias, first, last):
    unit, _ = normalise(wide(single[...]))
    normed = low(unit * wide(cond_gain[...]))
    return product(normed, cond_weight[:, first:last]) + wide(cond_bias[:, first:last])


def atom_project_kernel(
    features, single, cond_gain, cond_weight, cond_bias, proj_weight, query_bias, projections
):
    width = features.shape[1]
    pieces = conditioning(single, cond_gain, cond_weight, cond_bias, 0, 2 * width)
    unit, _ = normalise(wide(features[...]))
    normed_one = low(unit * sigmoid(pieces[:, :width]) + pieces[:, width:])
    raw = product(normed_one, proj_weight[...])
    projections[:, :width] = low(raw[:, :width] + wide(query_bias[...]))
    projections[:, width:] = low(raw[:, width:])


def atom_project(features, single, weights):
    atoms, width = features.shape
    gain, cond, offset, proj, query = weights[:5]
    flat = [gain[None], cond, offset[None], proj, query[None]]
    rows = 2 * ATOM_ROWS
    return pl.pallas_call(
        atom_project_kernel,
        grid=(atoms // rows,),
        in_specs=[pl.BlockSpec((rows, width), lambda i: (i, 0))] * 2
        + [full_spec(member) for member in flat],
        out_specs=pl.BlockSpec((rows, 4 * width), lambda i: (i, 0)),
        out_shape=jax.ShapeDtypeStruct((atoms, 4 * width), LOWTYPE),
        cost_estimate=takes(2),
        compiler_params=pltpu.CompilerParams(
            dimension_semantics=("arbitrary",), vmem_limit_bytes=32 * MEBI
        ),
        name="atom_project",
    )(features, single, *flat)


def atom_attend_kernel(
    last_part,
    starts,
    place,
    firsts,
    features,
    single,
    token_rows,
    projections,
    bias_own,
    bias_other,
    cond_gain,
    cond_weight,
    cond_bias,
    out_weight,
    gu_weight,
    down_weight,
    gather_weight,
    *rest,
):
    if last_part:
        pool_before, count_before, _, _, pooled, counts, attended, probability = rest[:8]
    else:
        pooled, counts, attended, probability = rest[:4]
    key_wide, value_wide, pool_sum, count_sum = rest[-4:]
    step = pl.program_id(0)
    blocks = pl.num_programs(0)
    block = step + (blocks if last_part else 0)
    width = features.shape[1]
    _, _, half_group, head_count, span, keys = bias_own.shape
    group = 2 * half_group
    head_size = width // head_count
    factor = head_size**-0.5
    half = gu_weight.shape[1] // 2

    @pl.when(step == 0)
    def _():
        key_wide[...] = wide(projections[:, width : 2 * width])
        value_wide[...] = wide(projections[:, 2 * width : 3 * width])

    rows = pl.ds(pl.multiple_of(block * ATOM_ROWS, ATOM_ROWS), ATOM_ROWS)
    masks = head_masks(head_count, head_size, width, LOWTYPE)
    wide_masks = head_masks(head_count, head_size, width, WIDE)
    query_rows = projections[rows, :width]
    value_wins, all_scores, chances, parts = [], [], [], []
    for u in range(group):
        start = starts[block * group + u]
        key_win = low(key_wide[pl.ds(start, keys), :])
        value_wins.append(low(value_wide[pl.ds(start, keys), :]))
        query_win = query_rows[u * span : (u + 1) * span]
        stacked = jnp.concatenate([query_win * mask for mask in masks], axis=0)
        all_scores.append(product_right(stacked, key_win))
    for u in range(group):
        own, other = bias_own[0, 0, u % half_group], bias_other[0, 0, u % half_group]
        bias = jnp.where(place[3] == u // half_group, own, other)
        scores = all_scores[u] * factor + wide(bias.reshape(head_count * span, keys))
        exponent = jnp.exp(scores - jnp.max(scores, axis=-1, keepdims=True))
        chance = low(exponent * (1.0 / jnp.sum(exponent, axis=-1, keepdims=True)))
        probability[u] = chance
        chances.append(chance)
    for u in range(group):
        mixed = product(chances[u], value_wins[u])
        parts.append(
            sum(mixed[h * span : (h + 1) * span] * wide_masks[h] for h in range(head_count))
        )
    mixed = jnp.concatenate(parts, axis=0)
    attended[...] = mixed
    gated = low(mixed * sigmoid(wide(projections[rows, 3 * width :])))
    pieces = conditioning(
        single, cond_gain, cond_weight, cond_bias, 2 * width, 6 * width
    )
    middle = wide(features[...]) + sigmoid(pieces[:, :width]) * product(
        gated, out_weight[...]
    )
    unit, _ = normalise(middle)
    normed_two = low(
        unit * sigmoid(pieces[:, width : 2 * width]) + pieces[:, 2 * width : 3 * width]
    )
    gate_up = product(normed_two, gu_weight[...])
    gate_half = gate_up[:, :half]
    hidden = low(gate_half * sigmoid(gate_half) * gate_up[:, half:])
    result = low(middle + sigmoid(pieces[:, 3 * width :]) * product(hidden, down_weight[...]))
    pre_act = product(result, gather_weight[...])
    pooled_atoms = low(pre_act * sigmoid(pre_act))
    reach = ATOM_ROWS + 8
    first = jnp.minimum(firsts[block] // 8 * 8, pooled.shape[0] - reach)
    token_ids = token_rows[block]
    tokens = lax.broadcasted_iota(jnp.int32, (reach, ATOM_ROWS), 0) + first
    onehot = jnp.where(tokens == token_ids, 1.0, 0.0)
    part = product(low(onehot), pooled_atoms)
    part_count = jnp.sum(onehot, axis=1, keepdims=True)

    @pl.when(step == 0)
    def _():
        pool_sum[...] = pool_before[...] if last_part else jnp.zeros_like(pool_sum)
        count_sum[...] = count_before[...] if last_part else jnp.zeros_like(count_sum)

    reached = pl.ds(pl.multiple_of(first, 8), reach)
    pool_sum[reached, :] += part
    count_sum[reached, :] += part_count

    @pl.when(step == blocks - 1)
    def _():
        counts[...] = count_sum[...]
        pooled[...] = low(pool_sum[...] / count_sum[...]) if last_part else pool_sum[...]


def far_at(run, place):
    distance = run ^ place[1]
    return distance % 2 * 2 + distance // 2


def block_of(step, place):
    return step % 2 ^ place[2], far_at(step // 2, place)


def atom_attend(
    starts, place, features, single, atom_token, projections, bias, weights, gather_weight, length, before
):
    atoms, width = features.shape
    blocks = atoms // ATOM_ROWS
    steps = blocks // 2
    _, _, half_group, head_count, span, keys = bias[0].shape
    group = 2 * half_group
    windows = group * blocks
    model_width = gather_weight.shape[1]
    token_rows = atom_token.reshape(blocks, 1, ATOM_ROWS)
    gain, cond, offset, _, _, out, gu, down = weights
    flat = [gain[None], cond, offset[None], out, gu, down, gather_weight]
    first = steps if before else 0

    def bias_block(i, starts, place, firsts):
        near, far = block_of(i + first, place)
        return near, far, 0, 0, 0, 0

    rows = pl.BlockSpec((ATOM_ROWS, width), lambda i, *_: (i + first, 0))
    outs = [
        jax.ShapeDtypeStruct((length, model_width), LOWTYPE if before else WIDE),
        jax.ShapeDtypeStruct((length, 1), WIDE),
        jax.ShapeDtypeStruct((atoms, width), WIDE),
        jax.ShapeDtypeStruct((windows, head_count * span, keys), LOWTYPE),
    ]
    members = [features, single, token_rows, projections, *bias, *flat]
    specs = [rows, rows, full_spec(token_rows), full_spec(projections)]
    specs += [pl.BlockSpec((1, 1, half_group, head_count, span, keys), bias_block)] * 2
    specs += [full_spec(member) for member in flat]
    aliases = {}
    if before:
        members += before
        specs += [full_spec(member) for member in before[:2]]
        specs += [pl.BlockSpec(memory_space=pl.ANY)] * 2
        aliases = {len(members) + 1 : 2, len(members) + 2 : 3}
    return pl.pallas_call(
        functools.partial(atom_attend_kernel, bool(before)),
        grid_spec=pltpu.PrefetchScalarGridSpec(
            num_scalar_prefetch=3,
            grid=(steps,),
            in_specs=specs,
            out_specs=[full_spec(member) for member in outs[:2]]
            + [rows, pl.BlockSpec((group, head_count * span, keys), lambda i, *_: (i + first, 0, 0))],
            scratch_shapes=[
                pltpu.VMEM((atoms, width), WIDE),
                pltpu.VMEM((atoms, width), WIDE),
                pltpu.VMEM((length, model_width), WIDE),
                pltpu.VMEM((length, 1), WIDE),
            ],
        ),
        out_shape=outs,
        input_output_aliases=aliases,
        cost_estimate=takes(2),
        compiler_params=pltpu.CompilerParams(
            dimension_semantics=("arbitrary",), vmem_limit_bytes=56 * MEBI
        ),
        name="atom_attend",
    )(starts, place, atom_token[::ATOM_ROWS], *members)


def atom_tokens_back_kernel(
    firsts,
    features,
    single,
    token_cols,
    gates,
    attended,
    d_tokens,
    counts,
    cond_gain,
    cond_weight,
    cond_bias,
    out_weight,
    gu_weight,
    down_weight,
    gather_weight,
    d_attended,
    d_gates,
    d_middles,
    d_pieces,
    packed,
    grad_out,
    grad_gu,
    grad_down,
    grad_gather,
    d_scaled,
):
    step = pl.program_id(0)
    blocks = pl.num_programs(0)
    width = features.shape[1]
    half = gu_weight.shape[1] // 2

    @pl.when(step == 0)
    def _():
        d_scaled[...] = low(wide(d_tokens[...]) * (1.0 / counts[...]))
        for member in (grad_out, grad_gu, grad_down, grad_gather):
            member[...] = jnp.zeros_like(member)

    rows = slice(None)
    unit, _ = normalise(wide(single[rows, :]))
    normed = low(unit * wide(cond_gain[...]))
    pieces = product(normed, cond_weight[:, 2 * width :]) + wide(cond_bias[:, 2 * width :])
    mixed = attended[rows, :]
    gate = sigmoid(wide(gates[rows, :]))
    gated = low(mixed * gate)
    attn_out = product(gated, out_weight[...])
    gate_one = sigmoid(pieces[:, :width])
    middle = wide(features[rows, :]) + gate_one * attn_out
    unit_two, spread_two = normalise(middle)
    scale_two = sigmoid(pieces[:, width : 2 * width])
    normed_two = low(unit_two * scale_two + pieces[:, 2 * width : 3 * width])
    gate_up = product(normed_two, gu_weight[...])
    gate_half, up_half = gate_up[:, :half], gate_up[:, half:]
    logistic = sigmoid(gate_half)
    hidden = low(gate_half * logistic * up_half)
    down_out = product(hidden, down_weight[...])
    gate_two = sigmoid(pieces[:, 3 * width :])
    result = low(middle + gate_two * down_out)
    pre_act = product(result, gather_weight[...])

    reach = ATOM_ROWS + 16
    first = jnp.minimum(firsts[step] // 16 * 16, d_tokens.shape[0] - reach)
    tokens = lax.broadcasted_iota(jnp.int32, (ATOM_ROWS, reach), 1) + first
    onehot = low(jnp.where(tokens == token_cols[...], 1.0, 0.0))
    d_rows = product(onehot, d_scaled[pl.ds(pl.multiple_of(first, 16), reach), :])
    pre_logistic = sigmoid(pre_act)
    d_pre = low(d_rows * (pre_logistic * (1.0 + pre_act * (1.0 - pre_logistic))))
    grad_gather[...] += product_left(result, d_pre)
    d_result = product_right(d_pre, gather_weight[...])

    d_down = low(d_result * gate_two)
    d_pieces[rows, 3 * width :] = low(d_result * down_out * gate_two * (1.0 - gate_two))
    grad_down[...] += product_left(hidden, d_down)
    d_hidden = wide(low(product_right(d_down, down_weight[...])))
    d_gate_half = low(d_hidden * up_half * logistic * (1.0 + gate_half * (1.0 - logistic)))
    d_up_half = low(d_hidden * gate_half * logistic)
    d_gate_up = jnp.concatenate([d_gate_half, d_up_half], axis=1)
    grad_gu[...] += product_left(normed_two, d_gate_up)
    d_normed_two = product_right(d_gate_up, gu_weight[...])
    d_pieces[rows, 2 * width : 3 * width] = low(d_normed_two)
    d_pieces[rows, width : 2 * width] = low(
        d_normed_two * unit_two * scale_two * (1.0 - scale_two)
    )
    d_middle = d_result + normalise_back(d_normed_two * scale_two, unit_two, spread_two)
    d_middles[rows, :] = d_middle
    d_attn_out = low(d_middle * gate_one)
    d_pieces[rows, :width] = low(
        d_middle * attn_out * gate_one * (1.0 - gate_one)
    )
    grad_out[...] += product_left(gated, d_attn_out)
    d_gated = wide(low(product_right(d_attn_out, out_weight[...])))
    d_attended[rows, :] = low(d_gated * gate)
    d_gates[rows, :] = low(d_gated * mixed * gate * (1.0 - gate))

    @pl.when(step == blocks - 1)
    def _():
        model_width = gather_weight.shape[1]
        packed[:, :model_width] = low(grad_gather[...])
        last = model_width + 2 * half
        packed[:, model_width:last] = low(grad_gu[...])
        packed[:, last : last + width] = low(grad_out[...])
        last = last + width
        run = grad_down.shape[0] // 4
        for part in range(4):
            rows_at = slice(part // 2 * run, (part // 2 + 1) * run)
            columns = slice(last + part % 2 * width, last + (part % 2 + 1) * width)
            packed[rows_at, columns] = low(grad_down[part * run : (part + 1) * run, :])


def atom_attention_back_kernel(
    starts,
    place,
    projections,
    attended,
    probability,
    d_attended,
    d_projections,
    d_bias_own,
    d_bias_other,
    key_wide,
    value_wide,
    d_keys,
    d_values,
):
    step = pl.program_id(0)
    blocks = pl.num_programs(0)
    width = attended.shape[1]
    group, stack, keys = probability.shape
    half_group = group // 2
    span = ATOM_ROWS // group
    head_count = stack // span
    head_size = width // head_count
    factor = head_size**-0.5

    @pl.when(step == 0)
    def _():
        for member in (d_keys, d_values):
            member[...] = jnp.zeros_like(member)
        key_wide[...] = wide(projections[:, width : 2 * width])
        value_wide[...] = wide(projections[:, 2 * width : 3 * width])

    rows = pl.ds(pl.multiple_of(step * ATOM_ROWS, ATOM_ROWS), ATOM_ROWS)
    row_grad = d_attended[...]
    row_part = wide(row_grad) * attended[...]

    masks = head_masks(head_count, head_size, width, LOWTYPE)
    wide_masks = head_masks(head_count, head_size, width, WIDE)
    query_rows = projections[rows, :width]
    held = []
    for u in range(group):
        start = starts[step * group + u]
        cut = slice(u * span, (u + 1) * span)
        key_win = low(key_wide[pl.ds(start, keys), :])
        value_win = low(value_wide[pl.ds(start, keys), :])
        stacked_query = jnp.concatenate([query_rows[cut] * mask for mask in masks], axis=0)
        stacked_grad = jnp.concatenate([row_grad[cut] * mask for mask in masks], axis=0)
        stacked_part = jnp.concatenate([row_part[cut] * mask for mask in wide_masks], axis=0)
        row_sum = jnp.sum(stacked_part, axis=-1, keepdims=True)
        d_chance = product_right(stacked_grad, value_win)
        held.append((start, key_win, stacked_query, stacked_grad, row_sum, d_chance))
    score_grads = [
        low(wide(probability[u]) * (held[u][5] - held[u][4])) for u in range(group)
    ]
    query_grads, key_grads, value_grads = [], [], []
    for u in range(group):
        _, key_win, stacked_query, stacked_grad, _, _ = held[u]
        d_stacked = product(score_grads[u], key_win) * factor
        query_grads.append(
            sum(d_stacked[h * span : (h + 1) * span] * wide_masks[h] for h in range(head_count))
        )
        key_grads.append(product_left(score_grads[u], stacked_query) * factor)
        value_grads.append(product_left(probability[u], stacked_grad))
    for u in range(group):
        window = pl.ds(held[u][0], keys)
        d_keys[window, :] += key_grads[u]
        d_values[window, :] += value_grads[u]
    d_projections[rows, :width] = low(jnp.concatenate(query_grads, axis=0))
    for u in range(half_group):
        first = place[3] == 0
        d_bias_own[0, 0, u] = jnp.where(first, score_grads[u], score_grads[u + half_group])
        d_bias_other[0, 0, u] = jnp.where(first, score_grads[u + half_group], score_grads[u])

    @pl.when(step == blocks - 1)
    def _():
        d_projections[:, width : 2 * width] = low(d_keys[...])
        d_projections[:, 2 * width : 3 * width] = low(d_values[...])


def atom_features_back_kernel(
    features,
    single,
    d_projections,
    d_gates,
    d_middles,
    d_pieces,
    cond_gain,
    cond_weight,
    cond_bias,
    proj_weight,
    d_features,
    packed,
    grad_gain,
    grad_offset,
    grad_query,
    grad_cond,
    grad_proj,
):
    step = pl.program_id(0)
    blocks = pl.num_programs(0)
    width = features.shape[1]

    @pl.when(step == 0)
    def _():
        for member in (grad_gain, grad_offset, grad_query, grad_cond, grad_proj):
            member[...] = jnp.zeros_like(member)

    unit, _ = normalise(wide(single[...]))
    normed = low(unit * wide(cond_gain[...]))
    pieces = product(normed, cond_weight[:, : 2 * width]) + wide(cond_bias[:, : 2 * width])
    unit_one, spread_one = normalise(wide(features[...]))
    scale_one = sigmoid(pieces[:, :width])
    normed_one = low(unit_one * scale_one + pieces[:, width:])
    d_projection = jnp.concatenate([d_projections[...], d_gates[...]], axis=1)
    grad_proj[...] += product_left(normed_one, d_projection)
    grad_query[...] += column_sum(wide(d_projection[:, :width]))
    d_normed_one = product_right(d_projection, proj_weight[...])
    d_features[...] = d_middles[...] + normalise_back(
        d_normed_one * scale_one, unit_one, spread_one
    )
    d_projected = jnp.concatenate(
        [
            low(d_normed_one * unit_one * scale_one * (1.0 - scale_one)),
            low(d_normed_one),
            d_pieces[...],
        ],
        axis=1,
    )
    grad_cond[...] += product_left(normed, d_projected)
    grad_offset[...] += column_sum(wide(d_projected))
    d_normed = product_right(d_projected, cond_weight[...])
    grad_gain[...] += column_sum(d_normed * unit)

    @pl.when(step == blocks - 1)
    def _():
        packed[:, : 6 * width] = low(grad_cond[...])
        packed[:, 6 * width :] = low(grad_proj[...])


def atom_tokens_back(features, single, atom_token, d_tokens, counts, stored, weights, gather_weight):
    projections, attended, _ = stored
    atoms, width = features.shape
    gain, cond, offset, _, _, out, gu, down = weights
    flat = [gain[None], cond, offset[None], out, gu, down, gather_weight]
    token_cols = atom_token.reshape(atoms, 1)
    columns = gather_weight.shape[1] + gu.shape[1] + 3 * width
    outs = [
        jax.ShapeDtypeStruct((atoms, width), LOWTYPE),
        jax.ShapeDtypeStruct((atoms, width), LOWTYPE),
        jax.ShapeDtypeStruct((atoms, width), WIDE),
        jax.ShapeDtypeStruct((atoms, 4 * width), LOWTYPE),
        jax.ShapeDtypeStruct((width, columns), LOWTYPE),
    ]

    def rows_of(member):
        return pl.BlockSpec((ATOM_ROWS, member.shape[1]), lambda i, *_: (i, 0))

    return pl.pallas_call(
        atom_tokens_back_kernel,
        grid_spec=pltpu.PrefetchScalarGridSpec(
            num_scalar_prefetch=1,
            grid=(atoms // ATOM_ROWS,),
            in_specs=[
            rows_of(features),
            rows_of(single),
            rows_of(token_cols),
            pl.BlockSpec((ATOM_ROWS, width), lambda i, *_: (i, 3)),
            rows_of(attended),
            full_spec(d_tokens),
            full_spec(counts),
        ]
        + [full_spec(member) for member in flat],
        out_specs=[rows_of(member) for member in outs[:4]] + [full_spec(outs[4])],
            scratch_shapes=[
                pltpu.VMEM(member.shape, WIDE) for member in (out, gu, down, gather_weight)
            ]
            + [pltpu.VMEM(d_tokens.shape, LOWTYPE)],
        ),
        out_shape=outs,
        cost_estimate=takes(3),
        compiler_params=pltpu.CompilerParams(
            dimension_semantics=("arbitrary",), vmem_limit_bytes=56 * MEBI
        ),
        name="atom_tokens_back",
    )(atom_token[::ATOM_ROWS], features, single, token_cols, projections, attended, d_tokens, counts, *flat)


def atom_attention_back(starts, place, d_attended, stored):
    projections, attended, probability = stored
    atoms, width = attended.shape
    blocks = atoms // ATOM_ROWS
    windows, stack, keys = probability.shape
    group = windows // blocks
    score_shape = (2, blocks // 2, group // 2, stack, keys)
    outs = [
        jax.ShapeDtypeStruct((atoms, 3 * width), LOWTYPE),
        jax.ShapeDtypeStruct(score_shape, LOWTYPE),
        jax.ShapeDtypeStruct(score_shape, LOWTYPE),
    ]

    def bias_block(i, starts, place):
        near, far = block_of(i, place)
        return near, far, 0, 0, 0

    block = pl.BlockSpec((ATOM_ROWS, width), lambda i, *_: (i, 0))
    return pl.pallas_call(
        atom_attention_back_kernel,
        grid_spec=pltpu.PrefetchScalarGridSpec(
            num_scalar_prefetch=2,
            grid=(blocks,),
            in_specs=[
                full_spec(projections),
                block,
                pl.BlockSpec((group, stack, keys), lambda i, *_: (i, 0, 0)),
                block,
            ],
            out_specs=[full_spec(outs[0])]
            + [pl.BlockSpec((1, 1, group // 2, stack, keys), bias_block)] * 2,
            scratch_shapes=[pltpu.VMEM((atoms, width), WIDE)] * 4,
        ),
        out_shape=outs,
        cost_estimate=takes(2),
        compiler_params=pltpu.CompilerParams(
            dimension_semantics=("arbitrary",), vmem_limit_bytes=56 * MEBI
        ),
        name="atom_attention_back",
    )(starts, place, projections, attended, probability, d_attended)


def atom_features_back(features, single, d_projections, d_gates, d_middles, d_pieces, weights):
    atoms, width = features.shape
    gain, cond, offset, proj = weights[:4]
    flat = [gain[None], cond, offset[None], proj]
    rows = [features, single, d_projections, d_gates, d_middles, d_pieces]
    outs = [
        jax.ShapeDtypeStruct((atoms, width), WIDE),
        jax.ShapeDtypeStruct((width, 10 * width), LOWTYPE),
        jax.ShapeDtypeStruct((1, width), WIDE),
        jax.ShapeDtypeStruct((1, 6 * width), WIDE),
        jax.ShapeDtypeStruct((1, width), WIDE),
    ]
    return pl.pallas_call(
        atom_features_back_kernel,
        grid=(atoms // ATOM_ROWS,),
        in_specs=[
            pl.BlockSpec((ATOM_ROWS, member.shape[1]), lambda i: (i, 0)) for member in rows
        ]
        + [full_spec(member) for member in flat],
        out_specs=[pl.BlockSpec((ATOM_ROWS, width), lambda i: (i, 0))]
        + [full_spec(member) for member in outs[1:]],
        out_shape=outs,
        scratch_shapes=[pltpu.VMEM(cond.shape, WIDE), pltpu.VMEM(proj.shape, WIDE)],
        cost_estimate=takes(0.5),
        compiler_params=pltpu.CompilerParams(
            dimension_semantics=("arbitrary",), vmem_limit_bytes=32 * MEBI
        ),
        name="atom_features_back",
    )(*rows, *flat)


LANES = 128
GROUP_HEADS = 8
STAGE = 1
FORWARD_PARTS = 1
BACKWARD_PARTS = 1


def head_window(head, head_size, total):
    first = min(head * head_size // LANES * LANES, total - 2 * LANES)
    return first, head * head_size - first


def head_lanes(offset, head_size, kind):
    lanes = lax.broadcasted_iota(jnp.int32, (1, 2 * LANES), 1)
    return jnp.where((lanes >= offset) & (lanes < offset + head_size), 1.0, 0.0).astype(kind)


def chosen_rows(place, own, other, head, runs, section_first):
    parts = []
    for far in runs:
        for near in range(2):
            for core in range(2):
                for section in range(2):
                    at = [near ^ place[2], section ^ place[0]]
                    at = (*(at[::-1] if section_first else at), far_at(far, place), head)
                    parts.append(jnp.where(place[3] == core, own[at], other[at]))
    return jnp.concatenate(parts, axis=0)


def token_forward_kernel(
    place, queries, keys, values, gates, own_a, other_a, own_b, other_b, probability, attended, gated
):
    heads = probability.shape[0]
    rows, total = queries.shape
    head_size = total // heads
    factor = head_size**-0.5

    run_count = FAR // FORWARD_PARTS
    runs = [pl.program_id(1) * run_count + index for index in range(run_count)]

    def score(h):
        first, offset = head_window(h, head_size, total)
        cut = slice(first, first + 2 * LANES)
        return product_right(queries[:, cut] * head_lanes(offset, head_size, LOWTYPE), keys[:, cut])

    def attend(own, other, section_first):
        tiles = [None] * (total // LANES)
        for start in range(0, heads, STAGE):
            run = range(start, start + STAGE)
            raw_scores = [score(h) for h in run]
            chances = []
            for h in run:
                scores = raw_scores[h - start] * factor + wide(
                    chosen_rows(place, own, other, h, runs, section_first)
                )
                exponent = jnp.exp(scores - jnp.max(scores, axis=-1, keepdims=True))
                chance = low(exponent * (1.0 / jnp.sum(exponent, axis=-1, keepdims=True)))
                probability[h] = chance
                chances.append(chance)
            for h in run:
                first, offset = head_window(h, head_size, total)
                mixed = product(chances[h - start], values[:, first : first + 2 * LANES])
                mixed = mixed * head_lanes(offset, head_size, WIDE)
                for t in range(2):
                    at = first // LANES + t
                    part = mixed[:, t * LANES : (t + 1) * LANES]
                    tiles[at] = part if tiles[at] is None else tiles[at] + part
        whole = jnp.concatenate(tiles, axis=1)
        attended[...] = whole
        gated[...] = low(whole * sigmoid(wide(gates[...])))

    @pl.when(pl.program_id(0) == 0)
    def _():
        attend(own_a, other_a, True)

    @pl.when(pl.program_id(0) == 1)
    def _():
        attend(own_b, other_b, False)


def token_forward(place, projections, bias):
    length, columns = projections.shape
    width = columns // 4
    rows = length // FORWARD_PARTS
    group_heads = bias[0].shape[3]
    groups = len(bias) // 2
    heads = group_heads * groups
    total = width // groups
    block = pl.BlockSpec((rows, total), lambda g, i, _: (i, g))
    return pl.pallas_call(
        token_forward_kernel,
        grid_spec=pltpu.PrefetchScalarGridSpec(
            num_scalar_prefetch=1,
            grid=(groups, FORWARD_PARTS),
            in_specs=[
                block,
                pl.BlockSpec((length, total), lambda g, i, _: (0, groups + g)),
                pl.BlockSpec((length, total), lambda g, i, _: (0, 2 * groups + g)),
                pl.BlockSpec((rows, total), lambda g, i, _: (i, 3 * groups + g)),
            ]
            + [full_spec(member) for member in bias],
            out_specs=[
                pl.BlockSpec((group_heads, rows, length), lambda g, i, _: (g, i, 0)),
                block,
                block,
            ],
        ),
        out_shape=[
            jax.ShapeDtypeStruct((heads, length, length), LOWTYPE),
            jax.ShapeDtypeStruct((length, width), WIDE),
            jax.ShapeDtypeStruct((length, width), LOWTYPE),
        ],
        cost_estimate=takes(2),
        compiler_params=pltpu.CompilerParams(
            dimension_semantics=("arbitrary", "arbitrary"), vmem_limit_bytes=56 * MEBI
        ),
        name="token_forward",
    )(place, projections, projections, projections, projections, *bias)


def token_backward_kernel(
    place,
    queries,
    keys,
    values,
    gates,
    probability,
    attended,
    d_gated,
    own,
    other,
    d_projections,
    d_keys,
    d_values,
):
    group, step = pl.program_id(0), pl.program_id(1)
    heads = probability.shape[0]
    rows, total = queries.shape
    head_size = total // heads
    factor = head_size**-0.5
    width = d_projections.shape[1] // 4
    run = own.shape[4]

    @pl.when(step == 0)
    def _():
        d_keys[...] = jnp.zeros_like(d_keys)
        d_values[...] = jnp.zeros_like(d_values)

    gate = sigmoid(wide(gates[...]))
    grad = wide(d_gated[...])
    mixed = attended[...]
    d_attended = low(grad * gate)
    d_gates = low(grad * mixed * gate * (1.0 - gate))
    row_part = wide(d_attended) * mixed

    def chance_grad(h):
        first, offset = head_window(h, head_size, total)
        cut = slice(first, first + 2 * LANES)
        mask = head_lanes(offset, head_size, LOWTYPE)
        return product_right(d_attended[:, cut] * mask, values[:, cut])

    tiles = [None] * (total // LANES)
    for begin in range(0, heads, STAGE):
        run_heads = range(begin, begin + STAGE)
        d_chances = [chance_grad(h) for h in run_heads]
        score_grads = []
        for h in run_heads:
            first, offset = head_window(h, head_size, total)
            cut = slice(first, first + 2 * LANES)
            row_sum = jnp.sum(
                row_part[:, cut] * head_lanes(offset, head_size, WIDE), axis=-1, keepdims=True
            )
            d_scores = low(wide(probability[h]) * (d_chances[h - begin] - row_sum))
            score_grads.append(d_scores)
            for index in range(FAR // BACKWARD_PARTS):
                far = far_at(step * (FAR // BACKWARD_PARTS) + index, place)
                for near in range(2):
                    for section in range(2):
                        at = (near ^ place[2], section ^ place[0], far, h)
                        pair = []
                        for core in range(2):
                            start = (8 * index + 4 * near + 2 * core + section) * run
                            pair.append(d_scores[start : start + run])
                        own[at] = jnp.where(place[3] == 0, pair[0], pair[1])
                        other[at] = jnp.where(place[3] == 0, pair[1], pair[0])
        for h in run_heads:
            first, offset = head_window(h, head_size, total)
            cut = slice(first, first + 2 * LANES)
            mask = head_lanes(offset, head_size, LOWTYPE)
            d_scores = score_grads[h - begin]
            part = product(d_scores, keys[:, cut]) * (wide(mask) * factor)
            for t in range(2):
                at = first // LANES + t
                piece = part[:, t * LANES : (t + 1) * LANES]
                tiles[at] = piece if tiles[at] is None else tiles[at] + piece
            d_keys[:, cut] += product_left(d_scores, queries[:, cut] * mask)
            d_values[:, cut] += product_left(probability[h], d_attended[:, cut] * mask)
    rows_at = pl.ds(pl.multiple_of(step * rows, rows), rows)
    first = group * total
    d_projections[rows_at, pl.ds(pl.multiple_of(first, LANES), total)] = low(
        jnp.concatenate(tiles, axis=1)
    )
    gates_at = pl.ds(pl.multiple_of(first + 3 * width, LANES), total)
    d_projections[rows_at, gates_at] = d_gates

    @pl.when(step == pl.num_programs(1) - 1)
    def _():
        first = group * total
        d_projections[:, pl.ds(pl.multiple_of(first + width, LANES), total)] = low(
            d_keys[...] * factor
        )
        d_projections[:, pl.ds(pl.multiple_of(first + 2 * width, LANES), total)] = low(
            d_values[...]
        )


def token_backward(place, projections, probability, attended, d_gated, run):
    length, columns = projections.shape
    width = columns // 4
    rows = length // BACKWARD_PARTS
    heads = probability.shape[0]
    groups = heads // GROUP_HEADS
    total = width // groups
    block = pl.BlockSpec((rows, total), lambda g, i, _: (i, g))
    grad = jax.ShapeDtypeStruct((2, 2, FAR, heads, run, length), LOWTYPE)
    grad_spec = pl.BlockSpec(
        (2, 2, FAR, GROUP_HEADS, run, length), lambda g, i, place: (0, 0, 0, g, 0, 0)
    )
    return pl.pallas_call(
        token_backward_kernel,
        grid_spec=pltpu.PrefetchScalarGridSpec(
            num_scalar_prefetch=1,
            grid=(groups, BACKWARD_PARTS),
            in_specs=[
                block,
                pl.BlockSpec((length, total), lambda g, i, _: (0, groups + g)),
                pl.BlockSpec((length, total), lambda g, i, _: (0, 2 * groups + g)),
                pl.BlockSpec((rows, total), lambda g, i, _: (i, 3 * groups + g)),
                pl.BlockSpec((GROUP_HEADS, rows, length), lambda g, i, _: (g, i, 0)),
                block,
                block,
            ],
            out_specs=[grad_spec] * 2
            + [pl.BlockSpec((length, columns), lambda g, i, _: (0, 0))],
            scratch_shapes=[pltpu.VMEM((length, total), WIDE)] * 2,
        ),
        out_shape=[grad] * 2 + [jax.ShapeDtypeStruct((length, columns), LOWTYPE)],
        cost_estimate=takes(3),
        compiler_params=pltpu.CompilerParams(
            dimension_semantics=("arbitrary", "arbitrary"), vmem_limit_bytes=56 * MEBI
        ),
        name="token_backward",
    )(place, projections, projections, projections, projections, probability, attended, d_gated)


PIECES = 8
COLUMNS = 384


def places():
    place = lax.axis_index("dp")
    return lax.axis_index("section"), place // 4, place // 2 % 2, place % 2


def swap_section(member):
    return lax.ppermute(member, "section", [(0, 1), (1, 0)])


def swap_bit(member, bit):
    return lax.ppermute(member, "dp", [(i, i ^ (1 << bit)) for i in range(lax.axis_size("dp"))])


def swap_core(member):
    return swap_bit(member, 0)


def swap_near(member):
    return swap_bit(member, 1)


def swap_far(member, bit):
    return swap_bit(member, 2 + bit)


def more_bits():
    return range(4, (lax.axis_size("dp") - 1).bit_length())


def piece_index():
    place = lax.axis_index("dp")
    return place // 2 % 2 * 4 + place // 4 % 2 * 2 + place // 8 % 2


def run_of(member, index, count):
    rows = member.shape[0] // count
    return lax.dynamic_slice_in_dim(member, index * rows, rows, 0)


def add_low(*members):
    return low(sum(wide(member) for member in members))


def scatter_plane(member):
    for bit, half in ((2, 2), (3, 1)):
        member = add_low(member[:half], swap_bit(member[half:], bit))
    for bit in more_bits():
        member = add_low(member, swap_bit(member, bit))
    return member


def rest_sum(*members):
    total = add_low(*members)
    for bit in more_bits():
        total = add_low(total, swap_bit(total, bit))
    return total


def from_here(member):
    half = member.shape[1] // 2
    first, second = member[:, :half], member[:, half:]
    turned = jnp.concatenate([second, first], axis=1)
    return jnp.where(lax.axis_index("section") == 0, member, turned)


def gather_pieces(member):
    for bit in (3, 2, 1):
        member = jnp.concatenate([member, swap_bit(member, bit)], axis=0)
    return member


class Weight:
    def __init__(self, rows, columns):
        self.rows, self.columns = rows // 2, columns
        self.blocks = columns // 2 // COLUMNS
        self.run = self.blocks * self.rows // PIECES

    def segments(self, piece):
        at, last, found = piece * self.run, (piece + 1) * self.run, []
        while at < last:
            block, row = divmod(at, self.rows)
            size = min(self.rows - row, last - at)
            found.append((block, row, size, at - piece * self.run))
            at += size
        return found


def aligned(start, size, step):
    return pl.ds(pl.multiple_of(start, step), size)


def product_blocks(place, weights, members, core, half):
    found, at = [], 0
    for weight in weights:
        if weight.direct:
            held = members[at]
            at += 1
        else:
            left, right = members[at], members[at + 1]
            at += 2
            if weight.rows % LANES:
                side = left[:, half * weight.rows : (half + 1) * weight.rows]
            else:
                side = left[:, aligned((half ^ place[0]) * weight.rows, weight.rows, LANES)]
        blocks = []
        for block in range(weight.blocks):
            columns = aligned(
                core * (weight.columns // 2) + block * COLUMNS, COLUMNS, LANES
            )
            if weight.direct:
                rows = aligned((half ^ place[0]) * weight.rows, weight.rows, 16)
                blocks.append(wide(held[rows, columns]))
            else:
                blocks.append(product_left(side, right[:, columns]))
        found.append(blocks)
    return found


def store_pieces(place, weights, found, store):
    for piece in range(PIECES):
        at = 0
        for weight, blocks in zip(weights, found):
            for block, row, size, offset in weight.segments(piece):
                store(piece ^ place[4], slice(at + offset, at + offset + size), blocks[block][row : row + size])
            at += weight.run


def given_kernel(weights, place, *refs):
    *members, out = refs
    for half in range(2):

        @pl.when(pl.program_id(0) == half)
        def _(half=half):
            def store(piece, rows, values):
                out[0, piece, rows, :] = low(values)

            store_pieces(
                place, weights, product_blocks(place, weights, members, 1 - place[3], half), store
            )


def kept_kernel(weights, place, *refs):
    *members, received, given, kept = refs
    for step, (half, target) in enumerate(((1, given), (0, kept))):

        @pl.when(pl.program_id(0) == step)
        def _(half=half, target=target):
            def store(piece, rows, values):
                target[piece, rows, :] = low(values + wide(received[0, piece, rows, :]))

            store_pieces(
                place, weights, product_blocks(place, weights, members, place[3], half), store
            )


def chunk_rows(weights):
    return sum(weight.run for weight in weights)


def chunk_given(place, weights, members):
    block = (1, PIECES, chunk_rows(weights), COLUMNS)
    return pl.pallas_call(
        functools.partial(given_kernel, weights),
        grid_spec=pltpu.PrefetchScalarGridSpec(
            num_scalar_prefetch=1,
            grid=(2,),
            in_specs=[full_spec(member) for member in members],
            out_specs=pl.BlockSpec(block, lambda i, _: (i, 0, 0, 0)),
        ),
        out_shape=jax.ShapeDtypeStruct((2, *block[1:]), LOWTYPE),
        cost_estimate=takes(0.5 if weights[0].direct else 3),
        compiler_params=pltpu.CompilerParams(
            dimension_semantics=("arbitrary",), vmem_limit_bytes=48 * MEBI
        ),
        name="chunk_given",
    )(place, *members)


def chunk_kept(place, weights, members, received):
    block = (1, PIECES, chunk_rows(weights), COLUMNS)
    out = jax.ShapeDtypeStruct(block[1:], LOWTYPE)
    return pl.pallas_call(
        functools.partial(kept_kernel, weights),
        grid_spec=pltpu.PrefetchScalarGridSpec(
            num_scalar_prefetch=1,
            grid=(2,),
            in_specs=[full_spec(member) for member in members]
            + [pl.BlockSpec(block, lambda i, _: (1 - i, 0, 0, 0))],
            out_specs=[full_spec(out), full_spec(out)],
        ),
        out_shape=[out, out],
        cost_estimate=takes(0.5 if weights[0].direct else 6),
        compiler_params=pltpu.CompilerParams(
            dimension_semantics=("arbitrary",), vmem_limit_bytes=48 * MEBI
        ),
        name="chunk_kept",
    )(place, *members, received)


def assemble_kernel(weights, place, own, other, *outs):
    for source, core in ((own, place[3]), (other, 1 - place[3])):
        for piece in range(PIECES):
            at = 0
            for weight, out in zip(weights, outs):
                for block, row, size, offset in weight.segments(piece):
                    columns = aligned(
                        core * (weight.columns // 2) + block * COLUMNS, COLUMNS, LANES
                    )
                    rows = slice(at + offset, at + offset + size)
                    out[row : row + size, columns] = wide(source[piece ^ place[4], rows, :])
                at += weight.run


def assemble(place, weights, own, other):
    outs = [jax.ShapeDtypeStruct((weight.rows, weight.columns), WIDE) for weight in weights]
    return pl.pallas_call(
        functools.partial(assemble_kernel, weights),
        grid_spec=pltpu.PrefetchScalarGridSpec(
            num_scalar_prefetch=1,
            grid=(1,),
            in_specs=[full_spec(own), full_spec(other)],
            out_specs=[full_spec(member) for member in outs],
        ),
        out_shape=outs,
        cost_estimate=takes(2),
        compiler_params=pltpu.CompilerParams(
            dimension_semantics=("arbitrary",), vmem_limit_bytes=48 * MEBI
        ),
        name="assemble",
    )(place, own, other)


def products(*shapes):
    weights = [Weight(*shape) for shape in shapes]
    for weight in weights:
        weight.direct = False
    return weights


def vector_sum(member):
    section = lax.axis_index("section")
    kept = lax.dynamic_index_in_dim(member, section, 0, keepdims=False)
    total = kept + swap_section(lax.dynamic_index_in_dim(member, 1 - section, 0, keepdims=False))
    for bit in range((lax.axis_size("dp") - 1).bit_length()):
        total = total + swap_bit(total, bit)
    return total


def half_block(shape, count=2):
    axis = len(shape) - 2
    if shape[axis] % (16 * count):
        axis -= 1
    block = list(shape)
    block[axis] //= count
    return pl.BlockSpec(tuple(block), lambda i: tuple(i if a == axis else 0 for a in range(len(shape))))


def exchange_kernel(entries, *refs):
    refs = list(refs)
    members = [[refs.pop(0) for _ in range(1 + count)] for _, count in entries]
    for (axis, _), (kept, *got) in zip(entries, members):
        if axis == "join":
            out = refs.pop(0)
            rows = kept.shape[0]
            for index, member in enumerate([kept, *got]):
                out[index * rows : (index + 1) * rows] = member[...]
        elif axis == "group":
            rows = kept.shape[0]
            for side in range(2):
                out = refs.pop(0)
                out[:rows] = kept[:, side]
                out[rows:] = got[0][:, side]
        elif axis == "far":
            rows = got[0].shape[0]
            refs.pop(0)[...] = low(
                wide(kept[:rows]) + wide(got[0][...]) + wide(got[1][...]) + wide(got[2][...])
            )
        elif axis is None:
            refs.pop(0)[...] = low(wide(kept[...]) + wide(got[0][...]))
        else:
            for side in range(2):
                at = (slice(None),) * axis + (side,)
                refs.pop(0)[...] = low(wide(kept[at]) + wide(got[0][at]))


def exchange(*entries):
    shapes, inputs, kinds = [], [], []
    for axis, kept, got in entries:
        got = list(got) if isinstance(got, (list, tuple)) else [got]
        inputs += [kept, *got]
        kinds.append((axis, len(got)))
        if axis == "join":
            shapes.append(((1 + len(got)) * kept.shape[0], *kept.shape[1:]))
        elif axis == "group":
            shapes += [(2 * kept.shape[0], *kept.shape[2:])] * 2
        elif axis == "far":
            shapes.append(got[0].shape)
        elif axis is None:
            shapes.append(kept.shape)
        else:
            shapes += [kept.shape[:axis] + kept.shape[axis + 1 :]] * 2
    return pl.pallas_call(
        functools.partial(exchange_kernel, kinds),
        grid=(2,),
        in_specs=[half_block(member.shape) for member in inputs],
        out_specs=[half_block(shape) for shape in shapes],
        out_shape=[jax.ShapeDtypeStruct(shape, LOWTYPE) for shape in shapes],
        cost_estimate=takes(0.5),
        compiler_params=pltpu.CompilerParams(
            dimension_semantics=("arbitrary",), vmem_limit_bytes=48 * MEBI
        ),
        name="exchange",
    )(*inputs)


def swap_plane(member, distance):
    size = lax.axis_size("dp")
    return lax.ppermute(member, "dp", [(i, i ^ (distance << 2)) for i in range(size)])


def paired(member):
    return member.reshape(2, member.shape[0] // 2, *member.shape[1:])


def vector_back_kernel(d_projected, cond_weight, unit, d_queries, offset, gain, query, d_normed):
    step = pl.program_id(0)
    offset[...] = column_sum(wide(d_projected[...]))
    part = product_right(d_projected[...], cond_weight[...])

    @pl.when(step == 0)
    def _():
        d_normed[...] = part
        query[...] = column_sum(wide(d_queries[...]))

    @pl.when(step > 0)
    def _():
        d_normed[...] += part

    @pl.when(step == pl.num_programs(0) - 1)
    def _():
        gain[...] = column_sum(d_normed[...] * unit[...])


def vector_back(d_projected, cond_weight, unit, d_projections):
    length, columns = d_projected.shape
    width = columns // 6
    depth = unit.shape[1]
    return pl.pallas_call(
        vector_back_kernel,
        grid=(6,),
        in_specs=[
            pl.BlockSpec((length, width), lambda i: (0, i)),
            pl.BlockSpec((depth, width), lambda i: (0, i)),
            full_spec(unit),
            pl.BlockSpec((length, width), lambda i: (0, 0)),
        ],
        out_specs=[
            pl.BlockSpec((1, width), lambda i: (0, i)),
            pl.BlockSpec((1, depth), lambda i: (0, 0)),
            pl.BlockSpec((1, width), lambda i: (0, 0)),
        ],
        out_shape=[
            jax.ShapeDtypeStruct((1, columns), WIDE),
            jax.ShapeDtypeStruct((1, depth), WIDE),
            jax.ShapeDtypeStruct((1, width), WIDE),
        ],
        scratch_shapes=[pltpu.VMEM((length, depth), WIDE)],
        cost_estimate=takes(3),
        compiler_params=pltpu.CompilerParams(
            dimension_semantics=("arbitrary",), vmem_limit_bytes=32 * MEBI
        ),
        name="vector_back",
    )(d_projected, cond_weight, unit, d_projections)


def far_paired(member):
    return member.reshape(member.shape[0], 2, 2, *member.shape[2:])


def by_group(member):
    return member.reshape(member.shape[0], -1, GROUP_HEADS, *member.shape[2:])


TOKEN_ROWS = 256


def rows_spec(columns, at=0):
    return pl.BlockSpec((TOKEN_ROWS, columns), lambda i: (i, at))


def transition_back_kernel(d_result, gate_two, down_out, gate_up, down_weight, d_down, d_last, d_gate_up):
    half = gate_up.shape[1] // 2
    result = wide(d_result[...])
    gate = sigmoid(gate_two[...])
    given = low(result * gate)
    d_down[...] = given
    d_last[...] = low(result * down_out[...] * gate * (1.0 - gate))
    d_hidden = wide(low(product_right(given, down_weight[...])))
    gate_half = gate_up[:, :half]
    logistic = sigmoid(gate_half)
    d_gate_up[:, :half] = low(
        d_hidden * gate_up[:, half:] * logistic * (1.0 + gate_half * (1.0 - logistic))
    )
    d_gate_up[:, half:] = low(d_hidden * gate_half * logistic)


def transition_back(d_result, projected, down_out, gate_up, down_weight):
    length, width = d_result.shape
    outs = [
        jax.ShapeDtypeStruct((length, width), LOWTYPE),
        jax.ShapeDtypeStruct((length, width), LOWTYPE),
        jax.ShapeDtypeStruct(gate_up.shape, LOWTYPE),
    ]
    return pl.pallas_call(
        transition_back_kernel,
        grid=(length // TOKEN_ROWS,),
        in_specs=[
            rows_spec(width),
            rows_spec(width, 5),
            rows_spec(width),
            rows_spec(gate_up.shape[1]),
            full_spec(down_weight),
        ],
        out_specs=[rows_spec(member.shape[1]) for member in outs],
        out_shape=outs,
        cost_estimate=takes(5),
        compiler_params=pltpu.CompilerParams(
            dimension_semantics=("arbitrary",), vmem_limit_bytes=48 * MEBI
        ),
        name="transition_back",
    )(d_result, projected, down_out, gate_up, down_weight)


def middle_back_kernel(
    d_result,
    gate_one,
    scale_two,
    d_gate_up,
    unit_two,
    spread_two,
    attn_out,
    gu_weight,
    out_weight,
    d_middle,
    d_attn_out,
    d_gated,
    d_pieces,
):
    width = d_result.shape[1]
    d_normed = product_right(d_gate_up[...], gu_weight[...])
    scale = sigmoid(scale_two[...])
    unit = unit_two[...]
    d_pieces[:, width : 2 * width] = low(d_normed * unit * scale * (1.0 - scale))
    d_pieces[:, 2 * width :] = low(d_normed)
    middle = wide(d_result[...]) + normalise_back(d_normed * scale, unit, spread_two[...])
    d_middle[...] = middle
    gate = sigmoid(gate_one[...])
    given = low(middle * gate)
    d_attn_out[...] = given
    d_pieces[:, :width] = low(middle * attn_out[...] * gate * (1.0 - gate))
    d_gated[...] = low(product_right(given, out_weight[...]))


def middle_back(
    d_result, projected, d_gate_up, unit_two, spread_two, attn_out, gu_weight, out_weight
):
    length, width = d_result.shape
    outs = [
        jax.ShapeDtypeStruct((length, width), WIDE),
        jax.ShapeDtypeStruct((length, width), LOWTYPE),
        jax.ShapeDtypeStruct((length, width), LOWTYPE),
        jax.ShapeDtypeStruct((length, 3 * width), LOWTYPE),
    ]
    return pl.pallas_call(
        middle_back_kernel,
        grid=(length // TOKEN_ROWS,),
        in_specs=[
            rows_spec(width),
            rows_spec(width, 2),
            rows_spec(width, 3),
            rows_spec(d_gate_up.shape[1]),
            rows_spec(width),
            rows_spec(1),
            rows_spec(width),
            full_spec(gu_weight),
            full_spec(out_weight),
        ],
        out_specs=[rows_spec(member.shape[1]) for member in outs],
        out_shape=outs,
        cost_estimate=takes(3),
        compiler_params=pltpu.CompilerParams(
            dimension_semantics=("arbitrary",), vmem_limit_bytes=48 * MEBI
        ),
        name="middle_back",
    )(
        d_result,
        projected,
        projected,
        d_gate_up,
        unit_two,
        spread_two,
        attn_out,
        gu_weight,
        out_weight,
    )


def input_back_kernel(
    d_projections,
    scale_one,
    unit_one,
    spread_one,
    d_middle,
    d_pieces,
    d_last,
    proj_weight,
    d_projected,
    d_tokens,
):
    width = unit_one.shape[1]
    d_normed = product_right(d_projections[...], proj_weight[...])
    scale = sigmoid(scale_one[...])
    unit = unit_one[...]
    d_projected[:, :width] = low(d_normed * unit * scale * (1.0 - scale))
    d_projected[:, width : 2 * width] = low(d_normed)
    d_projected[:, 2 * width : 5 * width] = d_pieces[...]
    d_projected[:, 5 * width :] = d_last[...]
    d_tokens[...] = low(d_middle[...] + normalise_back(d_normed * scale, unit, spread_one[...]))


def input_back(
    d_projections, projected, unit_one, spread_one, d_middle, d_pieces, d_last, proj_weight
):
    length, width = unit_one.shape
    outs = [
        jax.ShapeDtypeStruct((length, 6 * width), LOWTYPE),
        jax.ShapeDtypeStruct((length, width), LOWTYPE),
    ]
    return pl.pallas_call(
        input_back_kernel,
        grid=(length // TOKEN_ROWS,),
        in_specs=[
            rows_spec(4 * width),
            rows_spec(width),
            rows_spec(width),
            rows_spec(1),
            rows_spec(width),
            rows_spec(3 * width),
            rows_spec(width),
            full_spec(proj_weight),
        ],
        out_specs=[rows_spec(member.shape[1]) for member in outs],
        out_shape=outs,
        cost_estimate=takes(2),
        compiler_params=pltpu.CompilerParams(
            dimension_semantics=("arbitrary",), vmem_limit_bytes=48 * MEBI
        ),
        name="input_back",
    )(d_projections, projected, unit_one, spread_one, d_middle, d_pieces, d_last, proj_weight)


def together(*members):
    return lax.optimization_barrier(members)


def token_units(pair_rows):
    unit, _ = normalise(wide(pair_rows).reshape(-1, pair_rows.shape[-1]))
    return low(unit)


def atom_units(pair_rows):
    values = wide(pair_rows)
    centre = values - jnp.mean(values, axis=1, keepdims=True)
    return centre * lax.rsqrt(jnp.mean(centre * centre, axis=1, keepdims=True) + EPS)


def in_turn(member):
    member = jnp.stack([member, swap_bit(member, 3)])
    return jnp.concatenate([member, swap_bit(member, 2)], axis=0)


def halves_sum(kept, got):
    half = kept.shape[0] // 2
    return add_low(kept[:half], got[:half]), add_low(kept[half:], got[half:])


def cross_of_all(d_token_bias, d_atom_bias, both, pair_units, heads):
    whole = jnp.stack(d_token_bias).transpose(3, 1, 0, 2, 5, 4, 6)
    whole = whole.reshape(-1, heads, whole.shape[-1])
    slab = lax.psum_scatter(whole, both, scatter_dimension=0, tiled=True).transpose(1, 0, 2)
    token_cross = product(slab.reshape(heads, -1), pair_units)
    whole = jnp.stack(d_atom_bias).transpose(2, 1, 0, 3, 4, 5)
    whole = whole.reshape(-1, *whole.shape[4:])
    return token_cross, lax.psum_scatter(whole, "dp", scatter_dimension=0, tiled=True)


def token_conditioning(condition, weights):
    gain, cond_weight, cond_bias = weights[:3]
    unit_cond, _ = normalise(condition)
    normed = low(unit_cond * wide(gain))
    return unit_cond, normed, product(normed, cond_weight) + wide(cond_bias)


def token_block_forward(place, token_in, conditioned, weights, bias):
    proj_weight, query_bias, out_weight, gu_weight, down_weight = weights[3:]
    unit_cond, normed, projected = conditioned
    width = token_in.shape[1]
    pieces = [projected[:, i * width : (i + 1) * width] for i in range(6)]
    unit_one, spread_one = normalise(token_in)
    normed_one = low(unit_one * sigmoid(pieces[0]) + pieces[1])
    offset = jnp.concatenate([wide(query_bias), jnp.zeros((3 * width,), WIDE)])
    projections = low(product(normed_one, proj_weight) + offset)
    probability, attended, gated = token_forward(place, projections, bias)
    attn_out = product(gated, out_weight)
    middle = token_in + sigmoid(pieces[2]) * attn_out
    unit_two, spread_two = normalise(middle)
    normed_two = low(unit_two * sigmoid(pieces[3]) + pieces[4])
    gate_up = product(normed_two, gu_weight)
    half = gate_up.shape[1] // 2
    gate_half, up_half = gate_up[:, :half], gate_up[:, half:]
    hidden = low(gate_half * sigmoid(gate_half) * up_half)
    down_out = product(hidden, down_weight)
    output = middle + sigmoid(pieces[5]) * down_out
    stored = (
        unit_cond,
        normed,
        projected,
        unit_one,
        spread_one,
        normed_one,
        projections,
        probability,
        attended,
        gated,
        attn_out,
        unit_two,
        spread_two,
        normed_two,
        gate_up,
        hidden,
        down_out,
    )
    return output, stored


def local(
    atom_features,
    atom_single,
    atom_pairs,
    atom_token,
    window_start,
    pair_repr,
    single_repr,
    noise_table,
    noise_index,
    cotangent,
    *params,
):
    atom_block, atompair_gain, atompair_weight, gather_weight = (
        params[:8],
        params[8],
        params[9],
        params[10],
    )
    token_block, tokpair_gain, tokpair_weight = params[11:19], params[19], params[20]
    section, far, near, core = places()
    here = jnp.stack([section, far, near, core, piece_index()]).astype(jnp.int32)
    length = cotangent.shape[2]
    both = ("dp", "section")

    def mine(member):
        return lax.dynamic_index_in_dim(member, section, 0, keepdims=False)[0]

    rows = pair_repr.shape[0] // 2
    heads = tokpair_weight.shape[1]
    features = mine(atom_features)
    window_units = atom_units(atom_pairs)
    atom_gained = wide(atompair_gain)[:, None] * wide(atompair_weight)
    atom_part = low(
        jnp.sum(window_units[:, :, None] * atom_gained[None, :, :, None, None], axis=1)
    )
    windows, atom_heads, span, keys = atom_part.shape
    pair_rows = lax.dynamic_slice_in_dim(pair_repr, section * rows, rows, 0)
    atom_part, pair_rows = together(atom_part, pair_rows)
    pair_units = token_units(pair_rows)
    gained = low(wide(tokpair_gain)[:, None] * wide(tokpair_weight))
    token_part = low(
        lax.dot_general(
            gained, pair_units, (((0,), (1,)), ((), ())), preferred_element_type=WIDE
        )
    ).reshape(heads, rows, length)
    condition = wide(single_repr) + noise_table[mine(noise_index)]
    unit_cond, normed, projected = token_conditioning(condition, token_block)
    run = length // (8 * FAR)
    direct = lax.axis_size("dp") == 4 * FAR and rows == run
    if direct:
        place = jnp.stack([section, far, near, core]).astype(jnp.int32)
        got_atom = swap_plane(atom_part, 2)
        token_part, got_atom = together(token_part, got_atom)
        got_token = swap_plane(token_part, 2)
        runs = jnp.stack([atom_part, got_atom])
        runs = jnp.concatenate([runs, swap_plane(runs, 1)])
        runs, got_token = together(runs, got_token)
        got_atom = swap_near(runs)
        token_runs = jnp.stack([token_part, got_token])
        got_token = swap_plane(token_runs, 1)
        projections = atom_project(features, atom_single, atom_block)
        got_atom, got_token, projections, projected = together(
            got_atom, got_token, projections, projected
        )
        runs = jnp.stack([runs, got_atom])
        atom_bias = [runs, swap_core(runs)]
        runs_a, runs_b = exchange(("group", by_group(token_runs), by_group(got_token)))
        runs_a, runs_b, atom_bias[1] = together(runs_a, runs_b, atom_bias[1])
        got_a, got_b = swap_near(runs_a), swap_section(runs_b)
    else:
        place = jnp.zeros((4,), jnp.int32)
        projections = atom_project(features, atom_single, atom_block)
        whole = lax.all_gather(atom_part, "dp", axis=0, tiled=True)
        whole = whole.reshape(FAR, 2, 2, -1, atom_heads, span, keys).transpose(2, 1, 0, 3, 4, 5, 6)
        atom_bias = [whole[0], whole[1]]
        whole = lax.all_gather(token_part, both, axis=0).transpose(0, 2, 1, 3)
        whole = whole.reshape(FAR, 2, 2, 2, run, -1, GROUP_HEADS, length)
        whole = whole.transpose(5, 2, 1, 3, 0, 6, 4, 7)
        token_bias = [whole[0, 0].swapaxes(0, 1), whole[0, 1].swapaxes(0, 1), whole[1, 0], whole[1, 1]]

    atom_args = (window_start, place, features, atom_single, atom_token, projections, atom_bias)
    atom_args += (atom_block, gather_weight, length)
    before = list(atom_attend(*atom_args, None))
    if direct:
        before[0], got_a, got_b = together(before[0], got_a, got_b)
        runs_a, runs_b = exchange(("join", runs_a, got_a), ("join", runs_b, got_b))
        before[0], runs_a, runs_b = together(before[0], runs_a, runs_b)
        got_a, got_b = swap_section(runs_a), swap_near(runs_b)
    pooled, counts, attended, probability = atom_attend(*atom_args, before)
    atom_stored = [projections, attended, probability]
    if direct:
        pooled, got_a, got_b = together(pooled, got_a, got_b)
        runs_a, runs_b = exchange(("join", runs_a, got_a), ("join", runs_b, got_b))
        runs_a = runs_a.reshape(2, 2, FAR, *runs_a.shape[1:])
        runs_b = runs_b.reshape(2, 2, FAR, *runs_b.shape[1:])
        token_bias = [runs_a, swap_core(runs_a), runs_b, swap_core(runs_b)]
    output, token_stored = token_block_forward(
        place, wide(pooled), (unit_cond, normed, projected), token_block, token_bias
    )

    (
        unit_cond,
        normed,
        projected,
        unit_one,
        spread_one,
        normed_one,
        projections,
        probability,
        attended,
        gated,
        attn_out,
        unit_two,
        spread_two,
        normed_two,
        gate_up,
        hidden,
        down_out,
    ) = token_stored
    _, cond_weight, _, proj_weight, _, out_weight, gu_weight, down_weight = token_block
    width = output.shape[1]
    chunk_a = products(gu_weight.shape, down_weight.shape)
    chunk_b = products(proj_weight.shape, out_weight.shape, cond_weight.shape)
    d_result = mine(cotangent)
    normed_here = from_here(normed)
    d_result, normed_here, output_low = together(d_result, normed_here, low(output))
    d_down, d_last, d_gate_up = transition_back(
        d_result, projected, down_out, gate_up, down_weight
    )
    members_a = [normed_two, d_gate_up, hidden, d_down]
    given_a = chunk_given(here, chunk_a, members_a)
    given_a_there = swap_core(given_a)
    d_gate_up, given_a_there = together(d_gate_up, given_a_there)
    send_a, keep_a = chunk_kept(here, chunk_a, members_a, given_a_there)
    d_gate_up, send_a = together(d_gate_up, send_a)
    got_a = swap_section(send_a)
    d_middle, d_attn_out, d_gated, d_pieces = middle_back(
        d_result, projected, d_gate_up, unit_two, spread_two, attn_out, gu_weight, out_weight
    )
    *d_token_bias, d_projections = token_backward(
        place, projections, probability, attended, d_gated, run
    )

    d_projected, d_tokens = input_back(
        d_projections, projected, unit_one, spread_one, d_middle, d_pieces, d_last, proj_weight
    )
    d_projected, got_a = together(d_projected, got_a)
    keep_a, send_a = exchange((0, paired(keep_a), paired(got_a)))
    d_projected, send_a, d_token_bias[1] = together(d_projected, send_a, d_token_bias[1])
    got_a = swap_near(send_a)
    if direct:
        got_bias = swap_core(d_token_bias[1])
    members_b = [normed_one, d_projections, gated, d_attn_out, normed_here, d_projected]
    given_b = chunk_given(here, chunk_b, members_b)
    d_projected, given_b = together(d_projected, given_b)
    given_b_there = swap_core(given_b)
    grad_offset, grad_gain, grad_query = vector_back(
        d_projected, cond_weight, unit_cond, d_projections
    )
    if direct:
        grad_query, got_bias = together(grad_query, got_bias)
        bias, send_bias = exchange((0, d_token_bias[0], got_bias))
        grad_query, send_bias = together(grad_query, send_bias)
        got_bias = swap_near(send_bias)
    given_b_there, grad_query = together(given_b_there, grad_query)
    send_b, keep_b = chunk_kept(here, chunk_b, members_b, given_b_there)
    d_tokens, send_b, got_a = together(d_tokens, send_b, got_a)
    got_b = swap_section(send_b)
    keep_a, send_a = exchange((0, paired(keep_a), paired(got_a)))
    d_tokens, send_a = together(d_tokens, send_a)
    got_a = swap_plane(send_a, 1)
    d_attended, d_gates, d_middles, d_atom_pieces, packed_a = atom_tokens_back(
        features, atom_single, atom_token, d_tokens, counts, atom_stored, atom_block, gather_weight
    )
    d_attended, got_a = together(d_attended, got_a)
    keep_a, send_a = exchange((0, paired(keep_a), paired(got_a)))
    d_attended, send_a = together(d_attended, send_a)
    got_a = swap_plane(send_a, 2)
    d_atom_projections, *d_atom_bias = atom_attention_back(
        window_start, place, d_attended, atom_stored
    )
    d_atom_projections, got_b, got_a = together(d_atom_projections, got_b, got_a)
    entries = [(0, paired(keep_b), paired(got_b)), (None, keep_a, got_a)]
    if direct:
        entries.append((0, bias, got_bias))
    keep_b, send_b, total_a, *bias = exchange(*entries)
    total_a = rest_sum(total_a)
    d_middles, send_b, total_a, d_atom_bias[1], *bias = together(
        d_middles, send_b, total_a, d_atom_bias[1], *bias
    )
    got_b, got_a = swap_near(send_b), swap_plane(total_a, 2)
    if direct:
        bias, send_bias = bias
        got_bias = swap_section(send_bias)
        got_atom = swap_core(d_atom_bias[1])
    d_features, packed_b, gain, offset, query = atom_features_back(
        features, atom_single, d_atom_projections, d_gates, d_middles, d_atom_pieces, atom_block
    )
    packed = jnp.concatenate([packed_b, packed_a], axis=1)
    packed = jnp.pad(packed, ((0, 0), (0, -packed.shape[1] % (2 * COLUMNS))))
    chunk_d = products(packed.shape)
    chunk_d[0].direct = True
    given_d = chunk_given(here, chunk_d, [packed])
    given_d, got_a = together(given_d, got_a)
    entries = [("join", total_a, got_a)]
    if direct:
        entries.append((0, d_atom_bias[0], got_atom))
    total_a, *atom = exchange(*entries)
    given_d, total_a, *atom = together(given_d, total_a, *atom)
    got_d = swap_core(given_d)
    got_a = swap_plane(total_a, 1)
    if direct:
        atom, send_atom = atom
    send_d, keep_d = chunk_kept(here, chunk_d, [packed], got_d)
    got_d = swap_section(send_d)

    entries = [
        (0, paired(keep_b), paired(got_b)),
        (0, paired(keep_d), paired(got_d)),
        ("join", total_a, got_a),
    ]
    if direct:
        entries.append((0, paired(bias), paired(got_bias)))
    keep_b, send_b, keep_d, send_d, total_a, *bias = exchange(*entries)
    got_b, got_d, got_a = swap_plane(send_b, 1), swap_near(send_d), swap_near(total_a)
    if direct:
        bias, send_bias = bias
        got_bias = swap_plane(send_bias, 1)

    entries = [(0, paired(keep_b), paired(got_b)), (0, paired(keep_d), paired(got_d))]
    if direct:
        entries.append((0, paired(bias), paired(got_bias)))
    keep_b, send_b, keep_d, send_d, *bias = exchange(*entries)
    got_b, got_d = swap_plane(send_b, 2), swap_plane(send_d, 1)
    if direct:
        bias, send_bias = bias
        got_bias = swap_plane(send_bias, 2)
        send_d, send_atom = together(send_d, send_atom)
        got_atom = swap_near(send_atom)

    entries = [(None, keep_b, got_b), (0, paired(keep_d), paired(got_d))]
    if direct:
        entries.append((None, bias, got_bias))
    total_b, keep_d, send_d, *token_slab = exchange(*entries)
    total_b = rest_sum(total_b)
    total_b, send_d, output_low, features_low = together(
        total_b, send_d, output_low, low(d_features)
    )
    got_b, got_d = swap_plane(total_b, 2), swap_plane(send_d, 2)
    feature_halves = exchange_halves(features_low)
    output_halves = exchange_halves(output_low)
    if direct:
        token_cross = product(token_slab[0].reshape(heads, -1), pair_units)
        got_b, token_cross = together(got_b, token_cross)

    entries = [("join", total_b, got_b), (None, keep_d, got_d), ("join", total_a, got_a)]
    if direct:
        entries.append((0, paired(atom), paired(got_atom)))
    total_b, total_d, total_a, *atom = exchange(*entries)
    total_d = rest_sum(total_d)
    got_b, got_d = swap_plane(total_b, 1), swap_plane(total_d, 2)
    if direct:
        got_atom = swap_plane(atom[1], 1)

    entries = [("join", total_b, got_b), ("join", total_d, got_d)]
    if direct:
        entries.append((0, paired(atom[0]), paired(got_atom)))
    total_b, total_d, *atom = exchange(*entries)
    total_b, total_d, total_a = together(total_b, total_d, total_a)
    got_b, got_d, core_a = swap_near(total_b), swap_plane(total_d, 1), swap_core(total_a)
    entries = [("join", total_d, got_d)]
    if direct:
        entries.append((None, atom[0], swap_plane(atom[1], 2)))
    total_d, *atom = exchange(*entries)
    total_d, core_a, *atom = together(total_d, core_a, *atom)
    got_d = swap_near(total_d)
    if direct:
        (atom_slab,) = atom
    else:
        token_cross, atom_slab = cross_of_all(d_token_bias, d_atom_bias, both, pair_units, heads)
    atom_slab = atom_slab.reshape(windows, atom_heads, span, keys)
    atom_cross = jnp.sum(window_units[:, :, None] * wide(atom_slab)[:, None], axis=(0, 3, 4))
    vectors = [gain, offset, query, grad_gain, grad_offset, grad_query]
    vectors += [token_cross.reshape(1, -1), atom_cross.reshape(1, -1)]
    total = jnp.concatenate(vectors, axis=1)
    total = total + swap_section(total)
    total = total + swap_plane(total, 1)
    total = total + swap_plane(total, 2)
    for bit in more_bits():
        total = total + swap_bit(total, bit)
    total = total + swap_core(total)
    grad_gu, grad_down = assemble(here, chunk_a, total_a, core_a)
    got_d, got_b, total, feature_halves, output_halves, grad_gu = together(
        got_d, got_b, total, feature_halves, output_halves, grad_gu
    )
    total_b, total_d = exchange(("join", total_b, got_b), ("join", total_d, got_d))
    total_b, total_d, total = together(total_b, total_d, total)
    core_b, core_d, got = swap_core(total_b), swap_core(total_d), swap_near(total)
    core_d, got = together(core_d, got)
    total = (total + got)[0]
    (packed,) = assemble(here, chunk_d, total_d, core_d)
    core_b, packed, total = together(core_b, packed, total)
    grad_proj, grad_out, grad_cond = assemble(here, chunk_b, total_b, core_b)

    atom_width = features.shape[1]
    sizes = [6 * atom_width, 4 * atom_width, width, atom_block[6].shape[1], atom_width]
    sizes.append(2 * atom_width)
    pieces_of = []
    first = 0
    for size in sizes:
        pieces_of.append(packed[:, first : first + size])
        first += size
    atom_cond, atom_proj, atom_gather, atom_gu, atom_out, quarters = pieces_of
    atom_down = quarters.reshape(-1, 2, atom_width).transpose(1, 0, 2).reshape(-1, atom_width)


    sums = []
    first = 0
    for member in vectors:
        sums.append(total[first : first + member.size])
        first += member.size
    gain, offset, query, token_gain, token_offset, token_query = [
        run_of(member, section, 2) for member in sums[:6]
    ]
    token_cross = run_of(sums[6].reshape(heads, -1).T, section, 2)
    atom_cross = run_of(sums[7].reshape(atom_cross.shape), section, 2)
    token_pair_gain = jnp.sum(token_cross * wide(run_of(tokpair_weight, section, 2)), axis=1)
    token_pair_weight = token_cross * wide(run_of(tokpair_gain, section, 2))[:, None]
    pair_gain = jnp.sum(atom_cross * wide(run_of(atompair_weight, section, 2)), axis=1)
    pair_weight = atom_cross * wide(run_of(atompair_gain, section, 2))[:, None]
    return (
        output_halves,
        wide(feature_halves),
        gain,
        atom_cond,
        offset,
        atom_proj,
        query,
        atom_out,
        atom_gu,
        atom_down,
        pair_gain,
        pair_weight,
        atom_gather,
        token_gain,
        grad_cond,
        token_offset,
        grad_proj,
        token_query,
        grad_out,
        grad_gu,
        grad_down,
        token_pair_gain,
        token_pair_weight,
    )


def exchange_halves(member):
    section = lax.axis_index("section")
    halves = member.reshape(2, -1, member.shape[1])
    given = lax.dynamic_index_in_dim(halves, 1 - section, 0, keepdims=False)
    kept = lax.dynamic_index_in_dim(halves, section, 0, keepdims=False)
    taken = swap_section(given)
    first = section == 0
    return jnp.stack([jnp.where(first, kept, taken), jnp.where(first, taken, kept)])[:, None]


def solution(mesh):
    weights = [P()] * 21
    halves = P(None, "dp", "section", None)
    grads = [1, 2, 1, 2, 1, 2, 2, 2, 1, 2, 2, 1, 2, 1, 2, 1, 2, 2, 2, 1, 2]
    return jax.shard_map(
        local,
        mesh=mesh,
        in_specs=(
            P(None, "dp", None, None),
            P(),
            P("dp", None, None, None),
            P(),
            P(),
            P("dp", None, None),
            P(),
            P(),
            P(None, "dp"),
            P(None, "dp", None, None),
            *weights,
        ),
        out_specs=(halves, halves)
        + tuple(P("section") if rank == 1 else P("section", None) for rank in grads),
        check_vma=False,
    )
```

```python
import functools

import jax
import jax.numpy as jnp
from jax import lax
from jax.experimental import pallas as pl
from jax.experimental.pallas import tpu as pltpu
from jax.sharding import PartitionSpec as P

EPS = 1e-05
LOWTYPE = jnp.bfloat16
WIDE = jnp.float32
ATOM_ROWS = 256
MEBI = 1024 * 1024


def takes(microseconds):
    return pl.CostEstimate(flops=0, transcendentals=0, bytes_accessed=int(microseconds * 3690000))

FAR = 4


def product(left, right):
    return jnp.dot(left, right, preferred_element_type=WIDE)


def product_left(left, right):
    return lax.dot_general(left, right, (((0,), (0,)), ((), ())), preferred_element_type=WIDE)


def product_right(left, right):
    return lax.dot_general(left, right, (((1,), (1,)), ((), ())), preferred_element_type=WIDE)


def sigmoid(values):
    return 0.5 * jnp.tanh(0.5 * values) + 0.5


def normalise(values):
    centre = values - jnp.mean(values, axis=-1, keepdims=True)
    scale = lax.rsqrt(jnp.mean(centre * centre, axis=-1, keepdims=True) + EPS)
    return centre * scale, scale


def normalise_back(grad, unit, scale):
    return scale * (
        grad
        - jnp.mean(grad, axis=-1, keepdims=True)
        - unit * jnp.mean(grad * unit, axis=-1, keepdims=True)
    )


def column_sum(values):
    return jnp.sum(values, axis=0, keepdims=True)


def low(values):
    return values.astype(LOWTYPE)


def wide(values):
    return values.astype(WIDE)


def head_masks(head_count, head_size, width, kind):
    lanes = lax.broadcasted_iota(jnp.int32, (1, width), 1)
    return [
        jnp.where((lanes >= h * head_size) & (lanes < (h + 1) * head_size), 1.0, 0.0).astype(kind)
        for h in range(head_count)
    ]


def full_spec(member):
    rank = len(member.shape)
    return pl.BlockSpec(member.shape, lambda *_: (0,) * rank)


def conditioning(single, cond_gain, cond_weight, cond_bias, first, last):
    unit, _ = normalise(wide(single[...]))
    normed = low(unit * wide(cond_gain[...]))
    return product(normed, cond_weight[:, first:last]) + wide(cond_bias[:, first:last])


def atom_project_kernel(
    features, single, cond_gain, cond_weight, cond_bias, proj_weight, query_bias, projections
):
    width = features.shape[1]
    pieces = conditioning(single, cond_gain, cond_weight, cond_bias, 0, 2 * width)
    unit, _ = normalise(wide(features[...]))
    normed_one = low(unit * sigmoid(pieces[:, :width]) + pieces[:, width:])
    raw = product(normed_one, proj_weight[...])
    projections[:, :width] = low(raw[:, :width] + wide(query_bias[...]))
    projections[:, width:] = low(raw[:, width:])


def atom_project(features, single, weights):
    atoms, width = features.shape
    gain, cond, offset, proj, query = weights[:5]
    flat = [gain[None], cond, offset[None], proj, query[None]]
    rows = 2 * ATOM_ROWS
    return pl.pallas_call(
        atom_project_kernel,
        grid=(atoms // rows,),
        in_specs=[pl.BlockSpec((rows, width), lambda i: (i, 0))] * 2
        + [full_spec(member) for member in flat],
        out_specs=pl.BlockSpec((rows, 4 * width), lambda i: (i, 0)),
        out_shape=jax.ShapeDtypeStruct((atoms, 4 * width), LOWTYPE),
        cost_estimate=takes(2),
        compiler_params=pltpu.CompilerParams(
            dimension_semantics=("arbitrary",), vmem_limit_bytes=32 * MEBI
        ),
        name="atom_project",
    )(features, single, *flat)


def atom_attend_kernel(
    last_part,
    starts,
    place,
    firsts,
    features,
    single,
    token_rows,
    projections,
    bias_own,
    bias_other,
    cond_gain,
    cond_weight,
    cond_bias,
    out_weight,
    gu_weight,
    down_weight,
    gather_weight,
    *rest,
):
    if last_part:
        pool_before, count_before, _, _, pooled, counts, attended, probability = rest[:8]
    else:
        pooled, counts, attended, probability = rest[:4]
    key_wide, value_wide, pool_sum, count_sum = rest[-4:]
    step = pl.program_id(0)
    blocks = pl.num_programs(0)
    block = step + (blocks if last_part else 0)
    width = features.shape[1]
    _, _, half_group, head_count, span, keys = bias_own.shape
    group = 2 * half_group
    head_size = width // head_count
    factor = head_size**-0.5
    half = gu_weight.shape[1] // 2

    @pl.when(step == 0)
    def _():
        key_wide[...] = wide(projections[:, width : 2 * width])
        value_wide[...] = wide(projections[:, 2 * width : 3 * width])

    rows = pl.ds(pl.multiple_of(block * ATOM_ROWS, ATOM_ROWS), ATOM_ROWS)
    masks = head_masks(head_count, head_size, width, LOWTYPE)
    wide_masks = head_masks(head_count, head_size, width, WIDE)
    query_rows = projections[rows, :width]
    value_wins, all_scores, chances, parts = [], [], [], []
    for u in range(group):
        start = starts[block * group + u]
        key_win = low(key_wide[pl.ds(start, keys), :])
        value_wins.append(low(value_wide[pl.ds(start, keys), :]))
        query_win = query_rows[u * span : (u + 1) * span]
        stacked = jnp.concatenate([query_win * mask for mask in masks], axis=0)
        all_scores.append(product_right(stacked, key_win))
    for u in range(group):
        own, other = bias_own[0, 0, u % half_group], bias_other[0, 0, u % half_group]
        bias = jnp.where(place[3] == u // half_group, own, other)
        scores = all_scores[u] * factor + wide(bias.reshape(head_count * span, keys))
        exponent = jnp.exp(scores - jnp.max(scores, axis=-1, keepdims=True))
        chance = low(exponent * (1.0 / jnp.sum(exponent, axis=-1, keepdims=True)))
        probability[u] = chance
        chances.append(chance)
    for u in range(group):
        mixed = product(chances[u], value_wins[u])
        parts.append(
            sum(mixed[h * span : (h + 1) * span] * wide_masks[h] for h in range(head_count))
        )
    mixed = jnp.concatenate(parts, axis=0)
    attended[...] = mixed
    gated = low(mixed * sigmoid(wide(projections[rows, 3 * width :])))
    pieces = conditioning(
        single, cond_gain, cond_weight, cond_bias, 2 * width, 6 * width
    )
    middle = wide(features[...]) + sigmoid(pieces[:, :width]) * product(
        gated, out_weight[...]
    )
    unit, _ = normalise(middle)
    normed_two = low(
        unit * sigmoid(pieces[:, width : 2 * width]) + pieces[:, 2 * width : 3 * width]
    )
    gate_up = product(normed_two, gu_weight[...])
    gate_half = gate_up[:, :half]
    hidden = low(gate_half * sigmoid(gate_half) * gate_up[:, half:])
    result = low(middle + sigmoid(pieces[:, 3 * width :]) * product(hidden, down_weight[...]))
    pre_act = product(result, gather_weight[...])
    pooled_atoms = low(pre_act * sigmoid(pre_act))
    reach = ATOM_ROWS + 8
    first = jnp.minimum(firsts[block] // 8 * 8, pooled.shape[0] - reach)
    token_ids = token_rows[block]
    tokens = lax.broadcasted_iota(jnp.int32, (reach, ATOM_ROWS), 0) + first
    onehot = jnp.where(tokens == token_ids, 1.0, 0.0)
    part = product(low(onehot), pooled_atoms)
    part_count = jnp.sum(onehot, axis=1, keepdims=True)

    @pl.when(step == 0)
    def _():
        pool_sum[...] = pool_before[...] if last_part else jnp.zeros_like(pool_sum)
        count_sum[...] = count_before[...] if last_part else jnp.zeros_like(count_sum)

    reached = pl.ds(pl.multiple_of(first, 8), reach)
    pool_sum[reached, :] += part
    count_sum[reached, :] += part_count

    @pl.when(step == blocks - 1)
    def _():
        counts[...] = count_sum[...]
        pooled[...] = low(pool_sum[...] / count_sum[...]) if last_part else pool_sum[...]


def far_at(run, place):
    distance = run ^ place[1]
    return distance % 2 * 2 + distance // 2


def block_of(step, place):
    return step % 2 ^ place[2], far_at(step // 2, place)


def atom_attend(
    starts, place, features, single, atom_token, projections, bias, weights, gather_weight, length, before
):
    atoms, width = features.shape
    blocks = atoms // ATOM_ROWS
    steps = blocks // 2
    _, _, half_group, head_count, span, keys = bias[0].shape
    group = 2 * half_group
    windows = group * blocks
    model_width = gather_weight.shape[1]
    token_rows = atom_token.reshape(blocks, 1, ATOM_ROWS)
    gain, cond, offset, _, _, out, gu, down = weights
    flat = [gain[None], cond, offset[None], out, gu, down, gather_weight]
    first = steps if before else 0

    def bias_block(i, starts, place, firsts):
        near, far = block_of(i + first, place)
        return near, far, 0, 0, 0, 0

    rows = pl.BlockSpec((ATOM_ROWS, width), lambda i, *_: (i + first, 0))
    outs = [
        jax.ShapeDtypeStruct((length, model_width), LOWTYPE if before else WIDE),
        jax.ShapeDtypeStruct((length, 1), WIDE),
        jax.ShapeDtypeStruct((atoms, width), WIDE),
        jax.ShapeDtypeStruct((windows, head_count * span, keys), LOWTYPE),
    ]
    members = [features, single, token_rows, projections, *bias, *flat]
    specs = [rows, rows, full_spec(token_rows), full_spec(projections)]
    specs += [pl.BlockSpec((1, 1, half_group, head_count, span, keys), bias_block)] * 2
    specs += [full_spec(member) for member in flat]
    aliases = {}
    if before:
        members += before
        specs += [full_spec(member) for member in before[:2]]
        specs += [pl.BlockSpec(memory_space=pl.ANY)] * 2
        aliases = {len(members) + 1 : 2, len(members) + 2 : 3}
    return pl.pallas_call(
        functools.partial(atom_attend_kernel, bool(before)),
        grid_spec=pltpu.PrefetchScalarGridSpec(
            num_scalar_prefetch=3,
            grid=(steps,),
            in_specs=specs,
            out_specs=[full_spec(member) for member in outs[:2]]
            + [rows, pl.BlockSpec((group, head_count * span, keys), lambda i, *_: (i + first, 0, 0))],
            scratch_shapes=[
                pltpu.VMEM((atoms, width), WIDE),
                pltpu.VMEM((atoms, width), WIDE),
                pltpu.VMEM((length, model_width), WIDE),
                pltpu.VMEM((length, 1), WIDE),
            ],
        ),
        out_shape=outs,
        input_output_aliases=aliases,
        cost_estimate=takes(2),
        compiler_params=pltpu.CompilerParams(
            dimension_semantics=("arbitrary",), vmem_limit_bytes=56 * MEBI
        ),
        name="atom_attend",
    )(starts, place, atom_token[::ATOM_ROWS], *members)


def atom_tokens_back_kernel(
    firsts,
    features,
    single,
    token_cols,
    gates,
    attended,
    d_tokens,
    counts,
    cond_gain,
    cond_weight,
    cond_bias,
    out_weight,
    gu_weight,
    down_weight,
    gather_weight,
    d_attended,
    d_gates,
    d_middles,
    d_pieces,
    packed,
    grad_out,
    grad_gu,
    grad_down,
    grad_gather,
    d_scaled,
):
    step = pl.program_id(0)
    blocks = pl.num_programs(0)
    width = features.shape[1]
    half = gu_weight.shape[1] // 2

    @pl.when(step == 0)
    def _():
        d_scaled[...] = low(wide(d_tokens[...]) * (1.0 / counts[...]))
        for member in (grad_out, grad_gu, grad_down, grad_gather):
            member[...] = jnp.zeros_like(member)

    rows = slice(None)
    unit, _ = normalise(wide(single[rows, :]))
    normed = low(unit * wide(cond_gain[...]))
    pieces = product(normed, cond_weight[:, 2 * width :]) + wide(cond_bias[:, 2 * width :])
    mixed = attended[rows, :]
    gate = sigmoid(wide(gates[rows, :]))
    gated = low(mixed * gate)
    attn_out = product(gated, out_weight[...])
    gate_one = sigmoid(pieces[:, :width])
    middle = wide(features[rows, :]) + gate_one * attn_out
    unit_two, spread_two = normalise(middle)
    scale_two = sigmoid(pieces[:, width : 2 * width])
    normed_two = low(unit_two * scale_two + pieces[:, 2 * width : 3 * width])
    gate_up = product(normed_two, gu_weight[...])
    gate_half, up_half = gate_up[:, :half], gate_up[:, half:]
    logistic = sigmoid(gate_half)
    hidden = low(gate_half * logistic * up_half)
    down_out = product(hidden, down_weight[...])
    gate_two = sigmoid(pieces[:, 3 * width :])
    result = low(middle + gate_two * down_out)
    pre_act = product(result, gather_weight[...])

    reach = ATOM_ROWS + 16
    first = jnp.minimum(firsts[step] // 16 * 16, d_tokens.shape[0] - reach)
    tokens = lax.broadcasted_iota(jnp.int32, (ATOM_ROWS, reach), 1) + first
    onehot = low(jnp.where(tokens == token_cols[...], 1.0, 0.0))
    d_rows = product(onehot, d_scaled[pl.ds(pl.multiple_of(first, 16), reach), :])
    pre_logistic = sigmoid(pre_act)
    d_pre = low(d_rows * (pre_logistic * (1.0 + pre_act * (1.0 - pre_logistic))))
    grad_gather[...] += product_left(result, d_pre)
    d_result = product_right(d_pre, gather_weight[...])

    d_down = low(d_result * gate_two)
    d_pieces[rows, 3 * width :] = low(d_result * down_out * gate_two * (1.0 - gate_two))
    grad_down[...] += product_left(hidden, d_down)
    d_hidden = wide(low(product_right(d_down, down_weight[...])))
    d_gate_half = low(d_hidden * up_half * logistic * (1.0 + gate_half * (1.0 - logistic)))
    d_up_half = low(d_hidden * gate_half * logistic)
    d_gate_up = jnp.concatenate([d_gate_half, d_up_half], axis=1)
    grad_gu[...] += product_left(normed_two, d_gate_up)
    d_normed_two = product_right(d_gate_up, gu_weight[...])
    d_pieces[rows, 2 * width : 3 * width] = low(d_normed_two)
    d_pieces[rows, width : 2 * width] = low(
        d_normed_two * unit_two * scale_two * (1.0 - scale_two)
    )
    d_middle = d_result + normalise_back(d_normed_two * scale_two, unit_two, spread_two)
    d_middles[rows, :] = d_middle
    d_attn_out = low(d_middle * gate_one)
    d_pieces[rows, :width] = low(
        d_middle * attn_out * gate_one * (1.0 - gate_one)
    )
    grad_out[...] += product_left(gated, d_attn_out)
    d_gated = wide(low(product_right(d_attn_out, out_weight[...])))
    d_attended[rows, :] = low(d_gated * gate)
    d_gates[rows, :] = low(d_gated * mixed * gate * (1.0 - gate))

    @pl.when(step == blocks - 1)
    def _():
        model_width = gather_weight.shape[1]
        packed[:, :model_width] = low(grad_gather[...])
        last = model_width + 2 * half
        packed[:, model_width:last] = low(grad_gu[...])
        packed[:, last : last + width] = low(grad_out[...])
        last = last + width
        run = grad_down.shape[0] // 4
        for part in range(4):
            rows_at = slice(part // 2 * run, (part // 2 + 1) * run)
            columns = slice(last + part % 2 * width, last + (part % 2 + 1) * width)
            packed[rows_at, columns] = low(grad_down[part * run : (part + 1) * run, :])


def atom_attention_back_kernel(
    starts,
    place,
    projections,
    attended,
    probability,
    d_attended,
    d_projections,
    d_bias_own,
    d_bias_other,
    key_wide,
    value_wide,
    d_keys,
    d_values,
):
    step = pl.program_id(0)
    blocks = pl.num_programs(0)
    width = attended.shape[1]
    group, stack, keys = probability.shape
    half_group = group // 2
    span = ATOM_ROWS // group
    head_count = stack // span
    head_size = width // head_count
    factor = head_size**-0.5

    @pl.when(step == 0)
    def _():
        for member in (d_keys, d_values):
            member[...] = jnp.zeros_like(member)
        key_wide[...] = wide(projections[:, width : 2 * width])
        value_wide[...] = wide(projections[:, 2 * width : 3 * width])

    rows = pl.ds(pl.multiple_of(step * ATOM_ROWS, ATOM_ROWS), ATOM_ROWS)
    row_grad = d_attended[...]
    row_part = wide(row_grad) * attended[...]

    masks = head_masks(head_count, head_size, width, LOWTYPE)
    wide_masks = head_masks(head_count, head_size, width, WIDE)
    query_rows = projections[rows, :width]
    held = []
    for u in range(group):
        start = starts[step * group + u]
        cut = slice(u * span, (u + 1) * span)
        key_win = low(key_wide[pl.ds(start, keys), :])
        value_win = low(value_wide[pl.ds(start, keys), :])
        stacked_query = jnp.concatenate([query_rows[cut] * mask for mask in masks], axis=0)
        stacked_grad = jnp.concatenate([row_grad[cut] * mask for mask in masks], axis=0)
        stacked_part = jnp.concatenate([row_part[cut] * mask for mask in wide_masks], axis=0)
        row_sum = jnp.sum(stacked_part, axis=-1, keepdims=True)
        d_chance = product_right(stacked_grad, value_win)
        held.append((start, key_win, stacked_query, stacked_grad, row_sum, d_chance))
    score_grads = [
        low(wide(probability[u]) * (held[u][5] - held[u][4])) for u in range(group)
    ]
    query_grads, key_grads, value_grads = [], [], []
    for u in range(group):
        _, key_win, stacked_query, stacked_grad, _, _ = held[u]
        d_stacked = product(score_grads[u], key_win) * factor
        query_grads.append(
            sum(d_stacked[h * span : (h + 1) * span] * wide_masks[h] for h in range(head_count))
        )
        key_grads.append(product_left(score_grads[u], stacked_query) * factor)
        value_grads.append(product_left(probability[u], stacked_grad))
    for u in range(group):
        window = pl.ds(held[u][0], keys)
        d_keys[window, :] += key_grads[u]
        d_values[window, :] += value_grads[u]
    d_projections[rows, :width] = low(jnp.concatenate(query_grads, axis=0))
    for u in range(half_group):
        first = place[3] == 0
        d_bias_own[0, 0, u] = jnp.where(first, score_grads[u], score_grads[u + half_group])
        d_bias_other[0, 0, u] = jnp.where(first, score_grads[u + half_group], score_grads[u])

    @pl.when(step == blocks - 1)
    def _():
        d_projections[:, width : 2 * width] = low(d_keys[...])
        d_projections[:, 2 * width : 3 * width] = low(d_values[...])


def atom_features_back_kernel(
    features,
    single,
    d_projections,
    d_gates,
    d_middles,
    d_pieces,
    cond_gain,
    cond_weight,
    cond_bias,
    proj_weight,
    d_features,
    packed,
    grad_gain,
    grad_offset,
    grad_query,
    grad_cond,
    grad_proj,
):
    step = pl.program_id(0)
    blocks = pl.num_programs(0)
    width = features.shape[1]

    @pl.when(step == 0)
    def _():
        for member in (grad_gain, grad_offset, grad_query, grad_cond, grad_proj):
            member[...] = jnp.zeros_like(member)

    unit, _ = normalise(wide(single[...]))
    normed = low(unit * wide(cond_gain[...]))
    pieces = product(normed, cond_weight[:, : 2 * width]) + wide(cond_bias[:, : 2 * width])
    unit_one, spread_one = normalise(wide(features[...]))
    scale_one = sigmoid(pieces[:, :width])
    normed_one = low(unit_one * scale_one + pieces[:, width:])
    d_projection = jnp.concatenate([d_projections[...], d_gates[...]], axis=1)
    grad_proj[...] += product_left(normed_one, d_projection)
    grad_query[...] += column_sum(wide(d_projection[:, :width]))
    d_normed_one = product_right(d_projection, proj_weight[...])
    d_features[...] = d_middles[...] + normalise_back(
        d_normed_one * scale_one, unit_one, spread_one
    )
    d_projected = jnp.concatenate(
        [
            low(d_normed_one * unit_one * scale_one * (1.0 - scale_one)),
            low(d_normed_one),
            d_pieces[...],
        ],
        axis=1,
    )
    grad_cond[...] += product_left(normed, d_projected)
    grad_offset[...] += column_sum(wide(d_projected))
    d_normed = product_right(d_projected, cond_weight[...])
    grad_gain[...] += column_sum(d_normed * unit)

    @pl.when(step == blocks - 1)
    def _():
        packed[:, : 6 * width] = low(grad_cond[...])
        packed[:, 6 * width :] = low(grad_proj[...])


def atom_tokens_back(features, single, atom_token, d_tokens, counts, stored, weights, gather_weight):
    projections, attended, _ = stored
    atoms, width = features.shape
    gain, cond, offset, _, _, out, gu, down = weights
    flat = [gain[None], cond, offset[None], out, gu, down, gather_weight]
    token_cols = atom_token.reshape(atoms, 1)
    columns = gather_weight.shape[1] + gu.shape[1] + 3 * width
    outs = [
        jax.ShapeDtypeStruct((atoms, width), LOWTYPE),
        jax.ShapeDtypeStruct((atoms, width), LOWTYPE),
        jax.ShapeDtypeStruct((atoms, width), WIDE),
        jax.ShapeDtypeStruct((atoms, 4 * width), LOWTYPE),
        jax.ShapeDtypeStruct((width, columns), LOWTYPE),
    ]

    def rows_of(member):
        return pl.BlockSpec((ATOM_ROWS, member.shape[1]), lambda i, *_: (i, 0))

    return pl.pallas_call(
        atom_tokens_back_kernel,
        grid_spec=pltpu.PrefetchScalarGridSpec(
            num_scalar_prefetch=1,
            grid=(atoms // ATOM_ROWS,),
            in_specs=[
            rows_of(features),
            rows_of(single),
            rows_of(token_cols),
            pl.BlockSpec((ATOM_ROWS, width), lambda i, *_: (i, 3)),
            rows_of(attended),
            full_spec(d_tokens),
            full_spec(counts),
        ]
        + [full_spec(member) for member in flat],
        out_specs=[rows_of(member) for member in outs[:4]] + [full_spec(outs[4])],
            scratch_shapes=[
                pltpu.VMEM(member.shape, WIDE) for member in (out, gu, down, gather_weight)
            ]
            + [pltpu.VMEM(d_tokens.shape, LOWTYPE)],
        ),
        out_shape=outs,
        cost_estimate=takes(3),
        compiler_params=pltpu.CompilerParams(
            dimension_semantics=("arbitrary",), vmem_limit_bytes=56 * MEBI
        ),
        name="atom_tokens_back",
    )(atom_token[::ATOM_ROWS], features, single, token_cols, projections, attended, d_tokens, counts, *flat)


def atom_attention_back(starts, place, d_attended, stored):
    projections, attended, probability = stored
    atoms, width = attended.shape
    blocks = atoms // ATOM_ROWS
    windows, stack, keys = probability.shape
    group = windows // blocks
    score_shape = (2, blocks // 2, group // 2, stack, keys)
    outs = [
        jax.ShapeDtypeStruct((atoms, 3 * width), LOWTYPE),
        jax.ShapeDtypeStruct(score_shape, LOWTYPE),
        jax.ShapeDtypeStruct(score_shape, LOWTYPE),
    ]

    def bias_block(i, starts, place):
        near, far = block_of(i, place)
        return near, far, 0, 0, 0

    block = pl.BlockSpec((ATOM_ROWS, width), lambda i, *_: (i, 0))
    return pl.pallas_call(
        atom_attention_back_kernel,
        grid_spec=pltpu.PrefetchScalarGridSpec(
            num_scalar_prefetch=2,
            grid=(blocks,),
            in_specs=[
                full_spec(projections),
                block,
                pl.BlockSpec((group, stack, keys), lambda i, *_: (i, 0, 0)),
                block,
            ],
            out_specs=[full_spec(outs[0])]
            + [pl.BlockSpec((1, 1, group // 2, stack, keys), bias_block)] * 2,
            scratch_shapes=[pltpu.VMEM((atoms, width), WIDE)] * 4,
        ),
        out_shape=outs,
        cost_estimate=takes(2),
        compiler_params=pltpu.CompilerParams(
            dimension_semantics=("arbitrary",), vmem_limit_bytes=56 * MEBI
        ),
        name="atom_attention_back",
    )(starts, place, projections, attended, probability, d_attended)


def atom_features_back(features, single, d_projections, d_gates, d_middles, d_pieces, weights):
    atoms, width = features.shape
    gain, cond, offset, proj = weights[:4]
    flat = [gain[None], cond, offset[None], proj]
    rows = [features, single, d_projections, d_gates, d_middles, d_pieces]
    outs = [
        jax.ShapeDtypeStruct((atoms, width), WIDE),
        jax.ShapeDtypeStruct((width, 10 * width), LOWTYPE),
        jax.ShapeDtypeStruct((1, width), WIDE),
        jax.ShapeDtypeStruct((1, 6 * width), WIDE),
        jax.ShapeDtypeStruct((1, width), WIDE),
    ]
    return pl.pallas_call(
        atom_features_back_kernel,
        grid=(atoms // ATOM_ROWS,),
        in_specs=[
            pl.BlockSpec((ATOM_ROWS, member.shape[1]), lambda i: (i, 0)) for member in rows
        ]
        + [full_spec(member) for member in flat],
        out_specs=[pl.BlockSpec((ATOM_ROWS, width), lambda i: (i, 0))]
        + [full_spec(member) for member in outs[1:]],
        out_shape=outs,
        scratch_shapes=[pltpu.VMEM(cond.shape, WIDE), pltpu.VMEM(proj.shape, WIDE)],
        cost_estimate=takes(0.5),
        compiler_params=pltpu.CompilerParams(
            dimension_semantics=("arbitrary",), vmem_limit_bytes=32 * MEBI
        ),
        name="atom_features_back",
    )(*rows, *flat)


LANES = 128
GROUP_HEADS = 8
STAGE = 1
FORWARD_PARTS = 1
BACKWARD_PARTS = 1


def head_window(head, head_size, total):
    first = min(head * head_size // LANES * LANES, total - 2 * LANES)
    return first, head * head_size - first


def head_lanes(offset, head_size, kind):
    lanes = lax.broadcasted_iota(jnp.int32, (1, 2 * LANES), 1)
    return jnp.where((lanes >= offset) & (lanes < offset + head_size), 1.0, 0.0).astype(kind)


def chosen_rows(place, own, other, head, runs, section_first):
    parts = []
    for far in runs:
        for near in range(2):
            for core in range(2):
                for section in range(2):
                    at = [near ^ place[2], section ^ place[0]]
                    at = (*(at[::-1] if section_first else at), far_at(far, place), head)
                    parts.append(jnp.where(place[3] == core, own[at], other[at]))
    return jnp.concatenate(parts, axis=0)


def token_forward_kernel(
    place, queries, keys, values, gates, own_a, other_a, own_b, other_b, probability, attended, gated
):
    heads = probability.shape[0]
    rows, total = queries.shape
    head_size = total // heads
    factor = head_size**-0.5

    run_count = FAR // FORWARD_PARTS
    runs = [pl.program_id(1) * run_count + index for index in range(run_count)]

    def score(h):
        first, offset = head_window(h, head_size, total)
        cut = slice(first, first + 2 * LANES)
        return product_right(queries[:, cut] * head_lanes(offset, head_size, LOWTYPE), keys[:, cut])

    def attend(own, other, section_first):
        tiles = [None] * (total // LANES)
        for start in range(0, heads, STAGE):
            run = range(start, start + STAGE)
            raw_scores = [score(h) for h in run]
            chances = []
            for h in run:
                scores = raw_scores[h - start] * factor + wide(
                    chosen_rows(place, own, other, h, runs, section_first)
                )
                exponent = jnp.exp(scores - jnp.max(scores, axis=-1, keepdims=True))
                chance = low(exponent * (1.0 / jnp.sum(exponent, axis=-1, keepdims=True)))
                probability[h] = chance
                chances.append(chance)
            for h in run:
                first, offset = head_window(h, head_size, total)
                mixed = product(chances[h - start], values[:, first : first + 2 * LANES])
                mixed = mixed * head_lanes(offset, head_size, WIDE)
                for t in range(2):
                    at = first // LANES + t
                    part = mixed[:, t * LANES : (t + 1) * LANES]
                    tiles[at] = part if tiles[at] is None else tiles[at] + part
        whole = jnp.concatenate(tiles, axis=1)
        attended[...] = whole
        gated[...] = low(whole * sigmoid(wide(gates[...])))

    @pl.when(pl.program_id(0) == 0)
    def _():
        attend(own_a, other_a, True)

    @pl.when(pl.program_id(0) == 1)
    def _():
        attend(own_b, other_b, False)


def token_forward(place, projections, bias):
    length, columns = projections.shape
    width = columns // 4
    rows = length // FORWARD_PARTS
    group_heads = bias[0].shape[3]
    groups = len(bias) // 2
    heads = group_heads * groups
    total = width // groups
    block = pl.BlockSpec((rows, total), lambda g, i, _: (i, g))
    return pl.pallas_call(
        token_forward_kernel,
        grid_spec=pltpu.PrefetchScalarGridSpec(
            num_scalar_prefetch=1,
            grid=(groups, FORWARD_PARTS),
            in_specs=[
                block,
                pl.BlockSpec((length, total), lambda g, i, _: (0, groups + g)),
                pl.BlockSpec((length, total), lambda g, i, _: (0, 2 * groups + g)),
                pl.BlockSpec((rows, total), lambda g, i, _: (i, 3 * groups + g)),
            ]
            + [full_spec(member) for member in bias],
            out_specs=[
                pl.BlockSpec((group_heads, rows, length), lambda g, i, _: (g, i, 0)),
                block,
                block,
            ],
        ),
        out_shape=[
            jax.ShapeDtypeStruct((heads, length, length), LOWTYPE),
            jax.ShapeDtypeStruct((length, width), WIDE),
            jax.ShapeDtypeStruct((length, width), LOWTYPE),
        ],
        cost_estimate=takes(2),
        compiler_params=pltpu.CompilerParams(
            dimension_semantics=("arbitrary", "arbitrary"), vmem_limit_bytes=56 * MEBI
        ),
        name="token_forward",
    )(place, projections, projections, projections, projections, *bias)


def token_backward_kernel(
    place,
    queries,
    keys,
    values,
    gates,
    probability,
    attended,
    d_gated,
    own,
    other,
    d_projections,
    d_keys,
    d_values,
):
    group, step = pl.program_id(0), pl.program_id(1)
    heads = probability.shape[0]
    rows, total = queries.shape
    head_size = total // heads
    factor = head_size**-0.5
    width = d_projections.shape[1] // 4
    run = own.shape[4]

    @pl.when(step == 0)
    def _():
        d_keys[...] = jnp.zeros_like(d_keys)
        d_values[...] = jnp.zeros_like(d_values)

    gate = sigmoid(wide(gates[...]))
    grad = wide(d_gated[...])
    mixed = attended[...]
    d_attended = low(grad * gate)
    d_gates = low(grad * mixed * gate * (1.0 - gate))
    row_part = wide(d_attended) * mixed

    def chance_grad(h):
        first, offset = head_window(h, head_size, total)
        cut = slice(first, first + 2 * LANES)
        mask = head_lanes(offset, head_size, LOWTYPE)
        return product_right(d_attended[:, cut] * mask, values[:, cut])

    tiles = [None] * (total // LANES)
    for begin in range(0, heads, STAGE):
        run_heads = range(begin, begin + STAGE)
        d_chances = [chance_grad(h) for h in run_heads]
        score_grads = []
        for h in run_heads:
            first, offset = head_window(h, head_size, total)
            cut = slice(first, first + 2 * LANES)
            row_sum = jnp.sum(
                row_part[:, cut] * head_lanes(offset, head_size, WIDE), axis=-1, keepdims=True
            )
            d_scores = low(wide(probability[h]) * (d_chances[h - begin] - row_sum))
            score_grads.append(d_scores)
            for index in range(FAR // BACKWARD_PARTS):
                far = far_at(step * (FAR // BACKWARD_PARTS) + index, place)
                for near in range(2):
                    for section in range(2):
                        at = (near ^ place[2], section ^ place[0], far, h)
                        pair = []
                        for core in range(2):
                            start = (8 * index + 4 * near + 2 * core + section) * run
                            pair.append(d_scores[start : start + run])
                        own[at] = jnp.where(place[3] == 0, pair[0], pair[1])
                        other[at] = jnp.where(place[3] == 0, pair[1], pair[0])
        for h in run_heads:
            first, offset = head_window(h, head_size, total)
            cut = slice(first, first + 2 * LANES)
            mask = head_lanes(offset, head_size, LOWTYPE)
            d_scores = score_grads[h - begin]
            part = product(d_scores, keys[:, cut]) * (wide(mask) * factor)
            for t in range(2):
                at = first // LANES + t
                piece = part[:, t * LANES : (t + 1) * LANES]
                tiles[at] = piece if tiles[at] is None else tiles[at] + piece
            d_keys[:, cut] += product_left(d_scores, queries[:, cut] * mask)
            d_values[:, cut] += product_left(probability[h], d_attended[:, cut] * mask)
    rows_at = pl.ds(pl.multiple_of(step * rows, rows), rows)
    first = group * total
    d_projections[rows_at, pl.ds(pl.multiple_of(first, LANES), total)] = low(
        jnp.concatenate(tiles, axis=1)
    )
    gates_at = pl.ds(pl.multiple_of(first + 3 * width, LANES), total)
    d_projections[rows_at, gates_at] = d_gates

    @pl.when(step == pl.num_programs(1) - 1)
    def _():
        first = group * total
        d_projections[:, pl.ds(pl.multiple_of(first + width, LANES), total)] = low(
            d_keys[...] * factor
        )
        d_projections[:, pl.ds(pl.multiple_of(first + 2 * width, LANES), total)] = low(
            d_values[...]
        )


def token_backward(place, projections, probability, attended, d_gated, run):
    length, columns = projections.shape
    width = columns // 4
    rows = length // BACKWARD_PARTS
    heads = probability.shape[0]
    groups = heads // GROUP_HEADS
    total = width // groups
    block = pl.BlockSpec((rows, total), lambda g, i, _: (i, g))
    grad = jax.ShapeDtypeStruct((2, 2, FAR, heads, run, length), LOWTYPE)
    grad_spec = pl.BlockSpec(
        (2, 2, FAR, GROUP_HEADS, run, length), lambda g, i, place: (0, 0, 0, g, 0, 0)
    )
    return pl.pallas_call(
        token_backward_kernel,
        grid_spec=pltpu.PrefetchScalarGridSpec(
            num_scalar_prefetch=1,
            grid=(groups, BACKWARD_PARTS),
            in_specs=[
                block,
                pl.BlockSpec((length, total), lambda g, i, _: (0, groups + g)),
                pl.BlockSpec((length, total), lambda g, i, _: (0, 2 * groups + g)),
                pl.BlockSpec((rows, total), lambda g, i, _: (i, 3 * groups + g)),
                pl.BlockSpec((GROUP_HEADS, rows, length), lambda g, i, _: (g, i, 0)),
                block,
                block,
            ],
            out_specs=[grad_spec] * 2
            + [pl.BlockSpec((length, columns), lambda g, i, _: (0, 0))],
            scratch_shapes=[pltpu.VMEM((length, total), WIDE)] * 2,
        ),
        out_shape=[grad] * 2 + [jax.ShapeDtypeStruct((length, columns), LOWTYPE)],
        cost_estimate=takes(3),
        compiler_params=pltpu.CompilerParams(
            dimension_semantics=("arbitrary", "arbitrary"), vmem_limit_bytes=56 * MEBI
        ),
        name="token_backward",
    )(place, projections, projections, projections, projections, probability, attended, d_gated)


PIECES = 8
COLUMNS = 384


def places():
    place = lax.axis_index("dp")
    return lax.axis_index("section"), place // 4, place // 2 % 2, place % 2


def swap_section(member):
    return lax.ppermute(member, "section", [(0, 1), (1, 0)])


def swap_bit(member, bit):
    return lax.ppermute(member, "dp", [(i, i ^ (1 << bit)) for i in range(lax.axis_size("dp"))])


def swap_core(member):
    return swap_bit(member, 0)


def swap_near(member):
    return swap_bit(member, 1)


def swap_far(member, bit):
    return swap_bit(member, 2 + bit)


def more_bits():
    return range(4, (lax.axis_size("dp") - 1).bit_length())


def piece_index():
    place = lax.axis_index("dp")
    return place // 2 % 2 * 4 + place // 4 % 2 * 2 + place // 8 % 2


def run_of(member, index, count):
    rows = member.shape[0] // count
    return lax.dynamic_slice_in_dim(member, index * rows, rows, 0)


def add_low(*members):
    return low(sum(wide(member) for member in members))


def scatter_plane(member):
    for bit, half in ((2, 2), (3, 1)):
        member = add_low(member[:half], swap_bit(member[half:], bit))
    for bit in more_bits():
        member = add_low(member, swap_bit(member, bit))
    return member


def rest_sum(*members):
    total = add_low(*members)
    for bit in more_bits():
        total = add_low(total, swap_bit(total, bit))
    return total


def from_here(member):
    half = member.shape[1] // 2
    first, second = member[:, :half], member[:, half:]
    turned = jnp.concatenate([second, first], axis=1)
    return jnp.where(lax.axis_index("section") == 0, member, turned)


def gather_pieces(member):
    for bit in (3, 2, 1):
        member = jnp.concatenate([member, swap_bit(member, bit)], axis=0)
    return member


class Weight:
    def __init__(self, rows, columns):
        self.rows, self.columns = rows // 2, columns
        self.blocks = columns // 2 // COLUMNS
        self.run = self.blocks * self.rows // PIECES

    def segments(self, piece):
        at, last, found = piece * self.run, (piece + 1) * self.run, []
        while at < last:
            block, row = divmod(at, self.rows)
            size = min(self.rows - row, last - at)
            found.append((block, row, size, at - piece * self.run))
            at += size
        return found


def aligned(start, size, step):
    return pl.ds(pl.multiple_of(start, step), size)


def product_blocks(place, weights, members, core, half):
    found, at = [], 0
    for weight in weights:
        if weight.direct:
            held = members[at]
            at += 1
        else:
            left, right = members[at], members[at + 1]
            at += 2
            if weight.rows % LANES:
                side = left[:, half * weight.rows : (half + 1) * weight.rows]
            else:
                side = left[:, aligned((half ^ place[0]) * weight.rows, weight.rows, LANES)]
        blocks = []
        for block in range(weight.blocks):
            columns = aligned(
                core * (weight.columns // 2) + block * COLUMNS, COLUMNS, LANES
            )
            if weight.direct:
                rows = aligned((half ^ place[0]) * weight.rows, weight.rows, 16)
                blocks.append(wide(held[rows, columns]))
            else:
                blocks.append(product_left(side, right[:, columns]))
        found.append(blocks)
    return found


def store_pieces(place, weights, found, store):
    for piece in range(PIECES):
        at = 0
        for weight, blocks in zip(weights, found):
            for block, row, size, offset in weight.segments(piece):
                store(piece ^ place[4], slice(at + offset, at + offset + size), blocks[block][row : row + size])
            at += weight.run


def given_kernel(weights, place, *refs):
    *members, out = refs
    for half in range(2):

        @pl.when(pl.program_id(0) == half)
        def _(half=half):
            def store(piece, rows, values):
                out[0, piece, rows, :] = low(values)

            store_pieces(
                place, weights, product_blocks(place, weights, members, 1 - place[3], half), store
            )


def kept_kernel(weights, place, *refs):
    *members, received, given, kept = refs
    for step, (half, target) in enumerate(((1, given), (0, kept))):

        @pl.when(pl.program_id(0) == step)
        def _(half=half, target=target):
            def store(piece, rows, values):
                target[piece, rows, :] = low(values + wide(received[0, piece, rows, :]))

            store_pieces(
                place, weights, product_blocks(place, weights, members, place[3], half), store
            )


def chunk_rows(weights):
    return sum(weight.run for weight in weights)


def chunk_given(place, weights, members):
    block = (1, PIECES, chunk_rows(weights), COLUMNS)
    return pl.pallas_call(
        functools.partial(given_kernel, weights),
        grid_spec=pltpu.PrefetchScalarGridSpec(
            num_scalar_prefetch=1,
            grid=(2,),
            in_specs=[full_spec(member) for member in members],
            out_specs=pl.BlockSpec(block, lambda i, _: (i, 0, 0, 0)),
        ),
        out_shape=jax.ShapeDtypeStruct((2, *block[1:]), LOWTYPE),
        cost_estimate=takes(0.5 if weights[0].direct else 3),
        compiler_params=pltpu.CompilerParams(
            dimension_semantics=("arbitrary",), vmem_limit_bytes=48 * MEBI
        ),
        name="chunk_given",
    )(place, *members)


def chunk_kept(place, weights, members, received):
    block = (1, PIECES, chunk_rows(weights), COLUMNS)
    out = jax.ShapeDtypeStruct(block[1:], LOWTYPE)
    return pl.pallas_call(
        functools.partial(kept_kernel, weights),
        grid_spec=pltpu.PrefetchScalarGridSpec(
            num_scalar_prefetch=1,
            grid=(2,),
            in_specs=[full_spec(member) for member in members]
            + [pl.BlockSpec(block, lambda i, _: (1 - i, 0, 0, 0))],
            out_specs=[full_spec(out), full_spec(out)],
        ),
        out_shape=[out, out],
        cost_estimate=takes(0.5 if weights[0].direct else 6),
        compiler_params=pltpu.CompilerParams(
            dimension_semantics=("arbitrary",), vmem_limit_bytes=48 * MEBI
        ),
        name="chunk_kept",
    )(place, *members, received)


def assemble_kernel(weights, parts, place, *refs):
    outs = refs[2 * parts :]
    for index, core in ((0, place[3]), (1, 1 - place[3])):
        members = refs[index * parts : (index + 1) * parts]
        for piece in range(PIECES):
            at = 0
            for weight, out in zip(weights, outs):
                for block, row, size, offset in weight.segments(piece):
                    columns = aligned(
                        core * (weight.columns // 2) + block * COLUMNS, COLUMNS, LANES
                    )
                    rows = slice(at + offset, at + offset + size)
                    place_at = piece ^ place[4]
                    if parts == 1:
                        out[row : row + size, columns] = wide(members[0][place_at, rows, :])
                    else:
                        first = members[0][place_at % (PIECES // 2), rows, :]
                        second = members[1][place_at % (PIECES // 2), rows, :]
                        chosen = jnp.where(place_at < PIECES // 2, first, second)
                        out[row : row + size, columns] = wide(chosen)
                at += weight.run


def assemble(place, weights, own, other):
    outs = [jax.ShapeDtypeStruct((weight.rows, weight.columns), WIDE) for weight in weights]
    return pl.pallas_call(
        functools.partial(assemble_kernel, weights, len(own)),
        grid_spec=pltpu.PrefetchScalarGridSpec(
            num_scalar_prefetch=1,
            grid=(1,),
            in_specs=[full_spec(member) for member in [*own, *other]],
            out_specs=[full_spec(member) for member in outs],
        ),
        out_shape=outs,
        cost_estimate=takes(2),
        compiler_params=pltpu.CompilerParams(
            dimension_semantics=("arbitrary",), vmem_limit_bytes=48 * MEBI
        ),
        name="assemble",
    )(place, *own, *other)


def products(*shapes):
    weights = [Weight(*shape) for shape in shapes]
    for weight in weights:
        weight.direct = False
    return weights


def split_vectors(total, vectors, section, atom_shape, pair_params):
    tok_gain, tok_weight, atom_gain, atom_weight = pair_params
    sums = []
    first = 0
    for member in vectors:
        sums.append(total[first : first + member.size])
        first += member.size
    halves = [run_of(member, section, 2) for member in sums[:6]]
    token_cross = run_of(sums[6].reshape(tok_weight.shape[1], -1).T, section, 2)
    atom_cross = run_of(sums[7].reshape(atom_shape), section, 2)
    for cross, gain, weight in (
        (token_cross, tok_gain, tok_weight),
        (atom_cross, atom_gain, atom_weight),
    ):
        halves.append(jnp.sum(cross * wide(run_of(weight, section, 2)), axis=1))
        halves.append(cross * wide(run_of(gain, section, 2))[:, None])
    return halves


def half_block(shape, count=2):
    axis = len(shape) - 2
    if shape[axis] % (16 * count):
        axis -= 1
    block = list(shape)
    block[axis] //= count
    return pl.BlockSpec(tuple(block), lambda i: tuple(i if a == axis else 0 for a in range(len(shape))))


def exchange_kernel(entries, *refs):
    refs = list(refs)
    members = [[refs.pop(0) for _ in range(1 + count)] for _, count in entries]
    for (axis, _), (kept, *got) in zip(entries, members):
        if axis == "join":
            out = refs.pop(0)
            rows = kept.shape[0]
            for index, member in enumerate([kept, *got]):
                out[index * rows : (index + 1) * rows] = member[...]
        elif axis == "group":
            rows = kept.shape[0]
            for side in range(2):
                out = refs.pop(0)
                out[:rows] = kept[:, side]
                out[rows:] = got[0][:, side]
        elif axis == "far":
            rows = got[0].shape[0]
            refs.pop(0)[...] = low(
                wide(kept[:rows]) + wide(got[0][...]) + wide(got[1][...]) + wide(got[2][...])
            )
        elif axis is None:
            refs.pop(0)[...] = low(wide(kept[...]) + wide(got[0][...]))
        else:
            for side in range(2):
                at = (slice(None),) * axis + (side,)
                refs.pop(0)[...] = low(wide(kept[at]) + wide(got[0][at]))


def exchange(*entries):
    shapes, inputs, kinds = [], [], []
    for axis, kept, got in entries:
        got = list(got) if isinstance(got, (list, tuple)) else [got]
        inputs += [kept, *got]
        kinds.append((axis, len(got)))
        if axis == "join":
            shapes.append(((1 + len(got)) * kept.shape[0], *kept.shape[1:]))
        elif axis == "group":
            shapes += [(2 * kept.shape[0], *kept.shape[2:])] * 2
        elif axis == "far":
            shapes.append(got[0].shape)
        elif axis is None:
            shapes.append(kept.shape)
        else:
            shapes += [kept.shape[:axis] + kept.shape[axis + 1 :]] * 2
    return pl.pallas_call(
        functools.partial(exchange_kernel, kinds),
        grid=(2,),
        in_specs=[half_block(member.shape) for member in inputs],
        out_specs=[half_block(shape) for shape in shapes],
        out_shape=[jax.ShapeDtypeStruct(shape, LOWTYPE) for shape in shapes],
        cost_estimate=takes(0.5),
        compiler_params=pltpu.CompilerParams(
            dimension_semantics=("arbitrary",), vmem_limit_bytes=48 * MEBI
        ),
        name="exchange",
    )(*inputs)


def swap_plane(member, distance):
    size = lax.axis_size("dp")
    return lax.ppermute(member, "dp", [(i, i ^ (distance << 2)) for i in range(size)])


def paired(member):
    return member.reshape(2, member.shape[0] // 2, *member.shape[1:])


def vector_back_kernel(d_projected, cond_weight, unit, d_queries, offset, gain, query, d_normed):
    step = pl.program_id(0)
    offset[...] = column_sum(wide(d_projected[...]))
    part = product_right(d_projected[...], cond_weight[...])

    @pl.when(step == 0)
    def _():
        d_normed[...] = part
        query[...] = column_sum(wide(d_queries[...]))

    @pl.when(step > 0)
    def _():
        d_normed[...] += part

    @pl.when(step == pl.num_programs(0) - 1)
    def _():
        gain[...] = column_sum(d_normed[...] * unit[...])


def vector_back(d_projected, cond_weight, unit, d_projections):
    length, columns = d_projected.shape
    width = columns // 6
    depth = unit.shape[1]
    return pl.pallas_call(
        vector_back_kernel,
        grid=(6,),
        in_specs=[
            pl.BlockSpec((length, width), lambda i: (0, i)),
            pl.BlockSpec((depth, width), lambda i: (0, i)),
            full_spec(unit),
            pl.BlockSpec((length, width), lambda i: (0, 0)),
        ],
        out_specs=[
            pl.BlockSpec((1, width), lambda i: (0, i)),
            pl.BlockSpec((1, depth), lambda i: (0, 0)),
            pl.BlockSpec((1, width), lambda i: (0, 0)),
        ],
        out_shape=[
            jax.ShapeDtypeStruct((1, columns), WIDE),
            jax.ShapeDtypeStruct((1, depth), WIDE),
            jax.ShapeDtypeStruct((1, width), WIDE),
        ],
        scratch_shapes=[pltpu.VMEM((length, depth), WIDE)],
        cost_estimate=takes(3),
        compiler_params=pltpu.CompilerParams(
            dimension_semantics=("arbitrary",), vmem_limit_bytes=32 * MEBI
        ),
        name="vector_back",
    )(d_projected, cond_weight, unit, d_projections)


def far_paired(member):
    return member.reshape(member.shape[0], 2, 2, *member.shape[2:])


def by_group(member):
    return member.reshape(member.shape[0], -1, GROUP_HEADS, *member.shape[2:])


TOKEN_ROWS = 256


def rows_spec(columns, at=0):
    return pl.BlockSpec((TOKEN_ROWS, columns), lambda i: (i, at))


def transition_back_kernel(d_result, gate_two, down_out, gate_up, down_weight, d_down, d_last, d_gate_up):
    half = gate_up.shape[1] // 2
    result = wide(d_result[...])
    gate = sigmoid(gate_two[...])
    given = low(result * gate)
    d_down[...] = given
    d_last[...] = low(result * down_out[...] * gate * (1.0 - gate))
    d_hidden = wide(low(product_right(given, down_weight[...])))
    gate_half = gate_up[:, :half]
    logistic = sigmoid(gate_half)
    d_gate_up[:, :half] = low(
        d_hidden * gate_up[:, half:] * logistic * (1.0 + gate_half * (1.0 - logistic))
    )
    d_gate_up[:, half:] = low(d_hidden * gate_half * logistic)


def transition_back(d_result, projected, down_out, gate_up, down_weight):
    length, width = d_result.shape
    outs = [
        jax.ShapeDtypeStruct((length, width), LOWTYPE),
        jax.ShapeDtypeStruct((length, width), LOWTYPE),
        jax.ShapeDtypeStruct(gate_up.shape, LOWTYPE),
    ]
    return pl.pallas_call(
        transition_back_kernel,
        grid=(length // TOKEN_ROWS,),
        in_specs=[
            rows_spec(width),
            rows_spec(width, 5),
            rows_spec(width),
            rows_spec(gate_up.shape[1]),
            full_spec(down_weight),
        ],
        out_specs=[rows_spec(member.shape[1]) for member in outs],
        out_shape=outs,
        cost_estimate=takes(5),
        compiler_params=pltpu.CompilerParams(
            dimension_semantics=("arbitrary",), vmem_limit_bytes=48 * MEBI
        ),
        name="transition_back",
    )(d_result, projected, down_out, gate_up, down_weight)


def middle_back_kernel(
    d_result,
    gate_one,
    scale_two,
    d_gate_up,
    unit_two,
    spread_two,
    attn_out,
    gu_weight,
    out_weight,
    d_middle,
    d_attn_out,
    d_gated,
    d_pieces,
):
    width = d_result.shape[1]
    d_normed = product_right(d_gate_up[...], gu_weight[...])
    scale = sigmoid(scale_two[...])
    unit = unit_two[...]
    d_pieces[:, width : 2 * width] = low(d_normed * unit * scale * (1.0 - scale))
    d_pieces[:, 2 * width :] = low(d_normed)
    middle = wide(d_result[...]) + normalise_back(d_normed * scale, unit, spread_two[...])
    d_middle[...] = middle
    gate = sigmoid(gate_one[...])
    given = low(middle * gate)
    d_attn_out[...] = given
    d_pieces[:, :width] = low(middle * attn_out[...] * gate * (1.0 - gate))
    d_gated[...] = low(product_right(given, out_weight[...]))


def middle_back(
    d_result, projected, d_gate_up, unit_two, spread_two, attn_out, gu_weight, out_weight
):
    length, width = d_result.shape
    outs = [
        jax.ShapeDtypeStruct((length, width), WIDE),
        jax.ShapeDtypeStruct((length, width), LOWTYPE),
        jax.ShapeDtypeStruct((length, width), LOWTYPE),
        jax.ShapeDtypeStruct((length, 3 * width), LOWTYPE),
    ]
    return pl.pallas_call(
        middle_back_kernel,
        grid=(length // TOKEN_ROWS,),
        in_specs=[
            rows_spec(width),
            rows_spec(width, 2),
            rows_spec(width, 3),
            rows_spec(d_gate_up.shape[1]),
            rows_spec(width),
            rows_spec(1),
            rows_spec(width),
            full_spec(gu_weight),
            full_spec(out_weight),
        ],
        out_specs=[rows_spec(member.shape[1]) for member in outs],
        out_shape=outs,
        cost_estimate=takes(3),
        compiler_params=pltpu.CompilerParams(
            dimension_semantics=("arbitrary",), vmem_limit_bytes=48 * MEBI
        ),
        name="middle_back",
    )(
        d_result,
        projected,
        projected,
        d_gate_up,
        unit_two,
        spread_two,
        attn_out,
        gu_weight,
        out_weight,
    )


def input_back_kernel(
    d_projections,
    scale_one,
    unit_one,
    spread_one,
    d_middle,
    d_pieces,
    d_last,
    proj_weight,
    d_projected,
    d_tokens,
):
    width = unit_one.shape[1]
    d_normed = product_right(d_projections[...], proj_weight[...])
    scale = sigmoid(scale_one[...])
    unit = unit_one[...]
    d_projected[:, :width] = low(d_normed * unit * scale * (1.0 - scale))
    d_projected[:, width : 2 * width] = low(d_normed)
    d_projected[:, 2 * width : 5 * width] = d_pieces[...]
    d_projected[:, 5 * width :] = d_last[...]
    d_tokens[...] = low(d_middle[...] + normalise_back(d_normed * scale, unit, spread_one[...]))


def input_back(
    d_projections, projected, unit_one, spread_one, d_middle, d_pieces, d_last, proj_weight
):
    length, width = unit_one.shape
    outs = [
        jax.ShapeDtypeStruct((length, 6 * width), LOWTYPE),
        jax.ShapeDtypeStruct((length, width), LOWTYPE),
    ]
    return pl.pallas_call(
        input_back_kernel,
        grid=(length // TOKEN_ROWS,),
        in_specs=[
            rows_spec(4 * width),
            rows_spec(width),
            rows_spec(width),
            rows_spec(1),
            rows_spec(width),
            rows_spec(3 * width),
            rows_spec(width),
            full_spec(proj_weight),
        ],
        out_specs=[rows_spec(member.shape[1]) for member in outs],
        out_shape=outs,
        cost_estimate=takes(2),
        compiler_params=pltpu.CompilerParams(
            dimension_semantics=("arbitrary",), vmem_limit_bytes=48 * MEBI
        ),
        name="input_back",
    )(d_projections, projected, unit_one, spread_one, d_middle, d_pieces, d_last, proj_weight)


def together(*members):
    return lax.optimization_barrier(members)


def token_units(pair_rows):
    unit, _ = normalise(wide(pair_rows).reshape(-1, pair_rows.shape[-1]))
    return low(unit)


def atom_units(pair_rows):
    values = wide(pair_rows)
    centre = values - jnp.mean(values, axis=1, keepdims=True)
    return centre * lax.rsqrt(jnp.mean(centre * centre, axis=1, keepdims=True) + EPS)


def in_turn(member):
    member = jnp.stack([member, swap_bit(member, 3)])
    return jnp.concatenate([member, swap_bit(member, 2)], axis=0)


def halves_sum(kept, got):
    half = kept.shape[0] // 2
    return add_low(kept[:half], got[:half]), add_low(kept[half:], got[half:])


def cross_of_all(d_token_bias, d_atom_bias, both, pair_units, heads):
    whole = jnp.stack(d_token_bias).transpose(3, 1, 0, 2, 5, 4, 6)
    whole = whole.reshape(-1, heads, whole.shape[-1])
    slab = lax.psum_scatter(whole, both, scatter_dimension=0, tiled=True).transpose(1, 0, 2)
    token_cross = product(slab.reshape(heads, -1), pair_units)
    whole = jnp.stack(d_atom_bias).transpose(2, 1, 0, 3, 4, 5)
    whole = whole.reshape(-1, *whole.shape[4:])
    return token_cross, lax.psum_scatter(whole, "dp", scatter_dimension=0, tiled=True)


def token_conditioning(condition, weights):
    gain, cond_weight, cond_bias = weights[:3]
    unit_cond, _ = normalise(condition)
    normed = low(unit_cond * wide(gain))
    return unit_cond, normed, product(normed, cond_weight) + wide(cond_bias)


def token_block_forward(place, token_in, conditioned, weights, bias):
    proj_weight, query_bias, out_weight, gu_weight, down_weight = weights[3:]
    unit_cond, normed, projected = conditioned
    width = token_in.shape[1]
    pieces = [projected[:, i * width : (i + 1) * width] for i in range(6)]
    unit_one, spread_one = normalise(token_in)
    normed_one = low(unit_one * sigmoid(pieces[0]) + pieces[1])
    offset = jnp.concatenate([wide(query_bias), jnp.zeros((3 * width,), WIDE)])
    projections = low(product(normed_one, proj_weight) + offset)
    probability, attended, gated = token_forward(place, projections, bias)
    attn_out = product(gated, out_weight)
    middle = token_in + sigmoid(pieces[2]) * attn_out
    unit_two, spread_two = normalise(middle)
    normed_two = low(unit_two * sigmoid(pieces[3]) + pieces[4])
    gate_up = product(normed_two, gu_weight)
    half = gate_up.shape[1] // 2
    gate_half, up_half = gate_up[:, :half], gate_up[:, half:]
    hidden = low(gate_half * sigmoid(gate_half) * up_half)
    down_out = product(hidden, down_weight)
    output = middle + sigmoid(pieces[5]) * down_out
    stored = (
        unit_cond,
        normed,
        projected,
        unit_one,
        spread_one,
        normed_one,
        projections,
        probability,
        attended,
        gated,
        attn_out,
        unit_two,
        spread_two,
        normed_two,
        gate_up,
        hidden,
        down_out,
    )
    return output, stored


def local(
    atom_features,
    atom_single,
    atom_pairs,
    atom_token,
    window_start,
    pair_repr,
    single_repr,
    noise_table,
    noise_index,
    cotangent,
    *params,
):
    atom_block, atompair_gain, atompair_weight, gather_weight = (
        params[:8],
        params[8],
        params[9],
        params[10],
    )
    token_block, tokpair_gain, tokpair_weight = params[11:19], params[19], params[20]
    section, far, near, core = places()
    here = jnp.stack([section, far, near, core, piece_index()]).astype(jnp.int32)
    length = cotangent.shape[2]
    both = ("dp", "section")

    def mine(member):
        return lax.dynamic_index_in_dim(member, section, 0, keepdims=False)[0]

    rows = pair_repr.shape[0] // 2
    heads = tokpair_weight.shape[1]
    features = mine(atom_features)
    window_units = atom_units(atom_pairs)
    atom_gained = wide(atompair_gain)[:, None] * wide(atompair_weight)
    atom_part = low(
        jnp.sum(window_units[:, :, None] * atom_gained[None, :, :, None, None], axis=1)
    )
    windows, atom_heads, span, keys = atom_part.shape
    pair_rows = lax.dynamic_slice_in_dim(pair_repr, section * rows, rows, 0)
    atom_part, pair_rows = together(atom_part, pair_rows)
    pair_units = token_units(pair_rows)
    gained = low(wide(tokpair_gain)[:, None] * wide(tokpair_weight))
    token_part = low(
        lax.dot_general(
            gained, pair_units, (((0,), (1,)), ((), ())), preferred_element_type=WIDE
        )
    ).reshape(heads, rows, length)
    condition = wide(single_repr) + noise_table[mine(noise_index)]
    unit_cond, normed, projected = token_conditioning(condition, token_block)
    run = length // (8 * FAR)
    direct = lax.axis_size("dp") == 4 * FAR and rows == run
    if direct:
        place = jnp.stack([section, far, near, core]).astype(jnp.int32)
        got_atom = swap_plane(atom_part, 2)
        token_part, got_atom = together(token_part, got_atom)
        got_token = swap_plane(token_part, 2)
        runs = jnp.stack([atom_part, got_atom])
        runs = jnp.concatenate([runs, swap_plane(runs, 1)])
        runs, got_token = together(runs, got_token)
        got_atom = swap_near(runs)
        token_runs = jnp.stack([token_part, got_token])
        got_token = swap_plane(token_runs, 1)
        projections = atom_project(features, atom_single, atom_block)
        got_atom, got_token, projections, projected = together(
            got_atom, got_token, projections, projected
        )
        runs = jnp.stack([runs, got_atom])
        atom_bias = [runs, swap_core(runs)]
        runs_a, runs_b = exchange(("group", by_group(token_runs), by_group(got_token)))
        runs_a, runs_b, atom_bias[1] = together(runs_a, runs_b, atom_bias[1])
        got_a, got_b = swap_near(runs_a), swap_section(runs_b)
    else:
        place = jnp.zeros((4,), jnp.int32)
        projections = atom_project(features, atom_single, atom_block)
        whole = lax.all_gather(atom_part, "dp", axis=0, tiled=True)
        whole = whole.reshape(FAR, 2, 2, -1, atom_heads, span, keys).transpose(2, 1, 0, 3, 4, 5, 6)
        atom_bias = [whole[0], whole[1]]
        whole = lax.all_gather(token_part, both, axis=0).transpose(0, 2, 1, 3)
        whole = whole.reshape(FAR, 2, 2, 2, run, -1, GROUP_HEADS, length)
        whole = whole.transpose(5, 2, 1, 3, 0, 6, 4, 7)
        token_bias = [whole[0, 0].swapaxes(0, 1), whole[0, 1].swapaxes(0, 1), whole[1, 0], whole[1, 1]]

    atom_args = (window_start, place, features, atom_single, atom_token, projections, atom_bias)
    atom_args += (atom_block, gather_weight, length)
    before = list(atom_attend(*atom_args, None))
    if direct:
        before[0], got_a, got_b = together(before[0], got_a, got_b)
        runs_a, runs_b = exchange(("join", runs_a, got_a), ("join", runs_b, got_b))
        before[0], runs_a, runs_b = together(before[0], runs_a, runs_b)
        got_a, got_b = swap_section(runs_a), swap_near(runs_b)
    pooled, counts, attended, probability = atom_attend(*atom_args, before)
    atom_stored = [projections, attended, probability]
    if direct:
        pooled, got_a, got_b = together(pooled, got_a, got_b)
        runs_a, runs_b = exchange(("join", runs_a, got_a), ("join", runs_b, got_b))
        runs_a = runs_a.reshape(2, 2, FAR, *runs_a.shape[1:])
        runs_b = runs_b.reshape(2, 2, FAR, *runs_b.shape[1:])
        token_bias = [runs_a, swap_core(runs_a), runs_b, swap_core(runs_b)]
    output, token_stored = token_block_forward(
        place, wide(pooled), (unit_cond, normed, projected), token_block, token_bias
    )

    (
        unit_cond,
        normed,
        projected,
        unit_one,
        spread_one,
        normed_one,
        projections,
        probability,
        attended,
        gated,
        attn_out,
        unit_two,
        spread_two,
        normed_two,
        gate_up,
        hidden,
        down_out,
    ) = token_stored
    _, cond_weight, _, proj_weight, _, out_weight, gu_weight, down_weight = token_block
    width = output.shape[1]
    chunk_a = products(gu_weight.shape, down_weight.shape)
    chunk_b = products(proj_weight.shape, out_weight.shape, cond_weight.shape)
    d_result = mine(cotangent)
    normed_here = from_here(normed)
    d_result, normed_here, output_low = together(d_result, normed_here, low(output))
    d_down, d_last, d_gate_up = transition_back(
        d_result, projected, down_out, gate_up, down_weight
    )
    members_a = [normed_two, d_gate_up, hidden, d_down]
    given_a = chunk_given(here, chunk_a, members_a)
    given_a_there = swap_core(given_a)
    d_gate_up, given_a_there = together(d_gate_up, given_a_there)
    send_a, keep_a = chunk_kept(here, chunk_a, members_a, given_a_there)
    d_gate_up, send_a = together(d_gate_up, send_a)
    got_a = swap_section(send_a)
    d_middle, d_attn_out, d_gated, d_pieces = middle_back(
        d_result, projected, d_gate_up, unit_two, spread_two, attn_out, gu_weight, out_weight
    )
    *d_token_bias, d_projections = token_backward(
        place, projections, probability, attended, d_gated, run
    )

    d_projected, d_tokens = input_back(
        d_projections, projected, unit_one, spread_one, d_middle, d_pieces, d_last, proj_weight
    )
    d_projected, got_a = together(d_projected, got_a)
    keep_a, send_a = exchange((0, paired(keep_a), paired(got_a)))
    d_projected, send_a, d_token_bias[1] = together(d_projected, send_a, d_token_bias[1])
    got_a = swap_near(send_a)
    if direct:
        got_bias = swap_core(d_token_bias[1])
    members_b = [normed_one, d_projections, gated, d_attn_out, normed_here, d_projected]
    given_b = chunk_given(here, chunk_b, members_b)
    d_projected, given_b = together(d_projected, given_b)
    given_b_there = swap_core(given_b)
    grad_offset, grad_gain, grad_query = vector_back(
        d_projected, cond_weight, unit_cond, d_projections
    )
    given_b_there, grad_query = together(given_b_there, grad_query)
    send_b, keep_b = chunk_kept(here, chunk_b, members_b, given_b_there)
    d_tokens, send_b, got_a = together(d_tokens, send_b, got_a)
    got_b = swap_section(send_b)
    entries = [(0, paired(keep_a), paired(got_a))]
    if direct:
        entries.append((0, d_token_bias[0], got_bias))
    keep_a, send_a, *bias = exchange(*entries)
    d_tokens, send_a, *bias = together(d_tokens, send_a, *bias)
    got_a = swap_plane(send_a, 1)
    if direct:
        bias, send_bias = bias
        got_bias = swap_near(send_bias)
    d_attended, d_gates, d_middles, d_atom_pieces, packed_a = atom_tokens_back(
        features, atom_single, atom_token, d_tokens, counts, atom_stored, atom_block, gather_weight
    )
    d_attended, got_a = together(d_attended, got_a)
    keep_a, send_a = exchange((0, paired(keep_a), paired(got_a)))
    d_attended, send_a = together(d_attended, send_a)
    got_a = swap_plane(send_a, 2)
    d_atom_projections, *d_atom_bias = atom_attention_back(
        window_start, place, d_attended, atom_stored
    )
    d_atom_projections, got_b, got_a = together(d_atom_projections, got_b, got_a)
    entries = [(0, paired(keep_b), paired(got_b)), (None, keep_a, got_a)]
    if direct:
        entries.append((0, bias, got_bias))
    keep_b, send_b, total_a, *bias = exchange(*entries)
    total_a = rest_sum(total_a)
    d_middles, send_b, total_a, d_atom_bias[1], *bias = together(
        d_middles, send_b, total_a, d_atom_bias[1], *bias
    )
    got_b, got_a = swap_near(send_b), swap_plane(total_a, 2)
    if direct:
        bias, send_bias = bias
        got_bias = swap_section(send_bias)
        got_atom = swap_core(d_atom_bias[1])
    d_features, packed_b, gain, offset, query = atom_features_back(
        features, atom_single, d_atom_projections, d_gates, d_middles, d_atom_pieces, atom_block
    )
    packed = jnp.concatenate([packed_b, packed_a], axis=1)
    packed = jnp.pad(packed, ((0, 0), (0, -packed.shape[1] % (2 * COLUMNS))))
    chunk_d = products(packed.shape)
    chunk_d[0].direct = True
    given_d = chunk_given(here, chunk_d, [packed])
    given_d, got_a = together(given_d, got_a)
    entries = [("join", total_a, got_a)]
    if direct:
        entries.append((0, d_atom_bias[0], got_atom))
    total_a, *atom = exchange(*entries)
    given_d, total_a, *atom = together(given_d, total_a, *atom)
    got_d = swap_core(given_d)
    got_a = swap_plane(total_a, 1)
    if direct:
        atom, send_atom = atom
    send_d, keep_d = chunk_kept(here, chunk_d, [packed], got_d)
    got_d = swap_section(send_d)

    entries = [
        (0, paired(keep_b), paired(got_b)),
        (0, paired(keep_d), paired(got_d)),
        ("join", total_a, got_a),
    ]
    if direct:
        entries.append((0, paired(bias), paired(got_bias)))
    keep_b, send_b, keep_d, send_d, total_a, *bias = exchange(*entries)
    got_b, got_d, got_a = swap_plane(send_b, 1), swap_near(send_d), swap_near(total_a)
    if direct:
        bias, send_bias = bias
        got_bias = swap_plane(send_bias, 1)
    output_low, total_a = together(output_low, total_a)
    output_halves = exchange_halves(output_low)
    got_d, output_halves = together(got_d, output_halves)

    entries = [(0, paired(keep_b), paired(got_b)), (0, paired(keep_d), paired(got_d))]
    if direct:
        entries.append((0, paired(bias), paired(got_bias)))
    keep_b, send_b, keep_d, send_d, *bias = exchange(*entries)
    got_b, got_d = swap_plane(send_b, 2), swap_plane(send_d, 1)
    if direct:
        bias, send_bias = bias
        got_bias = swap_plane(send_bias, 2)
        send_d, send_atom = together(send_d, send_atom)
        got_atom = swap_near(send_atom)
    features_low, send_d = together(low(d_features), send_d)
    feature_halves = exchange_halves(features_low)
    got_d, feature_halves = together(got_d, feature_halves)

    entries = [(None, keep_b, got_b), (0, paired(keep_d), paired(got_d))]
    if direct:
        entries.append((None, bias, got_bias))
    total_b, keep_d, send_d, *token_slab = exchange(*entries)
    total_b = rest_sum(total_b)
    got_b, got_d = swap_plane(total_b, 2), swap_plane(send_d, 2)
    if direct:
        token_cross = product(token_slab[0].reshape(heads, -1), pair_units)
        got_b, token_cross = together(got_b, token_cross)

    entries = [("join", total_b, got_b), (None, keep_d, got_d), ("join", total_a, got_a)]
    if direct:
        entries.append((0, paired(atom), paired(got_atom)))
    total_b, total_d, total_a, *atom = exchange(*entries)
    total_d = rest_sum(total_d)
    got_b, got_d = swap_plane(total_b, 1), swap_plane(total_d, 2)
    if direct:
        got_atom = swap_plane(atom[1], 1)

    entries = [("join", total_b, got_b), ("join", total_d, got_d)]
    if direct:
        entries.append((0, paired(atom[0]), paired(got_atom)))
    total_b, total_d, *atom = exchange(*entries)
    total_b, total_d, total_a = together(total_b, total_d, total_a)
    got_b, got_d, core_a = swap_near(total_b), swap_plane(total_d, 1), swap_core(total_a)
    entries = [("join", total_d, got_d)]
    if direct:
        entries.append((None, atom[0], swap_plane(atom[1], 2)))
    total_d, *atom = exchange(*entries)
    total_d, core_a, *atom = together(total_d, core_a, *atom)
    got_d = swap_near(total_d)
    if direct:
        (atom_slab,) = atom
    else:
        token_cross, atom_slab = cross_of_all(d_token_bias, d_atom_bias, both, pair_units, heads)
    atom_slab = atom_slab.reshape(windows, atom_heads, span, keys)
    atom_cross = jnp.sum(window_units[:, :, None] * wide(atom_slab)[:, None], axis=(0, 3, 4))
    vectors = [gain, offset, query, grad_gain, grad_offset, grad_query]
    vectors += [token_cross.reshape(1, -1), atom_cross.reshape(1, -1)]
    total = jnp.concatenate(vectors, axis=1)
    total = total + swap_section(total)
    total = total + swap_plane(total, 1)
    total = total + swap_plane(total, 2)
    for bit in more_bits():
        total = total + swap_bit(total, bit)
    total = total + swap_core(total)
    core_b = swap_core(total_b)
    grad_gu, grad_down = assemble(here, chunk_a, [total_a], [core_a])
    got_d, got_b, total, grad_gu, core_b = together(got_d, got_b, total, grad_gu, core_b)
    (total_d,) = exchange(("join", total_d, got_d))
    total_d, got_b, total = together(total_d, got_b, total)
    core_got, core_d, got = swap_core(got_b), swap_core(total_d), swap_near(total)
    core_d, got = together(core_d, got)
    total = (total + got)[0]
    vector_grads = split_vectors(
        total,
        vectors,
        section,
        atom_cross.shape,
        (tokpair_gain, tokpair_weight, atompair_gain, atompair_weight),
    )
    core_d, *vector_grads = together(core_d, *vector_grads)
    (packed,) = assemble(here, chunk_d, [total_d], [core_d])
    core_got, packed = together(core_got, packed)
    grad_proj, grad_out, grad_cond = assemble(
        here, chunk_b, [total_b, got_b], [core_b, core_got]
    )

    atom_width = features.shape[1]
    sizes = [6 * atom_width, 4 * atom_width, width, atom_block[6].shape[1], atom_width]
    sizes.append(2 * atom_width)
    pieces_of = []
    first = 0
    for size in sizes:
        pieces_of.append(packed[:, first : first + size])
        first += size
    atom_cond, atom_proj, atom_gather, atom_gu, atom_out, quarters = pieces_of
    atom_down = quarters.reshape(-1, 2, atom_width).transpose(1, 0, 2).reshape(-1, atom_width)


    (
        gain,
        offset,
        query,
        token_gain,
        token_offset,
        token_query,
        token_pair_gain,
        token_pair_weight,
        pair_gain,
        pair_weight,
    ) = vector_grads
    return (
        output_halves,
        wide(feature_halves),
        gain,
        atom_cond,
        offset,
        atom_proj,
        query,
        atom_out,
        atom_gu,
        atom_down,
        pair_gain,
        pair_weight,
        atom_gather,
        token_gain,
        grad_cond,
        token_offset,
        grad_proj,
        token_query,
        grad_out,
        grad_gu,
        grad_down,
        token_pair_gain,
        token_pair_weight,
    )


def exchange_halves(member):
    section = lax.axis_index("section")
    halves = member.reshape(2, -1, member.shape[1])
    given = lax.dynamic_index_in_dim(halves, 1 - section, 0, keepdims=False)
    kept = lax.dynamic_index_in_dim(halves, section, 0, keepdims=False)
    taken = swap_section(given)
    first = section == 0
    return jnp.stack([jnp.where(first, kept, taken), jnp.where(first, taken, kept)])[:, None]


def solution(mesh):
    weights = [P()] * 21
    halves = P(None, "dp", "section", None)
    grads = [1, 2, 1, 2, 1, 2, 2, 2, 1, 2, 2, 1, 2, 1, 2, 1, 2, 2, 2, 1, 2]
    return jax.shard_map(
        local,
        mesh=mesh,
        in_specs=(
            P(None, "dp", None, None),
            P(),
            P("dp", None, None, None),
            P(),
            P(),
            P("dp", None, None),
            P(),
            P(),
            P(None, "dp"),
            P(None, "dp", None, None),
            *weights,
        ),
        out_specs=(halves, halves)
        + tuple(P("section") if rank == 1 else P("section", None) for rank in grads),
        check_vma=False,
    )
```
